32 devices in a mesh: groups: 2 (over x), seq: 2 (over core), vocab: 8 (over z, y).
Axes of the slice: x: 2, y: 2, z: 4, core: 2. Of those that a mesh axis runs over, the one named last changes fastest.
Arguments:
- teacher_rows: bfloat16 [2048, 8192], P(('groups', 'seq'), 'vocab'), parts along dimension 0, may hold values from -200 to 200
- owner: int32 [2048], P(('groups', 'seq')), parts along dimension 0, may hold values from 0 to 255, as said below
- counts: int32 [4], P(('groups', 'seq')), parts along dimension 0, may hold values from 256 to 512, as said below
- proj_weight: bfloat16 [8192, 3584], P('vocab'), may hold values from -0.0625 to 0.0625
- student_hidden: bfloat16 [1024, 3584], P(('groups', 'seq', 'vocab')), parts along dimension 0, may hold values from -150 to 150
- head_weight: bfloat16 [3584, 19456], P('seq', 'vocab'), may hold values from -0.09375 to 0.09375
- targets: int32 [1024], P(('groups', 'seq')), parts along dimension 0, may hold values from 0 to 19455
Outputs:
- row_loss: float32 [1024], P(('groups', 'seq')), parts along dimension 0
- hidden_grad: bfloat16 [1024, 3584], P(('groups', 'seq', 'vocab')), parts along dimension 0
The draws below stay inside these ranges and needn't reach their ends.
There are 2 independent parts, one for each index of `groups`. The reference program is written for one: setup_inputs(seed, part) draws one part's arguments, and reference() takes and returns one part's arrays. A program takes and returns all parts, laid end to end along the dimension named above; an argument that names none is the same for every part. Nothing has to cross between parts.
Inputs may be any that keep to these rules, and one draw needn't show every extreme that they name: `owner`: in each slab the live teacher tokens' owners never fall, start at 0, end at 255 and give every student token one or two teacher tokens; padded tokens have arbitrary owners. counts[s] is the number of live teacher tokens of slab s; some slab is full.
All inputs are finite; a program needn't handle non-finite values.
Results may differ from the reference program's by a relative error of at most 0.0098.
The reference program's roundings to bfloat16 on the way (of `aligned`, `projected` and `upstream`) count: a program that leaves them out, or rounds other values in their place, can miss the bound.
Values may be sent and summed in bfloat16 or wider, within the bound.
No kernel may reach another device: no remote copies, remote signals or barrier semaphores. Data moves between devices by JAX's collectives and lax.ppermute only.
A program may use at most 128 MiB of HBM per device.

```python
import math
import jax
import jax.numpy as jnp
import numpy as np
from jax import lax

DT = 8192
DS = 3584
SLAB = 256
TPAD = 512
SLABS = 2
TOKENS = 512
TEACHER = 1024
VOCAB = 19456


def span_layout(key):
    lengths = jax.random.randint(jax.random.fold_in(key, 5), (SLABS, SLAB), 1, 3)
    fullest = jax.random.randint(jax.random.fold_in(key, 6), (), 0, SLABS)
    lengths = jnp.where(jnp.arange(SLABS)[:, None] == fullest, 2, lengths)
    ends = jnp.cumsum(lengths, axis=1)
    totals = ends[:, -1]
    positions = jnp.arange(TPAD)
    owners = jnp.sum((ends[:, None, :] <= positions[None, :, None]).astype(jnp.int32), axis=2)
    filler = jax.random.randint(jax.random.fold_in(key, 7), (SLABS, TPAD), 0, SLAB)
    owners = jnp.where(positions[None, :] < totals[:, None], owners, filler)
    return (owners.reshape(TEACHER).astype(jnp.int32), totals.astype(jnp.int32))


def draw_owner(key, part):
    return span_layout(key)[0]


def draw_counts(key, part):
    return span_layout(key)[1]


def scaled_rows(key, rows, cols, scale, widest, bound):
    base = jax.random.normal(jax.random.fold_in(key, 1), (rows, cols), jnp.float32)
    factors = jnp.exp(jax.random.uniform(jax.random.fold_in(key, 2), (rows, 1), jnp.float32, 0.0, math.log(widest)))
    return jnp.clip(base * factors * scale, -bound, bound).astype(jnp.bfloat16)


def draw_teacher_rows(key, part):
    key = jax.random.fold_in(key, 11)
    return scaled_rows(key, TEACHER, DT, 4.0, 1.0, 24.0)


def draw_student_hidden(key, part):
    key = jax.random.fold_in(key, 13)
    return scaled_rows(key, TOKENS, DS, 3.0, 1.0, 18.0)


def with_ends(values, rng, least, high):
    longest = values.shape.index(max(values.shape))
    spots = []
    for shift in (0, 1):
        where = [jax.random.randint(jax.random.fold_in(rng, axis), (), 0, length) for axis, length in enumerate(values.shape)]
        where[longest] = (where[longest] + shift) % values.shape[longest]
        spots.append(tuple(where))
    return values.at[spots[0]].set(least).at[spots[1]].set(high)


def block_scale(own_key, shape, shards, least, top_value):
    def one(position, blocks):
        heights = jax.random.uniform(jax.random.fold_in(jax.random.fold_in(own_key, 6), position), (blocks,), jnp.float32, least / len(shards), top_value / len(shards))
        return jnp.repeat(jnp.exp(heights), shape[position] // blocks).reshape((-1,) + (1,) * (len(shape) - position - 1))

    loudness = one(*shards[0])
    for cut in shards[1:]:
        loudness = loudness * one(*cut)
    return loudness


def rank_bounds(number_of, lean):
    loads = [(1 << 20) // math.isqrt(standing ** lean) + 1 for standing in range(1, number_of + 1)]
    scale = 1 + sum(loads) // (1 << 30)
    return np.cumsum(np.array([max(1, weight // scale) for weight in loads]))


def ranked(rng, extent, count, lean):
    grid = rank_bounds(count, lean)
    lot = jax.random.randint(jax.random.fold_in(rng, 1), extent, 0, int(grid[count - 1]))
    grade = jnp.searchsorted(jnp.asarray(grid, jnp.int32), lot, side="right")
    return jax.random.permutation(jax.random.fold_in(rng, 2), count)[grade].astype(jnp.int32)


def gaussian(rng, dims, spread, reach, split=(), kind=jnp.bfloat16):
    result = spread * jax.random.normal(rng, dims, jnp.float32)
    if split:
        result = result * block_scale(rng, dims, split, -0.22, 0.18)
    return jnp.clip(result, -reach, reach).astype(kind)


def setup_inputs(seed: int = 0, part: int = 0) -> dict:
    keys = jax.random.split(jax.random.key(seed), 8)
    part_splits = jax.random.split(jax.random.fold_in(keys[7], part), 8)
    teacher_rows = draw_teacher_rows(jax.random.fold_in(jax.random.fold_in(keys[7], part), 71), part)
    owner = draw_owner(jax.random.fold_in(jax.random.fold_in(keys[7], part), 71), part)
    counts = draw_counts(jax.random.fold_in(jax.random.fold_in(keys[7], part), 71), part)
    proj_weight = gaussian(keys[3], (DT, DS), DT ** -0.5, 0.0625, ((0, 8),))
    student_hidden = draw_student_hidden(jax.random.fold_in(jax.random.fold_in(keys[7], part), 71), part)
    head_weight = gaussian(keys[5], (DS, VOCAB), DS ** -0.5, 0.09375, ((0, 2), (1, 8)))
    targets = with_ends(ranked(part_splits[6], (TOKENS,), VOCAB, 2), jax.random.fold_in(part_splits[6], 3), 0, VOCAB - 1).astype(jnp.int32)
    return dict(teacher_rows=teacher_rows, owner=owner, counts=counts, proj_weight=proj_weight, student_hidden=student_hidden, head_weight=head_weight, targets=targets)


loss_scale = 64.0


def log_normalize(logits):
    largest = jnp.max(logits, axis=1)
    totals = jnp.sum(jnp.exp(logits - largest[:, None]), axis=1)
    return logits - (largest + jnp.log(totals))[:, None], largest + jnp.log(totals)


def reference(teacher_rows, owner, counts, proj_weight, student_hidden, head_weight, targets):
    stacked = teacher_rows.reshape(SLABS, TPAD, DT).astype(jnp.float32)
    owners = owner.reshape(SLABS, TPAD)
    positions = jnp.arange(TPAD, dtype=jnp.int32)
    alive = positions[None, :] < counts[:, None]
    member = (owners[:, None, :] == jnp.arange(SLAB, dtype=jnp.int32)[None, :, None]) & alive[:, None, :]
    member_float = member.astype(jnp.float32)
    span_sizes = jnp.sum(member_float, axis=2)
    summed = jnp.einsum("sjt,std->sjd", member_float, stacked)
    aligned = (summed / span_sizes[:, :, None]).astype(jnp.bfloat16).reshape(TOKENS, DT)
    projected = jnp.dot(aligned, proj_weight, preferred_element_type=jnp.float32).astype(jnp.bfloat16)
    logit_teach = jnp.dot(projected, head_weight, preferred_element_type=jnp.float32)
    logit_stud = jnp.dot(student_hidden, head_weight, preferred_element_type=jnp.float32)
    log_teach, lse_teach = log_normalize(logit_teach)
    log_stud, lse_stud = log_normalize(logit_stud)
    prob_teach = jnp.exp(log_teach)
    prob_stud = jnp.exp(log_stud)
    target_hit = jnp.arange(VOCAB, dtype=jnp.int32)[None, :] == targets[:, None]
    divergence = jnp.sum(prob_teach * (log_teach - log_stud), axis=1)
    target_logit = jnp.sum(jnp.where(target_hit, logit_stud, 0.0), axis=1)
    row_loss = divergence + lse_stud - target_logit
    upstream = (loss_scale * (2.0 * prob_stud - prob_teach - target_hit.astype(jnp.float32))).astype(jnp.bfloat16)
    hidden_grad = lax.dot_general(upstream, head_weight, (((1,), (1,)), ((), ())), preferred_element_type=jnp.float32)
    return row_loss, hidden_grad.astype(jnp.bfloat16)
```

```python
import functools

import jax
import jax.numpy as jnp
from jax import lax
from jax.experimental import pallas as pl
from jax.experimental.pallas import tpu as pltpu
from jax.sharding import PartitionSpec as P

loss_scale = 64.0
wire = jnp.float16
lanes = 128
vmem_bytes = 18 * 1024 * 1024

in_vmem = pl.BlockSpec(memory_space=pltpu.VMEM)
in_smem = pl.BlockSpec(memory_space=pltpu.SMEM)
in_place = pl.BlockSpec(memory_space=pl.ANY)


def cuts(total, step):
    return [(start, min(step, total - start)) for start in range(0, total, step)]


def project_kernel(count, step, member_ref, teacher_ref, weight_ref, *rest):
    outs, (teacher, weight, sems) = rest[:count], rest[count:]
    blk = outs[0].shape[0]
    parts = cuts(weight.shape[1], step)
    first = pltpu.make_async_copy(teacher_ref, teacher, sems.at[len(parts)])
    first.start()
    copies = []
    for index, (start, size) in enumerate(parts):
        at = pl.ds(start, size)
        copies.append(pltpu.make_async_copy(weight_ref.at[:, at], weight.at[:, at], sems.at[index]))
        copies[-1].start()
    member = member_ref[...]
    sizes = jnp.sum(member.astype(jnp.float32), axis=1, keepdims=True)
    first.wait()
    summed = jnp.dot(member, teacher[...], preferred_element_type=jnp.float32)
    aligned = (summed / sizes).astype(jnp.bfloat16)
    for copy, (start, size) in zip(copies, parts):
        copy.wait()
        product = jnp.dot(aligned, weight[:, start : start + size], preferred_element_type=jnp.float32)
        for piece, out in enumerate(outs):
            out[:, start : start + size] = product[piece * blk : (piece + 1) * blk]


def project(member, teacher_rows, proj_weight, count, step):
    slab_rows, (depth, width) = member.shape[0], proj_weight.shape
    blk = slab_rows // count
    return pl.pallas_call(
        functools.partial(project_kernel, count, step),
        in_specs=[in_vmem, in_place, in_place],
        out_specs=[in_vmem] * count,
        out_shape=[jax.ShapeDtypeStruct((blk, width), jnp.float32)] * count,
        scratch_shapes=[
            pltpu.VMEM(teacher_rows.shape, jnp.bfloat16),
            pltpu.VMEM(proj_weight.shape, jnp.bfloat16),
            pltpu.SemaphoreType.DMA((len(cuts(width, step)) + 1,)),
        ],
        compiler_params=pltpu.CompilerParams(vmem_limit_bytes=vmem_bytes),
        cost_estimate=pl.CostEstimate(
            flops=2 * slab_rows * depth * (width + teacher_rows.shape[0]),
            bytes_accessed=2 * depth * (width + teacher_rows.shape[0]) + 4 * slab_rows * width,
            transcendentals=0,
        ),
    )(member, teacher_rows, proj_weight)


def multiply(core, pieces, heads, logit_ref, step):
    depth, total = heads[0].shape
    highest = None
    for start, size in cuts(total, step):
        part = None
        for half, head_ref in zip((core, 1 - core), heads):
            at = pl.ds(pl.multiple_of(half * depth, lanes), depth)
            rows = [ref[:, at] for ref in pieces]
            rows = jnp.concatenate(rows, axis=0) if len(rows) > 1 else rows[0]
            term = jnp.dot(rows, head_ref[:, start : start + size], preferred_element_type=jnp.float32)
            part = term if part is None else part + term
        logit_ref[:, start : start + size] = part
        for lane in range(0, size, lanes):
            top = part[:, lane : lane + lanes]
            highest = top if highest is None else jnp.maximum(highest, top)
    return highest


def as_columns(first, second, third):
    lane = lax.broadcasted_iota(jnp.int32, (first.shape[0], lanes), 1)
    return jnp.where(lane == 0, first, jnp.where(lane == 1, second, jnp.where(lane == 2, third, 0.0)))


def student_kernel(count, step, chunk, place_ref, *refs):
    pieces, heads = refs[:count], refs[count : count + 2]
    column_ref, logit_ref, scaled_ref, stats_ref, highest, table = refs[count + 2 :]
    highest[...] = multiply(place_ref[1], pieces, heads, logit_ref, step)

    def one(part, carry):
        rows = pl.ds(pl.multiple_of(part * chunk, chunk), chunk)
        logit = logit_ref[rows, :]
        top = jnp.max(highest[rows, :], axis=1, keepdims=True)
        scaled = jnp.exp(logit - top)
        hit = lax.broadcasted_iota(jnp.int32, logit.shape, 1) == column_ref[rows, :]
        picked = jnp.sum(jnp.where(hit, logit, 0.0), axis=1, keepdims=True)
        scaled_ref[rows, :] = scaled
        table[rows, :] = as_columns(top, jnp.sum(scaled, axis=1, keepdims=True), picked)
        return carry

    lax.fori_loop(0, logit_ref.shape[0] // chunk, one, 0)
    stats_ref[...] = table[...].T[0:8]


def teacher_kernel(count, step, chunk, place_ref, *refs):
    pieces, heads = refs[:count], refs[count : count + 2]
    stud_logit_ref, stud_ref, scaled_ref, stats_ref, highest, table = refs[count + 2 :]
    highest[...] = multiply(place_ref[1], pieces, heads, scaled_ref, step)

    def one(part, carry):
        rows = pl.ds(pl.multiple_of(part * chunk, chunk), chunk)
        logit = scaled_ref[rows, :]
        top = jnp.max(highest[rows, :], axis=1, keepdims=True)
        scaled = jnp.exp(logit - top)
        gap = jnp.sum(scaled * (logit - stud_logit_ref[rows, :]), axis=1, keepdims=True)
        scaled_ref[rows, :] = scaled
        table[rows, :] = as_columns(top, jnp.sum(scaled, axis=1, keepdims=True), gap)
        return carry

    lax.fori_loop(0, scaled_ref.shape[0] // chunk, one, 0)
    teach = table[...].T[0:8]
    row = lax.broadcasted_iota(jnp.int32, teach.shape, 0)
    stats_ref[...] = jnp.where(row < 4, teach, pltpu.roll(stud_ref[...], 4, 0))


def head_cost(rows, heads):
    depth, vocab_dev = 2 * heads[0].shape[0], heads[0].shape[1]
    return pl.CostEstimate(
        flops=2 * rows * depth * vocab_dev,
        bytes_accessed=2 * depth * vocab_dev + 12 * rows * vocab_dev,
        transcendentals=rows * vocab_dev,
    )


def student_logits(place, pieces, heads, column, step, chunk):
    rows, vocab_dev = column.shape[0], heads[0].shape[1]
    wide = (rows, vocab_dev)
    return pl.pallas_call(
        functools.partial(student_kernel, len(pieces), step, chunk),
        in_specs=[in_smem] + [in_vmem] * (len(pieces) + 3),
        out_specs=[in_vmem] * 3,
        out_shape=[
            jax.ShapeDtypeStruct(wide, jnp.float32),
            jax.ShapeDtypeStruct(wide, jnp.float32),
            jax.ShapeDtypeStruct((8, rows), jnp.float32),
        ],
        scratch_shapes=[pltpu.VMEM((rows, lanes), jnp.float32)] * 2,
        compiler_params=pltpu.CompilerParams(vmem_limit_bytes=vmem_bytes),
        cost_estimate=head_cost(rows, heads),
    )(place, *pieces, *heads, column)


def teacher_logits(place, pieces, heads, logit_stud, stats_stud, step, chunk):
    rows, vocab_dev = logit_stud.shape
    return pl.pallas_call(
        functools.partial(teacher_kernel, len(pieces), step, chunk),
        in_specs=[in_smem] + [in_vmem] * (len(pieces) + 4),
        out_specs=[in_vmem] * 2,
        out_shape=[
            jax.ShapeDtypeStruct((rows, vocab_dev), jnp.float32),
            jax.ShapeDtypeStruct((8, rows), jnp.float32),
        ],
        scratch_shapes=[pltpu.VMEM((rows, lanes), jnp.float32)] * 2,
        compiler_params=pltpu.CompilerParams(vmem_limit_bytes=vmem_bytes),
        cost_estimate=head_cost(rows, heads),
    )(place, *pieces, *heads, logit_stud, stats_stud)


def swapped(values, distance):
    total = values.shape[1]
    lane = lax.broadcasted_iota(jnp.int32, values.shape, 1)
    return jnp.where(
        (lane & distance) != 0, pltpu.roll(values, distance, 1), pltpu.roll(values, total - distance, 1)
    )


def merged(me, bit, distance, mine, theirs):
    theirs = swapped(theirs, distance)
    upper = ((me >> bit) & 1) == 1
    low, high = jnp.where(upper, theirs, mine), jnp.where(upper, mine, theirs)
    rows = [None] * 8
    for at in (0, 4):
        top = jnp.maximum(low[at : at + 1], high[at : at + 1])
        left, right = jnp.exp(low[at : at + 1] - top), jnp.exp(high[at : at + 1] - top)
        rows[at] = top
        rows[at + 1] = left * low[at + 1 : at + 2] + right * high[at + 1 : at + 2]
        if at == 0:
            rows[2] = left * low[2:3] + right * high[2:3]
    rows[6] = low[6:7] + high[6:7]
    return rows


def merge_kernel(bit, distance, place_ref, mine_ref, theirs_ref, out_ref):
    rows = merged(place_ref[0], bit, distance, mine_ref[...], theirs_ref[...])
    for at, row in enumerate(rows):
        out_ref[at : at + 1, :] = jnp.zeros_like(rows[0]) if row is None else row


def merge(place, bit, distance, mine, theirs):
    return pl.pallas_call(
        functools.partial(merge_kernel, bit, distance),
        in_specs=[in_smem, in_vmem, in_vmem],
        out_specs=in_vmem,
        out_shape=jax.ShapeDtypeStruct(mine.shape, jnp.float32),
    )(place, mine, theirs)


def gradient_kernel(bits, step, chunk, place_ref, *refs):
    count = 1 << bits
    mine_ref, theirs_ref, own_ref, teach_ref, stud_ref, column_ref, *heads, loss_ref = refs[:9]
    outs = refs[9 : count + 9]
    upstream, factors = refs[count + 9 :]
    rows = upstream.shape[0]
    blk = rows // count
    me, core = place_ref[0], place_ref[1]
    last = bits - 1
    top_teach, total_teach, gap, _, top_stud, total_stud, picked, _ = merged(
        me, last, blk << last, mine_ref[...], theirs_ref[...]
    )
    lse_teach = top_teach + jnp.log(total_teach)
    lse_stud = top_stud + jnp.log(total_stud)
    loss = jnp.broadcast_to(gap / total_teach - lse_teach + 2.0 * lse_stud - picked, loss_ref.shape)
    for bit in range(bits):
        loss = jnp.where(((me >> bit) & 1) == 1, swapped(loss, blk << bit), loss)
    loss_ref[...] = loss
    own = own_ref[...]
    scale_teach = -loss_scale * jnp.exp(own[0:1] - lse_teach)
    scale_stud = 2.0 * loss_scale * jnp.exp(own[4:5] - lse_stud)
    line = lax.broadcasted_iota(jnp.int32, (lanes, rows), 0)
    factors[...] = jnp.where(line == 0, scale_teach, scale_stud).T

    def one(part, carry):
        at = pl.ds(pl.multiple_of(part * chunk, chunk), chunk)
        hit = lax.broadcasted_iota(jnp.int32, (chunk, teach_ref.shape[1]), 1) == column_ref[at, :]
        both = teach_ref[at, :] * factors[at, 0:1] + stud_ref[at, :] * factors[at, 1:2]
        upstream[at, :] = jnp.where(hit, both - loss_scale, both).astype(jnp.bfloat16)
        return carry

    lax.fori_loop(0, rows // chunk, one, 0)
    depth = heads[0].shape[0]
    for half, head_ref in zip((core, 1 - core), heads):
        for start, size in cuts(depth, step):
            product = lax.dot_general(
                upstream[...],
                head_ref[start : start + size, :],
                (((1,), (1,)), ((), ())),
                preferred_element_type=jnp.float32,
            )
            at = pl.ds(pl.multiple_of(half * depth + start, lanes), size)
            for piece, out in enumerate(outs):
                out[:, at] = product[piece * blk : (piece + 1) * blk]


def gradient(place, mine, theirs, own, scaled_teach, scaled_stud, column, heads, bits, step, chunk):
    rows, vocab_dev = scaled_teach.shape
    count = 1 << bits
    width = 2 * heads[0].shape[0]
    return pl.pallas_call(
        functools.partial(gradient_kernel, bits, step, chunk),
        in_specs=[in_smem] + [in_vmem] * 8,
        out_specs=[in_vmem] * (count + 1),
        out_shape=[jax.ShapeDtypeStruct((8, rows), jnp.float32)]
        + [jax.ShapeDtypeStruct((rows // count, width), jnp.float32)] * count,
        scratch_shapes=[
            pltpu.VMEM((rows, vocab_dev), jnp.bfloat16),
            pltpu.VMEM((rows, lanes), jnp.float32),
        ],
        compiler_params=pltpu.CompilerParams(vmem_limit_bytes=vmem_bytes),
        cost_estimate=head_cost(rows, heads),
    )(place, mine, theirs, own, scaled_teach, scaled_stud, column, *heads)


def tie(block, *others):
    return lax.optimization_barrier((block, *others))[0]


def make_body(vocab_size):
    bits = vocab_size.bit_length() - 1
    assert vocab_size == 1 << bits

    def swap(block, bit):
        return lax.ppermute(block, "vocab", [(at, at ^ (1 << bit)) for at in range(vocab_size)])

    def lowest(mask):
        return (mask & -mask).bit_length() - 1

    def spread(own, line=None):
        blocks = [own]
        for mask in range(1, vocab_size):
            bit = lowest(mask)
            block = blocks[mask ^ (1 << bit)]
            if line is not None and bit == 0:
                block = tie(block, line[-2])
            blocks.append(swap(block, bit))
            if line is not None and bit == 0:
                line.append(blocks[-1])
        return blocks

    def reduce_blocks(parts):
        terms, line = list(parts), []
        for mask in range(vocab_size - 1, 0, -1):
            bit = lowest(mask)
            block = terms[mask].astype(wire)
            if bit == 0 and len(line) > 1:
                block = tie(block, line[-2])
            block = swap(block, bit)
            if bit == 0:
                line.append(block)
            terms[mask ^ (1 << bit)] = terms[mask ^ (1 << bit)] + block.astype(jnp.float32)
        return terms[0], line

    def body(teacher_rows, owner, counts, proj_weight, student_hidden, head_weight, targets):
        teach_rows = teacher_rows.shape[0]
        slab_rows = targets.shape[0]
        vocab_dev = head_weight.shape[1]
        blk = slab_rows // vocab_size
        chunk = min(slab_rows, 32)
        me = lax.axis_index("vocab")
        place = jnp.stack([me, lax.axis_index("seq")]).astype(jnp.int32)

        def in_order(vec):
            grid = vec.reshape((2,) * bits + (blk,))
            for bit in range(bits):
                grid = jnp.where((me >> bit) & 1 == 1, jnp.flip(grid, bits - 1 - bit), grid)
            return grid.reshape(slab_rows)

        def as_pieces(blocks):
            return blocks if blk % 16 == 0 else [jnp.concatenate(blocks, axis=0)]

        heads = (head_weight, lax.ppermute(head_weight, "seq", [(0, 1), (1, 0)]))

        spot = lax.iota(jnp.int32, slab_rows)
        row_id = ((spot // blk) ^ me) * blk + spot % blk
        alive = lax.iota(jnp.int32, teach_rows) < counts[0]
        member = (owner[None, :] == row_id[:, None]) & alive[None, :]
        parts = project(member.astype(jnp.bfloat16), teacher_rows, proj_weight, vocab_size, 896)
        projected_own, line = reduce_blocks(parts)
        hidden = spread(tie(student_hidden, parts[-1]), line)
        projected = spread(projected_own.astype(jnp.bfloat16))

        column = (in_order(targets) - me * vocab_dev)[:, None]
        logit_stud, scaled_stud, stats_stud = student_logits(
            place, as_pieces(hidden), heads, column, 1280, chunk
        )
        scaled_teach, stats = teacher_logits(
            place, as_pieces(projected), heads, logit_stud, stats_stud, 1280, chunk
        )
        mine = stats
        for bit in range(bits):
            theirs = swap(mine, bit)
            if bit < bits - 1:
                mine = merge(place, bit, blk << bit, mine, theirs)
        loss, *terms = gradient(
            place, mine, theirs, stats, scaled_teach, scaled_stud, column, heads, bits, 896, chunk
        )
        return (loss[0], reduce_blocks(terms)[0].astype(jnp.bfloat16))

    return body


def solution(mesh):
    return jax.shard_map(
        make_body(mesh.shape["vocab"]),
        mesh=mesh,
        in_specs=(
            P(("groups", "seq"), "vocab"),
            P(("groups", "seq")),
            P(("groups", "seq")),
            P("vocab", None),
            P(("groups", "seq", "vocab"), None),
            P("seq", "vocab"),
            P(("groups", "seq")),
        ),
        out_specs=(P(("groups", "seq")), P(("groups", "seq", "vocab"), None)),
        check_vma=False,
    )
```

```python
import functools

import jax
import jax.numpy as jnp
from jax import lax
from jax.experimental import pallas as pl
from jax.experimental.pallas import tpu as pltpu
from jax.sharding import PartitionSpec as P

loss_scale = 64.0
wire = jnp.float16
lanes = 128
vmem_bytes = 46 * 1024 * 1024
project_bytes = 54 * 1024 * 1024
chunk_columns = 512

in_vmem = pl.BlockSpec(memory_space=pltpu.VMEM)
in_smem = pl.BlockSpec(memory_space=pltpu.SMEM)
in_place = pl.BlockSpec(memory_space=pl.ANY)


def cuts(total, step):
    return [(start, min(step, total - start)) for start in range(0, total, step)]


def project_kernel(count, step, member_ref, teacher_ref, weight_ref, *rest):
    outs, (teacher, weight, sems) = rest[:count], rest[count:]
    blk = outs[0].shape[0]
    parts = cuts(weight.shape[1], step)
    first = pltpu.make_async_copy(teacher_ref, teacher, sems.at[len(parts)])
    first.start()
    copies = []
    for index, (start, size) in enumerate(parts):
        at = pl.ds(start, size)
        copies.append(pltpu.make_async_copy(weight_ref.at[:, at], weight.at[:, at], sems.at[index]))
        copies[-1].start()
    member = member_ref[...]
    sizes = jnp.sum(member.astype(jnp.float32), axis=1, keepdims=True)
    first.wait()
    summed = jnp.dot(member, teacher[...], preferred_element_type=jnp.float32)
    aligned = (summed / sizes).astype(jnp.bfloat16)
    for copy, (start, size) in zip(copies, parts):
        copy.wait()
        product = jnp.dot(aligned, weight[:, start : start + size], preferred_element_type=jnp.float32)
        for piece, out in enumerate(outs):
            out[:, start : start + size] = product[piece * blk : (piece + 1) * blk]


def project(member, teacher_rows, proj_weight, count, step):
    slab_rows, (depth, width) = member.shape[0], proj_weight.shape
    blk = slab_rows // count
    return pl.pallas_call(
        functools.partial(project_kernel, count, step),
        in_specs=[in_vmem, in_place, in_place],
        out_specs=[in_vmem] * count,
        out_shape=[jax.ShapeDtypeStruct((blk, width), jnp.float32)] * count,
        scratch_shapes=[
            pltpu.VMEM(teacher_rows.shape, jnp.bfloat16),
            pltpu.VMEM(proj_weight.shape, jnp.bfloat16),
            pltpu.SemaphoreType.DMA((len(cuts(width, step)) + 1,)),
        ],
        compiler_params=pltpu.CompilerParams(vmem_limit_bytes=project_bytes),
        cost_estimate=pl.CostEstimate(
            flops=2 * slab_rows * depth * (width + teacher_rows.shape[0]),
            bytes_accessed=2 * depth * (width + teacher_rows.shape[0]) + 4 * slab_rows * width,
            transcendentals=0,
        ),
    )(member, teacher_rows, proj_weight)


class Fetch:
    def __init__(self, sems):
        self.sems, self.used = sems, 0

    def start(self, source, target):
        copy = pltpu.make_async_copy(source, target, self.sems.at[self.used])
        copy.start()
        self.used += 1
        return copy


def multiply(pieces, heads, rows, head, logit_ref, highest, fetch, step):
    depth, total = heads[0].shape
    blk = pieces[0].shape[0]
    waits = [fetch.start(piece, rows.at[pl.ds(i * blk, blk)]) for i, piece in enumerate(pieces)]
    first = fetch.used
    for start, size in cuts(total, step):
        for half, source in enumerate(heads):
            at = pl.ds(start, size)
            fetch.start(source.at[:, at], head.at[pl.ds(half * depth, depth), at])
    highest[...] = jnp.full(highest.shape, -jnp.inf, jnp.float32)
    for wait in waits:
        wait.wait()

    def one(index, start, size):
        at = pl.ds(start, size)
        for half, source in enumerate(heads):
            sem = fetch.sems.at[first + 2 * index + half]
            pltpu.make_async_copy(source.at[:, at], head.at[pl.ds(half * depth, depth), at], sem).wait()
        part = jnp.dot(rows[...], head[:, at], preferred_element_type=jnp.float32)
        logit_ref[:, at] = part
        top = part[:, :lanes]
        for lane in range(lanes, size, lanes):
            top = jnp.maximum(top, part[:, lane : lane + lanes])
        highest[...] = jnp.maximum(highest[...], top)

    def body(index, carry):
        one(index, pl.multiple_of(index * step, step), step)
        return carry

    full = total // step
    lax.fori_loop(0, full, body, 0)
    if total % step:
        one(full, full * step, total % step)


def as_columns(first, second, third):
    lane = lax.broadcasted_iota(jnp.int32, (first.shape[0], lanes), 1)
    return jnp.where(lane == 0, first, jnp.where(lane == 1, second, jnp.where(lane == 2, third, 0.0)))


def student_kernel(count, step, chunk, *refs):
    pieces, heads = refs[:count], refs[count : count + 2]
    column_ref, logit_out, scaled_out, stats_ref = refs[count + 2 : count + 6]
    held, head, logit_ref, scaled_ref, highest, table, sems = refs[count + 6 :]
    fetch = Fetch(sems)
    multiply(pieces, heads, held, head, logit_ref, highest, fetch, step)
    first = fetch.start(logit_ref, logit_out)

    def one(part, carry):
        rows = pl.ds(pl.multiple_of(part * chunk, chunk), chunk)
        logit = logit_ref[rows, :]
        top = jnp.max(highest[rows, :], axis=1, keepdims=True)
        scaled = jnp.exp(logit - top)
        hit = lax.broadcasted_iota(jnp.int32, logit.shape, 1) == column_ref[rows, :]
        picked = jnp.sum(jnp.where(hit, logit, 0.0), axis=1, keepdims=True)
        scaled_ref[rows, :] = scaled
        table[rows, :] = as_columns(top, jnp.sum(scaled, axis=1, keepdims=True), picked)
        return carry

    lax.fori_loop(0, logit_ref.shape[0] // chunk, one, 0)
    second = fetch.start(scaled_ref, scaled_out)
    stats_ref[...] = table[...].T[0:8]
    first.wait()
    second.wait()


def teacher_kernel(count, step, chunk, *refs):
    pieces, heads = refs[:count], refs[count : count + 2]
    stud_logit, stud_ref, scaled_ref, stats_ref = refs[count + 2 : count + 6]
    held, head, stud_logit_ref, highest, table, sems = refs[count + 6 :]
    fetch = Fetch(sems)
    multiply(pieces, heads, held, head, scaled_ref, highest, fetch, step)
    copy = fetch.start(stud_logit, stud_logit_ref)
    copy.wait()

    def one(part, carry):
        rows = pl.ds(pl.multiple_of(part * chunk, chunk), chunk)
        logit = scaled_ref[rows, :]
        top = jnp.max(highest[rows, :], axis=1, keepdims=True)
        scaled = jnp.exp(logit - top)
        gap = jnp.sum(scaled * (logit - stud_logit_ref[rows, :]), axis=1, keepdims=True)
        scaled_ref[rows, :] = scaled
        table[rows, :] = as_columns(top, jnp.sum(scaled, axis=1, keepdims=True), gap)
        return carry

    lax.fori_loop(0, scaled_ref.shape[0] // chunk, one, 0)
    teach = table[...].T[0:8]
    row = lax.broadcasted_iota(jnp.int32, teach.shape, 0)
    stats_ref[...] = jnp.where(row < 4, teach, pltpu.roll(stud_ref[...], 4, 0))


def head_cost(rows, heads):
    depth, vocab_dev = 2 * heads[0].shape[0], heads[0].shape[1]
    return pl.CostEstimate(
        flops=2 * rows * depth * vocab_dev,
        bytes_accessed=2 * depth * vocab_dev + 12 * rows * vocab_dev,
        transcendentals=rows * vocab_dev,
    )


def logit_scratch(pieces, heads, wide, extra):
    rows, (depth, vocab_dev) = wide[0], heads[0].shape
    return (
        [pltpu.VMEM((rows, 2 * depth), jnp.bfloat16), pltpu.VMEM((2 * depth, vocab_dev), jnp.bfloat16)]
        + [pltpu.VMEM(wide, jnp.float32)] * extra
        + [pltpu.VMEM((rows, lanes), jnp.float32)] * 2
        + [pltpu.SemaphoreType.DMA((len(pieces) + 2 * len(cuts(vocab_dev, chunk_columns)) + 2,))]
    )


def student_logits(pieces, heads, column, chunk):
    rows, vocab_dev = column.shape[0], heads[0].shape[1]
    wide = (rows, vocab_dev)
    return pl.pallas_call(
        functools.partial(student_kernel, len(pieces), chunk_columns, chunk),
        in_specs=[in_place] * (len(pieces) + 2) + [in_vmem],
        out_specs=[in_place, in_place, in_vmem],
        out_shape=[
            jax.ShapeDtypeStruct(wide, jnp.float32),
            jax.ShapeDtypeStruct(wide, jnp.float32),
            jax.ShapeDtypeStruct((8, rows), jnp.float32),
        ],
        scratch_shapes=logit_scratch(pieces, heads, wide, 2),
        compiler_params=pltpu.CompilerParams(vmem_limit_bytes=vmem_bytes),
        cost_estimate=head_cost(rows, heads),
    )(*pieces, *heads, column)


def teacher_logits(pieces, heads, logit_stud, stats_stud, chunk):
    wide = logit_stud.shape
    return pl.pallas_call(
        functools.partial(teacher_kernel, len(pieces), chunk_columns, chunk),
        in_specs=[in_place] * (len(pieces) + 3) + [in_vmem],
        out_specs=[in_vmem] * 2,
        out_shape=[
            jax.ShapeDtypeStruct(wide, jnp.float32),
            jax.ShapeDtypeStruct((8, wide[0]), jnp.float32),
        ],
        scratch_shapes=logit_scratch(pieces, heads, wide, 1),
        compiler_params=pltpu.CompilerParams(vmem_limit_bytes=vmem_bytes),
        cost_estimate=head_cost(wide[0], heads),
    )(*pieces, *heads, logit_stud, stats_stud)


def swapped(values, distance):
    total = values.shape[1]
    lane = lax.broadcasted_iota(jnp.int32, values.shape, 1)
    return jnp.where(
        (lane & distance) != 0, pltpu.roll(values, distance, 1), pltpu.roll(values, total - distance, 1)
    )


def gradient_kernel(bits, step, fine, chunk, place_ref, *refs):
    count = 1 << bits
    tables, refs = refs[:count], refs[count:]
    teach, stud, column_ref, *heads, loss_ref = refs[:6]
    outs = refs[6 : count + 6]
    entries, teach_ref, stud_ref, head, upstream, factors, sems = refs[count + 6 :]
    rows = upstream.shape[0]
    blk = rows // count
    depth = heads[0].shape[0]
    me = place_ref[0]
    fetch = Fetch(sems)
    waits = [fetch.start(teach, teach_ref), fetch.start(stud, stud_ref)]
    first = fetch.used
    for half, source in enumerate(heads):
        for start, size in cuts(depth, fine):
            fetch.start(source.at[pl.ds(start, size)], head.at[pl.ds(half * depth + start, size)])
    for mask in range(count):
        values = tables[mask][...]
        for bit in range(bits):
            if mask >> bit & 1:
                values = swapped(values, blk << bit)
        entries[me ^ mask] = values
    every = entries[...]
    top_teach = jnp.max(every[:, 0:1], axis=0)
    top_stud = jnp.max(every[:, 4:5], axis=0)
    weight = jnp.exp(every[:, 0:1] - top_teach)
    total_teach = jnp.sum(weight * every[:, 1:2], axis=0)
    total_stud = jnp.sum(jnp.exp(every[:, 4:5] - top_stud) * every[:, 5:6], axis=0)
    lse_teach = top_teach + jnp.log(total_teach)
    lse_stud = top_stud + jnp.log(total_stud)
    gap = jnp.sum(weight * every[:, 2:3], axis=0) / total_teach
    loss = gap - lse_teach + 2.0 * lse_stud - jnp.sum(every[:, 6:7], axis=0)
    loss = jnp.broadcast_to(loss, loss_ref.shape)
    for bit in range(bits):
        loss = jnp.where(((me >> bit) & 1) == 1, swapped(loss, blk << bit), loss)
    loss_ref[...] = loss
    own = tables[0][...]
    scale_teach = -loss_scale * jnp.exp(own[0:1] - lse_teach)
    scale_stud = 2.0 * loss_scale * jnp.exp(own[4:5] - lse_stud)
    line = lax.broadcasted_iota(jnp.int32, (lanes, rows), 0)
    factors[...] = jnp.where(line == 0, scale_teach, scale_stud).T
    for wait in waits:
        wait.wait()

    def one(part, carry):
        at = pl.ds(pl.multiple_of(part * chunk, chunk), chunk)
        hit = lax.broadcasted_iota(jnp.int32, (chunk, teach_ref.shape[1]), 1) == column_ref[at, :]
        both = teach_ref[at, :] * factors[at, 0:1] + stud_ref[at, :] * factors[at, 1:2]
        upstream[at, :] = jnp.where(hit, both - loss_scale, both).astype(jnp.bfloat16)
        return carry

    lax.fori_loop(0, rows // chunk, one, 0)

    def two(index, carry):
        start = pl.multiple_of(index * step, step)
        for part in range(step // fine):
            at = pl.ds(start + part * fine, fine)
            sem = sems.at[first + index * (step // fine) + part]
            pltpu.make_async_copy(head.at[at], head.at[at], sem).wait()
        at = pl.ds(start, step)
        product = lax.dot_general(
            upstream[...], head[at, :], (((1,), (1,)), ((), ())), preferred_element_type=jnp.float32
        )
        for piece, out in enumerate(outs):
            out[:, at] = product[piece * blk : (piece + 1) * blk]
        return carry

    lax.fori_loop(0, 2 * depth // step, two, 0)


def gradient(place, tables, scaled_teach, scaled_stud, column, heads, bits, chunk):
    rows, vocab_dev = scaled_teach.shape
    count = 1 << bits
    depth = heads[0].shape[0]
    fine = 256 if depth % 256 == 0 else depth
    step = 512 if depth % 256 == 0 else depth
    return pl.pallas_call(
        functools.partial(gradient_kernel, bits, step, fine, chunk),
        in_specs=[in_smem] + [in_vmem] * count + [in_place] * 2 + [in_vmem] + [in_place] * 2,
        out_specs=[in_vmem] * (count + 1),
        out_shape=[jax.ShapeDtypeStruct((8, rows), jnp.float32)]
        + [jax.ShapeDtypeStruct((rows // count, 2 * depth), jnp.float32)] * count,
        scratch_shapes=[
            pltpu.VMEM((count, 8, rows), jnp.float32),
            pltpu.VMEM((rows, vocab_dev), jnp.float32),
            pltpu.VMEM((rows, vocab_dev), jnp.float32),
            pltpu.VMEM((2 * depth, vocab_dev), jnp.bfloat16),
            pltpu.VMEM((rows, vocab_dev), jnp.bfloat16),
            pltpu.VMEM((rows, lanes), jnp.float32),
            pltpu.SemaphoreType.DMA((2 + 2 * len(cuts(depth, fine)),)),
        ],
        compiler_params=pltpu.CompilerParams(vmem_limit_bytes=vmem_bytes),
        cost_estimate=head_cost(rows, heads),
    )(place, *tables, scaled_teach, scaled_stud, column, *heads)


def tie(block, *others):
    return lax.optimization_barrier((block, *others))[0]


def make_body(vocab_size):
    bits = vocab_size.bit_length() - 1
    assert vocab_size == 1 << bits

    def swap(block, bit):
        return lax.ppermute(block, "vocab", [(at, at ^ (1 << bit)) for at in range(vocab_size)])

    def lowest(mask):
        return (mask & -mask).bit_length() - 1

    def spread(own, line=None):
        blocks = [own]
        for mask in range(1, vocab_size):
            bit = lowest(mask)
            block = blocks[mask ^ (1 << bit)]
            if line is not None and bit == 0:
                block = tie(block, line[-2])
            blocks.append(swap(block, bit))
            if line is not None and bit == 0:
                line.append(blocks[-1])
        return blocks

    def reduce_blocks(parts):
        terms, line = list(parts), []
        for mask in range(vocab_size - 1, 0, -1):
            bit = lowest(mask)
            block = terms[mask].astype(wire)
            if bit == 0 and len(line) > 1:
                block = tie(block, line[-2])
            block = swap(block, bit)
            if bit == 0:
                line.append(block)
            terms[mask ^ (1 << bit)] = terms[mask ^ (1 << bit)] + block.astype(jnp.float32)
        return terms[0], line

    def body(teacher_rows, owner, counts, proj_weight, student_hidden, head_weight, targets):
        teach_rows = teacher_rows.shape[0]
        slab_rows = targets.shape[0]
        vocab_dev = head_weight.shape[1]
        blk = slab_rows // vocab_size
        chunk = min(slab_rows, 32)
        me = lax.axis_index("vocab")
        core = lax.axis_index("seq")
        place = jnp.stack([me, core]).astype(jnp.int32)

        def in_order(vec):
            grid = vec.reshape((2,) * bits + (blk,))
            for bit in range(bits):
                grid = jnp.where((me >> bit) & 1 == 1, jnp.flip(grid, bits - 1 - bit), grid)
            return grid.reshape(slab_rows)

        def turned(block):
            return jnp.where(core == 1, jnp.roll(block, block.shape[1] // 2, axis=1), block)

        def as_pieces(blocks):
            return blocks if blk % 16 == 0 else [jnp.concatenate(blocks, axis=0)]

        heads = (head_weight, lax.ppermute(head_weight, "seq", [(0, 1), (1, 0)]))

        spot = lax.iota(jnp.int32, slab_rows)
        row_id = ((spot // blk) ^ me) * blk + spot % blk
        alive = lax.iota(jnp.int32, teach_rows) < counts[0]
        member = (owner[None, :] == row_id[:, None]) & alive[None, :]
        parts = project(member.astype(jnp.bfloat16), teacher_rows, proj_weight, vocab_size, 896)
        projected_own, line = reduce_blocks(parts)
        hidden = spread(tie(turned(student_hidden), parts[-1]), line)
        projected = spread(turned(projected_own.astype(jnp.bfloat16)))

        column = (in_order(targets) - me * vocab_dev)[:, None]
        logit_stud, scaled_stud, stats_stud = student_logits(as_pieces(hidden), heads, column, chunk)
        scaled_teach, stats = teacher_logits(as_pieces(projected), heads, logit_stud, stats_stud, chunk)
        tables = [stats] + [
            lax.ppermute(stats, "vocab", [(at, at ^ mask) for at in range(vocab_size)])
            for mask in range(1, vocab_size)
        ]
        loss, *terms = gradient(place, tables, scaled_teach, scaled_stud, column, heads, bits, chunk)
        return (loss[0], turned(reduce_blocks(terms)[0].astype(jnp.bfloat16)))

    return body


def solution(mesh):
    return jax.shard_map(
        make_body(mesh.shape["vocab"]),
        mesh=mesh,
        in_specs=(
            P(("groups", "seq"), "vocab"),
            P(("groups", "seq")),
            P(("groups", "seq")),
            P("vocab", None),
            P(("groups", "seq", "vocab"), None),
            P("seq", "vocab"),
            P(("groups", "seq")),
        ),
        out_specs=(P(("groups", "seq")), P(("groups", "seq", "vocab"), None)),
        check_vma=False,
    )
```

```python
import functools

import jax
import jax.numpy as jnp
from jax import lax
from jax.experimental import pallas as pl
from jax.experimental.pallas import tpu as pltpu
from jax.sharding import PartitionSpec as P

loss_scale = 64.0
wire = jnp.float16
lanes = 128
vmem_bytes = 12 * 1024 * 1024
project_bytes = 52 * 1024 * 1024

in_vmem = pl.BlockSpec(memory_space=pltpu.VMEM)
in_smem = pl.BlockSpec(memory_space=pltpu.SMEM)
in_place = pl.BlockSpec(memory_space=pl.ANY)


def cuts(total, step):
    return [(start, min(step, total - start)) for start in range(0, total, step)]


def project_kernel(count, step, member_ref, teacher_ref, weight_ref, *rest):
    outs, (teacher, weight, aligned, sems) = rest[:count], rest[count:]
    blk = outs[0].shape[0]
    parts = cuts(weight.shape[1], step)
    first = pltpu.make_async_copy(teacher_ref, teacher, sems.at[len(parts)])
    first.start()
    for index, (start, size) in enumerate(parts):
        at = pl.ds(start, size)
        pltpu.make_async_copy(weight_ref.at[:, at], weight.at[:, at], sems.at[index]).start()
    member = member_ref[...]
    sizes = jnp.sum(member.astype(jnp.float32), axis=1, keepdims=True)
    first.wait()
    summed = jnp.dot(member, teacher[...], preferred_element_type=jnp.float32)
    aligned[...] = (summed / sizes).astype(jnp.bfloat16)

    def one(index, carry):
        at = pl.ds(pl.multiple_of(index * step, step), step)
        pltpu.make_async_copy(weight_ref.at[:, at], weight.at[:, at], sems.at[index]).wait()
        product = jnp.dot(aligned[...], weight[:, at], preferred_element_type=jnp.float32)
        for piece, out in enumerate(outs):
            out[:, at] = product[piece * blk : (piece + 1) * blk]
        return carry

    lax.fori_loop(0, len(parts), one, 0)


def project(member, teacher_rows, proj_weight, count, step):
    slab_rows, (depth, width) = member.shape[0], proj_weight.shape
    blk = slab_rows // count
    return pl.pallas_call(
        functools.partial(project_kernel, count, step),
        in_specs=[in_vmem, in_place, in_place],
        out_specs=[in_vmem] * count,
        out_shape=[jax.ShapeDtypeStruct((blk, width), jnp.float32)] * count,
        scratch_shapes=[
            pltpu.VMEM(teacher_rows.shape, jnp.bfloat16),
            pltpu.VMEM(proj_weight.shape, jnp.bfloat16),
            pltpu.VMEM((slab_rows, depth), jnp.bfloat16),
            pltpu.SemaphoreType.DMA((len(cuts(width, step)) + 1,)),
        ],
        compiler_params=pltpu.CompilerParams(vmem_limit_bytes=project_bytes),
        cost_estimate=pl.CostEstimate(
            flops=2 * slab_rows * depth * (width + teacher_rows.shape[0]),
            bytes_accessed=2 * depth * (width + teacher_rows.shape[0]) + 4 * slab_rows * width,
            transcendentals=0,
        ),
    )(member, teacher_rows, proj_weight)


class Fetch:
    def __init__(self, sems):
        self.sems, self.used = sems, 0

    def start(self, source, target):
        copy = pltpu.make_async_copy(source, target, self.sems.at[self.used])
        copy.start()
        self.used += 1
        return copy


def multiply(read_rows, head, logit_ref, highest, step, ready=None):
    total = head.shape[1]
    highest[...] = jnp.full(highest.shape, -jnp.inf, jnp.float32)

    def one(index, start, size):
        at = pl.ds(start, size)
        if ready is not None:
            ready(index, at)
        part = jnp.dot(read_rows(), head[:, at], preferred_element_type=jnp.float32)
        logit_ref[:, at] = part
        top = part[:, :lanes]
        for lane in range(lanes, size, lanes):
            top = jnp.maximum(top, part[:, lane : lane + lanes])
        highest[...] = jnp.maximum(highest[...], top)

    def body(index, carry):
        one(index, pl.multiple_of(index * step, step), step)
        return carry

    full = total // step
    lax.fori_loop(0, full, body, 0)
    if total % step:
        one(full, full * step, total % step)


def as_columns(first, second, third):
    lane = lax.broadcasted_iota(jnp.int32, (first.shape[0], lanes), 1)
    return jnp.where(lane == 0, first, jnp.where(lane == 1, second, jnp.where(lane == 2, third, 0.0)))


def student_kernel(count, step, chunk, *refs):
    pieces, heads = refs[:count], refs[count : count + 2]
    column_ref, logit_ref, scaled_ref, stats_ref, head = refs[count + 2 : count + 7]
    held, highest, table, sems = refs[count + 7 :]
    depth, total = heads[0].shape
    blk = pieces[0].shape[0]
    fetch = Fetch(sems)
    waits = [fetch.start(piece, held.at[pl.ds(i * blk, blk)]) for i, piece in enumerate(pieces)]
    first = fetch.used

    def columns(half, at):
        return heads[half].at[:, at], head.at[pl.ds(half * depth, depth), at]

    for start, size in cuts(total, step):
        for half in range(2):
            fetch.start(*columns(half, pl.ds(start, size)))

    def ready(index, at):
        for half in range(2):
            pltpu.make_async_copy(*columns(half, at), sems.at[first + 2 * index + half]).wait()

    for wait in waits:
        wait.wait()
    multiply(lambda: held[...], head, logit_ref, highest, step, ready)

    def one(part, carry):
        rows = pl.ds(pl.multiple_of(part * chunk, chunk), chunk)
        logit = logit_ref[rows, :]
        top = jnp.max(highest[rows, :], axis=1, keepdims=True)
        scaled = jnp.exp(logit - top)
        hit = lax.broadcasted_iota(jnp.int32, logit.shape, 1) == column_ref[rows, :]
        picked = jnp.sum(jnp.where(hit, logit, 0.0), axis=1, keepdims=True)
        scaled_ref[rows, :] = scaled
        table[rows, :] = as_columns(top, jnp.sum(scaled, axis=1, keepdims=True), picked)
        return carry

    lax.fori_loop(0, logit_ref.shape[0] // chunk, one, 0)
    stats_ref[...] = table[...].T[0:8]


def teacher_kernel(count, step, chunk, *refs):
    pieces = refs[:count]
    head, stud_logit_ref, stud_ref, scaled_ref, stats_ref, highest, table = refs[count:]

    def read_rows():
        return jnp.concatenate([ref[...] for ref in pieces], axis=0) if count > 1 else pieces[0][...]

    multiply(read_rows, head, scaled_ref, highest, step)

    def one(part, carry):
        rows = pl.ds(pl.multiple_of(part * chunk, chunk), chunk)
        logit = scaled_ref[rows, :]
        top = jnp.max(highest[rows, :], axis=1, keepdims=True)
        scaled = jnp.exp(logit - top)
        gap = jnp.sum(scaled * (logit - stud_logit_ref[rows, :]), axis=1, keepdims=True)
        scaled_ref[rows, :] = scaled
        table[rows, :] = as_columns(top, jnp.sum(scaled, axis=1, keepdims=True), gap)
        return carry

    lax.fori_loop(0, scaled_ref.shape[0] // chunk, one, 0)
    teach = table[...].T[0:8]
    row = lax.broadcasted_iota(jnp.int32, teach.shape, 0)
    stats_ref[...] = jnp.where(row < 4, teach, pltpu.roll(stud_ref[...], 4, 0))


def head_cost(rows, head):
    depth, vocab_dev = head.shape
    return pl.CostEstimate(
        flops=2 * rows * depth * vocab_dev,
        bytes_accessed=2 * depth * vocab_dev + 12 * rows * vocab_dev,
        transcendentals=rows * vocab_dev,
    )


def student_logits(pieces, heads, column, step, chunk):
    rows, (depth, vocab_dev) = column.shape[0], heads[0].shape
    wide = (rows, vocab_dev)
    return pl.pallas_call(
        functools.partial(student_kernel, len(pieces), step, chunk),
        in_specs=[in_place] * (len(pieces) + 2) + [in_vmem],
        out_specs=[in_vmem] * 4,
        out_shape=[
            jax.ShapeDtypeStruct(wide, jnp.float32),
            jax.ShapeDtypeStruct(wide, jnp.float32),
            jax.ShapeDtypeStruct((8, rows), jnp.float32),
            jax.ShapeDtypeStruct((2 * depth, vocab_dev), jnp.bfloat16),
        ],
        scratch_shapes=[
            pltpu.VMEM((rows, 2 * depth), jnp.bfloat16),
            pltpu.VMEM((rows, lanes), jnp.float32),
            pltpu.VMEM((rows, lanes), jnp.float32),
            pltpu.SemaphoreType.DMA((len(pieces) + 2 * len(cuts(vocab_dev, step)),)),
        ],
        compiler_params=pltpu.CompilerParams(vmem_limit_bytes=vmem_bytes),
        cost_estimate=head_cost(rows, heads[0]),
    )(*pieces, *heads, column)


def teacher_logits(pieces, head, logit_stud, stats_stud, step, chunk):
    wide = logit_stud.shape
    return pl.pallas_call(
        functools.partial(teacher_kernel, len(pieces), step, chunk),
        in_specs=[in_vmem] * (len(pieces) + 3),
        out_specs=[in_vmem] * 2,
        out_shape=[
            jax.ShapeDtypeStruct(wide, jnp.float32),
            jax.ShapeDtypeStruct((8, wide[0]), jnp.float32),
        ],
        scratch_shapes=[pltpu.VMEM((wide[0], lanes), jnp.float32)] * 2,
        compiler_params=pltpu.CompilerParams(vmem_limit_bytes=vmem_bytes),
        cost_estimate=head_cost(wide[0], head),
    )(*pieces, head, logit_stud, stats_stud)


def swapped(values, distance):
    total = values.shape[1]
    lane = lax.broadcasted_iota(jnp.int32, values.shape, 1)
    return jnp.where(
        (lane & distance) != 0, pltpu.roll(values, distance, 1), pltpu.roll(values, total - distance, 1)
    )


def gradient_kernel(bits, step, chunk, place_ref, *refs):
    count = 1 << bits
    tables, refs = refs[:count], refs[count:]
    teach_ref, stud_ref, column_ref, head, loss_ref = refs[:5]
    outs = refs[5 : count + 5]
    entries, upstream, factors = refs[count + 5 :]
    rows = upstream.shape[0]
    blk = rows // count
    me = place_ref[0]
    for mask in range(count):
        values = tables[mask][...]
        for bit in range(bits):
            if mask >> bit & 1:
                values = swapped(values, blk << bit)
        entries[me ^ mask] = values
    every = entries[...]
    top_teach = jnp.max(every[:, 0:1], axis=0)
    top_stud = jnp.max(every[:, 4:5], axis=0)
    weight = jnp.exp(every[:, 0:1] - top_teach)
    total_teach = jnp.sum(weight * every[:, 1:2], axis=0)
    total_stud = jnp.sum(jnp.exp(every[:, 4:5] - top_stud) * every[:, 5:6], axis=0)
    lse_teach = top_teach + jnp.log(total_teach)
    lse_stud = top_stud + jnp.log(total_stud)
    gap = jnp.sum(weight * every[:, 2:3], axis=0) / total_teach
    loss = gap - lse_teach + 2.0 * lse_stud - jnp.sum(every[:, 6:7], axis=0)
    loss = jnp.broadcast_to(loss, loss_ref.shape)
    for bit in range(bits):
        loss = jnp.where(((me >> bit) & 1) == 1, swapped(loss, blk << bit), loss)
    loss_ref[...] = loss
    own = tables[0][...]
    scale_teach = -loss_scale * jnp.exp(own[0:1] - lse_teach)
    scale_stud = 2.0 * loss_scale * jnp.exp(own[4:5] - lse_stud)
    line = lax.broadcasted_iota(jnp.int32, (lanes, rows), 0)
    factors[...] = jnp.where(line == 0, scale_teach, scale_stud).T

    def one(part, carry):
        at = pl.ds(pl.multiple_of(part * chunk, chunk), chunk)
        hit = lax.broadcasted_iota(jnp.int32, (chunk, teach_ref.shape[1]), 1) == column_ref[at, :]
        both = teach_ref[at, :] * factors[at, 0:1] + stud_ref[at, :] * factors[at, 1:2]
        upstream[at, :] = jnp.where(hit, both - loss_scale, both).astype(jnp.bfloat16)
        return carry

    lax.fori_loop(0, rows // chunk, one, 0)

    def two(index, carry):
        at = pl.ds(pl.multiple_of(index * step, step), step)
        product = lax.dot_general(
            upstream[...], head[at, :], (((1,), (1,)), ((), ())), preferred_element_type=jnp.float32
        )
        for piece, out in enumerate(outs):
            out[:, at] = product[piece * blk : (piece + 1) * blk]
        return carry

    lax.fori_loop(0, head.shape[0] // step, two, 0)


def gradient(place, tables, scaled_teach, scaled_stud, column, head, bits, chunk):
    rows, vocab_dev = scaled_teach.shape
    count, width = 1 << bits, head.shape[0]
    step = 512 if width % 512 == 0 else width
    return pl.pallas_call(
        functools.partial(gradient_kernel, bits, step, chunk),
        in_specs=[in_smem] + [in_vmem] * (count + 4),
        out_specs=[in_vmem] * (count + 1),
        out_shape=[jax.ShapeDtypeStruct((8, rows), jnp.float32)]
        + [jax.ShapeDtypeStruct((rows // count, width), jnp.float32)] * count,
        scratch_shapes=[
            pltpu.VMEM((count, 8, rows), jnp.float32),
            pltpu.VMEM((rows, vocab_dev), jnp.bfloat16),
            pltpu.VMEM((rows, lanes), jnp.float32),
        ],
        compiler_params=pltpu.CompilerParams(vmem_limit_bytes=vmem_bytes),
        cost_estimate=head_cost(rows, head),
    )(place, *tables, scaled_teach, scaled_stud, column, head)


def tie(block, *others):
    return lax.optimization_barrier((block, *others))[0]


def make_body(vocab_size):
    bits = vocab_size.bit_length() - 1
    assert vocab_size == 1 << bits

    def swap(block, bit):
        return lax.ppermute(block, "vocab", [(at, at ^ (1 << bit)) for at in range(vocab_size)])

    def lowest(mask):
        return (mask & -mask).bit_length() - 1

    def spread(own, line):
        blocks = [own]
        for mask in range(1, vocab_size):
            bit = lowest(mask)
            block = blocks[mask ^ (1 << bit)]
            if bit == 0:
                block = tie(block, line[-2])
            blocks.append(swap(block, bit))
            if bit == 0:
                line.append(blocks[-1])
        return blocks

    def reduce_blocks(parts):
        terms, line = list(parts), []
        for mask in range(vocab_size - 1, 0, -1):
            bit = lowest(mask)
            block = terms[mask].astype(wire)
            if bit == 0 and line:
                block = tie(block, line[-1])
            block = swap(block, bit)
            if bit == 0:
                line.append(block)
            terms[mask ^ (1 << bit)] = terms[mask ^ (1 << bit)] + block.astype(jnp.float32)
        return terms[0], line

    def body(teacher_rows, owner, counts, proj_weight, student_hidden, head_weight, targets):
        teach_rows = teacher_rows.shape[0]
        slab_rows = targets.shape[0]
        vocab_dev = head_weight.shape[1]
        blk = slab_rows // vocab_size
        chunk = min(slab_rows, 32)
        me = lax.axis_index("vocab")
        core = lax.axis_index("seq")
        place = jnp.stack([me, core]).astype(jnp.int32)

        def in_order(vec):
            grid = vec.reshape((2,) * bits + (blk,))
            for bit in range(bits):
                grid = jnp.where((me >> bit) & 1 == 1, jnp.flip(grid, bits - 1 - bit), grid)
            return grid.reshape(slab_rows)

        def turned(block):
            return jnp.where(core == 1, jnp.roll(block, block.shape[1] // 2, axis=1), block)

        def as_pieces(blocks):
            return blocks if blk % 16 == 0 else [jnp.concatenate(blocks, axis=0)]

        heads = (head_weight, lax.ppermute(head_weight, "seq", [(0, 1), (1, 0)]))

        spot = lax.iota(jnp.int32, slab_rows)
        row_id = ((spot // blk) ^ me) * blk + spot % blk
        alive = lax.iota(jnp.int32, teach_rows) < counts[0]
        member = (owner[None, :] == row_id[:, None]) & alive[None, :]
        parts = project(member.astype(jnp.bfloat16), teacher_rows, proj_weight, vocab_size, 512 if student_hidden.shape[1] % 512 == 0 else student_hidden.shape[1])
        projected_own, line = reduce_blocks(parts)
        line.append(line[-1])
        hidden = spread(tie(turned(student_hidden), parts[-1]), line)
        projected = spread(turned(projected_own.astype(jnp.bfloat16)), line)

        column = (in_order(targets) - me * vocab_dev)[:, None]
        logit_stud, scaled_stud, stats_stud, head = student_logits(as_pieces(hidden), heads, column, 256, chunk)
        scaled_teach, stats = teacher_logits(as_pieces(projected), head, logit_stud, stats_stud, 512, chunk)
        tables = [stats] + [
            lax.ppermute(stats, "vocab", [(at, at ^ mask) for at in range(vocab_size)])
            for mask in range(1, vocab_size)
        ]
        loss, *terms = gradient(place, tables, scaled_teach, scaled_stud, column, head, bits, chunk)
        return (loss[0], turned(reduce_blocks(terms)[0].astype(jnp.bfloat16)))

    return body


def solution(mesh):
    return jax.shard_map(
        make_body(mesh.shape["vocab"]),
        mesh=mesh,
        in_specs=(
            P(("groups", "seq"), "vocab"),
            P(("groups", "seq")),
            P(("groups", "seq")),
            P("vocab", None),
            P(("groups", "seq", "vocab"), None),
            P("seq", "vocab"),
            P(("groups", "seq")),
        ),
        out_specs=(P(("groups", "seq")), P(("groups", "seq", "vocab"), None)),
        check_vma=False,
    )
```

```python
import functools

import jax
import jax.numpy as jnp
from jax import lax
from jax.experimental import pallas as pl
from jax.experimental.pallas import tpu as pltpu
from jax.sharding import PartitionSpec as P

loss_scale = 64.0
wire = jnp.float16
lanes = 128
vmem_bytes = 12 * 1024 * 1024
project_bytes = 50 * 1024 * 1024

in_vmem = pl.BlockSpec(memory_space=pltpu.VMEM)
in_smem = pl.BlockSpec(memory_space=pltpu.SMEM)
in_place = pl.BlockSpec(memory_space=pl.ANY)


def cuts(total, step):
    return [(start, min(step, total - start)) for start in range(0, total, step)]


def project_kernel(count, step, member_ref, teacher_ref, weight_ref, *rest):
    outs, (teacher, weight, aligned, sems) = rest[:count], rest[count:]
    blk = outs[0].shape[0]
    parts = cuts(weight.shape[1], step)
    first = pltpu.make_async_copy(teacher_ref, teacher, sems.at[len(parts)])
    first.start()
    for index, (start, size) in enumerate(parts):
        at = pl.ds(start, size)
        pltpu.make_async_copy(weight_ref.at[:, at], weight.at[:, at], sems.at[index]).start()
    member = member_ref[...]
    sizes = jnp.sum(member.astype(jnp.float32), axis=1, keepdims=True)
    first.wait()
    summed = jnp.dot(member, teacher[...], preferred_element_type=jnp.float32)
    aligned[...] = (summed / sizes).astype(jnp.bfloat16)

    def one(index, carry):
        at = pl.ds(pl.multiple_of(index * step, step), step)
        pltpu.make_async_copy(weight_ref.at[:, at], weight.at[:, at], sems.at[index]).wait()
        product = jnp.dot(aligned[...], weight[:, at], preferred_element_type=jnp.float32)
        for piece, out in enumerate(outs):
            out[:, at] = product[piece * blk : (piece + 1) * blk]
        return carry

    lax.fori_loop(0, len(parts), one, 0)


def project(member, teacher_rows, proj_weight, count, step):
    slab_rows, (depth, width) = member.shape[0], proj_weight.shape
    blk = slab_rows // count
    return pl.pallas_call(
        functools.partial(project_kernel, count, step),
        in_specs=[in_vmem, in_place, in_place],
        out_specs=[in_vmem] * count,
        out_shape=[jax.ShapeDtypeStruct((blk, width), jnp.float32)] * count,
        scratch_shapes=[
            pltpu.VMEM(teacher_rows.shape, jnp.bfloat16),
            pltpu.VMEM(proj_weight.shape, jnp.bfloat16),
            pltpu.VMEM((slab_rows, depth), jnp.bfloat16),
            pltpu.SemaphoreType.DMA((len(cuts(width, step)) + 1,)),
        ],
        compiler_params=pltpu.CompilerParams(vmem_limit_bytes=project_bytes),
        cost_estimate=pl.CostEstimate(
            flops=2 * slab_rows * depth * (width + teacher_rows.shape[0]),
            bytes_accessed=2 * depth * (width + teacher_rows.shape[0]) + 4 * slab_rows * width,
            transcendentals=0,
        ),
    )(member, teacher_rows, proj_weight)


class Fetch:
    def __init__(self, sems):
        self.sems, self.used = sems, 0

    def start(self, source, target):
        copy = pltpu.make_async_copy(source, target, self.sems.at[self.used])
        copy.start()
        self.used += 1
        return copy


def multiply(read_rows, head, logit_ref, highest, step, ready=None):
    total = head.shape[1]
    highest[...] = jnp.full(highest.shape, -jnp.inf, jnp.float32)

    def one(index, start, size):
        at = pl.ds(start, size)
        if ready is not None:
            ready(index, at)
        part = jnp.dot(read_rows(), head[:, at], preferred_element_type=jnp.float32)
        logit_ref[:, at] = part
        top = part[:, :lanes]
        for lane in range(lanes, size, lanes):
            top = jnp.maximum(top, part[:, lane : lane + lanes])
        highest[...] = jnp.maximum(highest[...], top)

    def body(index, carry):
        one(index, pl.multiple_of(index * step, step), step)
        return carry

    full = total // step
    lax.fori_loop(0, full, body, 0)
    if total % step:
        one(full, full * step, total % step)


def as_columns(first, second, third):
    lane = lax.broadcasted_iota(jnp.int32, (first.shape[0], lanes), 1)
    return jnp.where(lane == 0, first, jnp.where(lane == 1, second, jnp.where(lane == 2, third, 0.0)))


def student_kernel(count, step, chunk, *refs):
    pieces, heads = refs[:count], refs[count : count + 2]
    column_ref, logit_ref, scaled_ref, stats_ref, head = refs[count + 2 : count + 7]
    held, highest, table, sems = refs[count + 7 :]
    depth, total = heads[0].shape
    blk = pieces[0].shape[0]
    fetch = Fetch(sems)
    waits = [fetch.start(piece, held.at[pl.ds(i * blk, blk)]) for i, piece in enumerate(pieces)]
    first = fetch.used

    def columns(half, at):
        return heads[half].at[:, at], head.at[pl.ds(half * depth, depth), at]

    for start, size in cuts(total, step):
        for half in range(2):
            fetch.start(*columns(half, pl.ds(start, size)))

    def ready(index, at):
        for half in range(2):
            pltpu.make_async_copy(*columns(half, at), sems.at[first + 2 * index + half]).wait()

    for wait in waits:
        wait.wait()
    multiply(lambda: held[...], head, logit_ref, highest, step, ready)

    def one(part, carry):
        rows = pl.ds(pl.multiple_of(part * chunk, chunk), chunk)
        logit = logit_ref[rows, :]
        top = jnp.max(highest[rows, :], axis=1, keepdims=True)
        scaled = jnp.exp(logit - top)
        hit = lax.broadcasted_iota(jnp.int32, logit.shape, 1) == column_ref[rows, :]
        picked = jnp.sum(jnp.where(hit, logit, 0.0), axis=1, keepdims=True)
        scaled_ref[rows, :] = scaled
        table[rows, :] = as_columns(top, jnp.sum(scaled, axis=1, keepdims=True), picked)
        return carry

    lax.fori_loop(0, logit_ref.shape[0] // chunk, one, 0)
    stats_ref[...] = table[...].T[0:8]


def teacher_kernel(count, step, chunk, *refs):
    pieces = refs[:count]
    head, stud_logit_ref, stud_ref, scaled_ref, stats_ref, highest, table = refs[count:]

    def read_rows():
        return jnp.concatenate([ref[...] for ref in pieces], axis=0) if count > 1 else pieces[0][...]

    multiply(read_rows, head, scaled_ref, highest, step)

    def one(part, carry):
        rows = pl.ds(pl.multiple_of(part * chunk, chunk), chunk)
        logit = scaled_ref[rows, :]
        top = jnp.max(highest[rows, :], axis=1, keepdims=True)
        scaled = jnp.exp(logit - top)
        gap = jnp.sum(scaled * (logit - stud_logit_ref[rows, :]), axis=1, keepdims=True)
        scaled_ref[rows, :] = scaled
        table[rows, :] = as_columns(top, jnp.sum(scaled, axis=1, keepdims=True), gap)
        return carry

    lax.fori_loop(0, scaled_ref.shape[0] // chunk, one, 0)
    teach = table[...].T[0:8]
    row = lax.broadcasted_iota(jnp.int32, teach.shape, 0)
    stats_ref[...] = jnp.where(row < 4, teach, pltpu.roll(stud_ref[...], 4, 0))


def head_cost(rows, head):
    depth, vocab_dev = head.shape
    return pl.CostEstimate(
        flops=2 * rows * depth * vocab_dev,
        bytes_accessed=2 * depth * vocab_dev + 12 * rows * vocab_dev,
        transcendentals=rows * vocab_dev,
    )


def student_logits(pieces, heads, column, step, chunk):
    rows, (depth, vocab_dev) = column.shape[0], heads[0].shape
    wide = (rows, vocab_dev)
    return pl.pallas_call(
        functools.partial(student_kernel, len(pieces), step, chunk),
        in_specs=[in_place] * (len(pieces) + 2) + [in_vmem],
        out_specs=[in_vmem] * 4,
        out_shape=[
            jax.ShapeDtypeStruct(wide, jnp.float32),
            jax.ShapeDtypeStruct(wide, jnp.float32),
            jax.ShapeDtypeStruct((8, rows), jnp.float32),
            jax.ShapeDtypeStruct((2 * depth, vocab_dev), jnp.bfloat16),
        ],
        scratch_shapes=[
            pltpu.VMEM((rows, 2 * depth), jnp.bfloat16),
            pltpu.VMEM((rows, lanes), jnp.float32),
            pltpu.VMEM((rows, lanes), jnp.float32),
            pltpu.SemaphoreType.DMA((len(pieces) + 2 * len(cuts(vocab_dev, step)),)),
        ],
        compiler_params=pltpu.CompilerParams(vmem_limit_bytes=vmem_bytes),
        cost_estimate=head_cost(rows, heads[0]),
    )(*pieces, *heads, column)


def teacher_logits(pieces, head, logit_stud, stats_stud, step, chunk):
    wide = logit_stud.shape
    return pl.pallas_call(
        functools.partial(teacher_kernel, len(pieces), step, chunk),
        in_specs=[in_vmem] * (len(pieces) + 3),
        out_specs=[in_vmem] * 2,
        out_shape=[
            jax.ShapeDtypeStruct(wide, jnp.float32),
            jax.ShapeDtypeStruct((8, wide[0]), jnp.float32),
        ],
        scratch_shapes=[pltpu.VMEM((wide[0], lanes), jnp.float32)] * 2,
        compiler_params=pltpu.CompilerParams(vmem_limit_bytes=vmem_bytes),
        cost_estimate=head_cost(wide[0], head),
    )(*pieces, head, logit_stud, stats_stud)


def swapped(values, distance):
    total = values.shape[1]
    lane = lax.broadcasted_iota(jnp.int32, values.shape, 1)
    return jnp.where(
        (lane & distance) != 0, pltpu.roll(values, distance, 1), pltpu.roll(values, total - distance, 1)
    )


def gradient_kernel(bits, step, chunk, place_ref, *refs):
    count = 1 << bits
    tables, refs = refs[:count], refs[count:]
    teach_ref, stud_ref, column_ref, head, loss_ref = refs[:5]
    outs = refs[5 : count + 5]
    entries, upstream, factors = refs[count + 5 :]
    rows = upstream.shape[0]
    blk = rows // count
    me = place_ref[0]
    for mask in range(count):
        values = tables[mask][...]
        for bit in range(bits):
            if mask >> bit & 1:
                values = swapped(values, blk << bit)
        entries[me ^ mask] = values
    every = entries[...]
    top_teach = jnp.max(every[:, 0:1], axis=0)
    top_stud = jnp.max(every[:, 4:5], axis=0)
    weight = jnp.exp(every[:, 0:1] - top_teach)
    total_teach = jnp.sum(weight * every[:, 1:2], axis=0)
    total_stud = jnp.sum(jnp.exp(every[:, 4:5] - top_stud) * every[:, 5:6], axis=0)
    lse_teach = top_teach + jnp.log(total_teach)
    lse_stud = top_stud + jnp.log(total_stud)
    gap = jnp.sum(weight * every[:, 2:3], axis=0) / total_teach
    loss = gap - lse_teach + 2.0 * lse_stud - jnp.sum(every[:, 6:7], axis=0)
    loss = jnp.broadcast_to(loss, loss_ref.shape)
    for bit in range(bits):
        loss = jnp.where(((me >> bit) & 1) == 1, swapped(loss, blk << bit), loss)
    loss_ref[...] = loss
    own = tables[0][...]
    scale_teach = -loss_scale * jnp.exp(own[0:1] - lse_teach)
    scale_stud = 2.0 * loss_scale * jnp.exp(own[4:5] - lse_stud)
    line = lax.broadcasted_iota(jnp.int32, (lanes, rows), 0)
    factors[...] = jnp.where(line == 0, scale_teach, scale_stud).T

    def one(part, carry):
        at = pl.ds(pl.multiple_of(part * chunk, chunk), chunk)
        hit = lax.broadcasted_iota(jnp.int32, (chunk, teach_ref.shape[1]), 1) == column_ref[at, :]
        both = teach_ref[at, :] * factors[at, 0:1] + stud_ref[at, :] * factors[at, 1:2]
        upstream[at, :] = jnp.where(hit, both - loss_scale, both).astype(jnp.bfloat16)
        return carry

    lax.fori_loop(0, rows // chunk, one, 0)

    def two(index, carry):
        at = pl.ds(pl.multiple_of(index * step, step), step)
        product = lax.dot_general(
            upstream[...], head[at, :], (((1,), (1,)), ((), ())), preferred_element_type=jnp.float32
        )
        for piece, out in enumerate(outs):
            out[:, at] = product[piece * blk : (piece + 1) * blk]
        return carry

    lax.fori_loop(0, head.shape[0] // step, two, 0)


def gradient(place, tables, scaled_teach, scaled_stud, column, head, bits, chunk):
    rows, vocab_dev = scaled_teach.shape
    count, width = 1 << bits, head.shape[0]
    step = 512 if width % 512 == 0 else width
    return pl.pallas_call(
        functools.partial(gradient_kernel, bits, step, chunk),
        in_specs=[in_smem] + [in_vmem] * (count + 4),
        out_specs=[in_vmem] * (count + 1),
        out_shape=[jax.ShapeDtypeStruct((8, rows), jnp.float32)]
        + [jax.ShapeDtypeStruct((rows // count, width), jnp.float32)] * count,
        scratch_shapes=[
            pltpu.VMEM((count, 8, rows), jnp.float32),
            pltpu.VMEM((rows, vocab_dev), jnp.bfloat16),
            pltpu.VMEM((rows, lanes), jnp.float32),
        ],
        compiler_params=pltpu.CompilerParams(vmem_limit_bytes=vmem_bytes),
        cost_estimate=head_cost(rows, head),
    )(place, *tables, scaled_teach, scaled_stud, column, head)


def tie(block, *others):
    return lax.optimization_barrier((block, *others))[0]


def make_body(vocab_size):
    bits = vocab_size.bit_length() - 1
    assert vocab_size == 1 << bits

    def swap(block, bit):
        return lax.ppermute(block, "vocab", [(at, at ^ (1 << bit)) for at in range(vocab_size)])

    def lowest(mask):
        return (mask & -mask).bit_length() - 1

    def spread(own, line):
        blocks = [own]
        for mask in range(1, vocab_size):
            bit = lowest(mask)
            block = blocks[mask ^ (1 << bit)]
            if bit == 0:
                block = tie(block, line[-3])
            blocks.append(swap(block, bit))
            if bit == 0:
                line.append(blocks[-1])
        return blocks

    def reduce_blocks(parts):
        terms, line = list(parts), []
        for mask in range(vocab_size - 1, 0, -1):
            bit = lowest(mask)
            block = terms[mask].astype(wire)
            if bit == 0 and len(line) > 1:
                block = tie(block, line[-2])
            block = swap(block, bit)
            if bit == 0:
                line.append(block)
            terms[mask ^ (1 << bit)] = terms[mask ^ (1 << bit)] + block.astype(jnp.float32)
        return terms[0], line

    def body(teacher_rows, owner, counts, proj_weight, student_hidden, head_weight, targets):
        teach_rows = teacher_rows.shape[0]
        slab_rows = targets.shape[0]
        vocab_dev = head_weight.shape[1]
        blk = slab_rows // vocab_size
        chunk = min(slab_rows, 32)
        me = lax.axis_index("vocab")
        core = lax.axis_index("seq")
        place = jnp.stack([me, core]).astype(jnp.int32)

        def in_order(vec):
            grid = vec.reshape((2,) * bits + (blk,))
            for bit in range(bits):
                grid = jnp.where((me >> bit) & 1 == 1, jnp.flip(grid, bits - 1 - bit), grid)
            return grid.reshape(slab_rows)

        def turned(block):
            return jnp.where(core == 1, jnp.roll(block, block.shape[1] // 2, axis=1), block)

        def as_pieces(blocks):
            return blocks if blk % 16 == 0 else [jnp.concatenate(blocks, axis=0)]

        heads = (head_weight, lax.ppermute(head_weight, "seq", [(0, 1), (1, 0)]))

        spot = lax.iota(jnp.int32, slab_rows)
        row_id = ((spot // blk) ^ me) * blk + spot % blk
        alive = lax.iota(jnp.int32, teach_rows) < counts[0]
        member = (owner[None, :] == row_id[:, None]) & alive[None, :]
        parts = project(member.astype(jnp.bfloat16), teacher_rows, proj_weight, vocab_size, 512 if student_hidden.shape[1] % 512 == 0 else student_hidden.shape[1])
        projected_own, line = reduce_blocks(parts)
        hidden = spread(tie(turned(student_hidden), parts[-1]), line)
        projected = spread(turned(projected_own.astype(jnp.bfloat16)), line)

        column = (in_order(targets) - me * vocab_dev)[:, None]
        logit_stud, scaled_stud, stats_stud, head = student_logits(as_pieces(hidden), heads, column, 256, chunk)
        scaled_teach, stats = teacher_logits(as_pieces(projected), head, logit_stud, stats_stud, 512, chunk)
        tables = [stats] + [
            lax.ppermute(stats, "vocab", [(at, at ^ mask) for at in range(vocab_size)])
            for mask in range(1, vocab_size)
        ]
        loss, *terms = gradient(place, tables, scaled_teach, scaled_stud, column, head, bits, chunk)
        return (loss[0], turned(reduce_blocks(terms)[0].astype(jnp.bfloat16)))

    return body


def solution(mesh):
    return jax.shard_map(
        make_body(mesh.shape["vocab"]),
        mesh=mesh,
        in_specs=(
            P(("groups", "seq"), "vocab"),
            P(("groups", "seq")),
            P(("groups", "seq")),
            P("vocab", None),
            P(("groups", "seq", "vocab"), None),
            P("seq", "vocab"),
            P(("groups", "seq")),
        ),
        out_specs=(P(("groups", "seq")), P(("groups", "seq", "vocab"), None)),
        check_vma=False,
    )
```

```python
import functools

import jax
import jax.numpy as jnp
from jax import lax
from jax.experimental import pallas as pl
from jax.experimental.pallas import tpu as pltpu
from jax.sharding import PartitionSpec as P

loss_scale = 64.0
wire = jnp.float16
lanes = 128
vmem_bytes = 12 * 1024 * 1024
student_bytes = 12 * 1024 * 1024
project_bytes = 50 * 1024 * 1024

in_vmem = pl.BlockSpec(memory_space=pltpu.VMEM)
in_smem = pl.BlockSpec(memory_space=pltpu.SMEM)
in_place = pl.BlockSpec(memory_space=pl.ANY)


def cuts(total, step):
    return [(start, min(step, total - start)) for start in range(0, total, step)]


def project_kernel(count, step, member_ref, teacher_ref, weight_ref, *rest):
    outs, (teacher, weight, aligned, sems) = rest[:count], rest[count:]
    blk = outs[0].shape[0]
    parts = cuts(weight.shape[1], step)
    first = pltpu.make_async_copy(teacher_ref, teacher, sems.at[len(parts)])
    first.start()
    for index, (start, size) in enumerate(parts):
        at = pl.ds(start, size)
        pltpu.make_async_copy(weight_ref.at[:, at], weight.at[:, at], sems.at[index]).start()
    member = member_ref[...]
    sizes = jnp.sum(member.astype(jnp.float32), axis=1, keepdims=True)
    first.wait()
    summed = jnp.dot(member, teacher[...], preferred_element_type=jnp.float32)
    aligned[...] = (summed / sizes).astype(jnp.bfloat16)

    def one(index, carry):
        at = pl.ds(pl.multiple_of(index * step, step), step)
        pltpu.make_async_copy(weight_ref.at[:, at], weight.at[:, at], sems.at[index]).wait()
        product = jnp.dot(aligned[...], weight[:, at], preferred_element_type=jnp.float32)
        for piece, out in enumerate(outs):
            out[:, at] = product[piece * blk : (piece + 1) * blk]
        return carry

    lax.fori_loop(0, len(parts), one, 0)


def project(member, teacher_rows, proj_weight, count, step):
    slab_rows, (depth, width) = member.shape[0], proj_weight.shape
    blk = slab_rows // count
    return pl.pallas_call(
        functools.partial(project_kernel, count, step),
        in_specs=[in_vmem, in_place, in_place],
        out_specs=[in_vmem] * count,
        out_shape=[jax.ShapeDtypeStruct((blk, width), jnp.float32)] * count,
        scratch_shapes=[
            pltpu.VMEM(teacher_rows.shape, jnp.bfloat16),
            pltpu.VMEM(proj_weight.shape, jnp.bfloat16),
            pltpu.VMEM((slab_rows, depth), jnp.bfloat16),
            pltpu.SemaphoreType.DMA((len(cuts(width, step)) + 1,)),
        ],
        compiler_params=pltpu.CompilerParams(vmem_limit_bytes=project_bytes),
        cost_estimate=pl.CostEstimate(
            flops=2 * slab_rows * depth * (width + teacher_rows.shape[0]),
            bytes_accessed=2 * depth * (width + teacher_rows.shape[0]) + 4 * slab_rows * width,
            transcendentals=0,
        ),
    )(member, teacher_rows, proj_weight)


class Fetch:
    def __init__(self, sems):
        self.sems, self.used = sems, 0

    def start(self, source, target):
        copy = pltpu.make_async_copy(source, target, self.sems.at[self.used])
        copy.start()
        self.used += 1
        return copy


def multiply(read_rows, head, logit_ref, highest, step, ready=None):
    total = head.shape[1]
    highest[...] = jnp.full(highest.shape, -jnp.inf, jnp.float32)

    def one(index, start, size):
        at = pl.ds(start, size)
        if ready is not None:
            ready(index, at)
        part = jnp.dot(read_rows(), head[:, at], preferred_element_type=jnp.float32)
        logit_ref[:, at] = part
        top = part[:, :lanes]
        for lane in range(lanes, size, lanes):
            top = jnp.maximum(top, part[:, lane : lane + lanes])
        highest[...] = jnp.maximum(highest[...], top)

    def body(index, carry):
        one(index, pl.multiple_of(index * step, step), step)
        return carry

    full = total // step
    lax.fori_loop(0, full, body, 0)
    if total % step:
        one(full, full * step, total % step)


def as_columns(first, second, third):
    lane = lax.broadcasted_iota(jnp.int32, (first.shape[0], lanes), 1)
    return jnp.where(lane == 0, first, jnp.where(lane == 1, second, jnp.where(lane == 2, third, 0.0)))


def student_kernel(count, step, chunk, *refs):
    pieces, heads = refs[:count], refs[count : count + 2]
    column_ref, logit_ref, scaled_ref, stats_ref, head = refs[count + 2 : count + 7]
    held, highest, table, sems = refs[count + 7 :]
    depth, total = heads[0].shape
    blk = pieces[0].shape[0]
    fetch = Fetch(sems)
    waits = [fetch.start(piece, held.at[pl.ds(i * blk, blk)]) for i, piece in enumerate(pieces)]
    first = fetch.used

    def columns(half, at):
        return heads[half].at[:, at], head.at[pl.ds(half * depth, depth), at]

    for start, size in cuts(total, step):
        for half in range(2):
            fetch.start(*columns(half, pl.ds(start, size)))

    def ready(index, at):
        for half in range(2):
            pltpu.make_async_copy(*columns(half, at), sems.at[first + 2 * index + half]).wait()

    for wait in waits:
        wait.wait()
    multiply(lambda: held[...], head, logit_ref, highest, step, ready)

    def one(part, carry):
        rows = pl.ds(pl.multiple_of(part * chunk, chunk), chunk)
        logit = logit_ref[rows, :]
        top = jnp.max(highest[rows, :], axis=1, keepdims=True)
        scaled = jnp.exp(logit - top)
        hit = lax.broadcasted_iota(jnp.int32, logit.shape, 1) == column_ref[rows, :]
        picked = jnp.sum(jnp.where(hit, logit, 0.0), axis=1, keepdims=True)
        scaled_ref[rows, :] = scaled
        table[rows, :] = as_columns(top, jnp.sum(scaled, axis=1, keepdims=True), picked)
        return carry

    lax.fori_loop(0, logit_ref.shape[0] // chunk, one, 0)
    stats_ref[...] = table[...].T[0:8]


def teacher_kernel(count, step, chunk, *refs):
    pieces = refs[:count]
    head, stud_logit_ref, stud_ref, scaled_ref, stats_ref, highest, table = refs[count:]

    def read_rows():
        return jnp.concatenate([ref[...] for ref in pieces], axis=0) if count > 1 else pieces[0][...]

    multiply(read_rows, head, scaled_ref, highest, step)

    def one(part, carry):
        rows = pl.ds(pl.multiple_of(part * chunk, chunk), chunk)
        logit = scaled_ref[rows, :]
        top = jnp.max(highest[rows, :], axis=1, keepdims=True)
        scaled = jnp.exp(logit - top)
        gap = jnp.sum(scaled * (logit - stud_logit_ref[rows, :]), axis=1, keepdims=True)
        scaled_ref[rows, :] = scaled
        table[rows, :] = as_columns(top, jnp.sum(scaled, axis=1, keepdims=True), gap)
        return carry

    lax.fori_loop(0, scaled_ref.shape[0] // chunk, one, 0)
    teach = table[...].T[0:8]
    row = lax.broadcasted_iota(jnp.int32, teach.shape, 0)
    stats_ref[...] = jnp.where(row < 4, teach, pltpu.roll(stud_ref[...], 4, 0))


def head_cost(rows, head):
    depth, vocab_dev = head.shape
    return pl.CostEstimate(
        flops=2 * rows * depth * vocab_dev,
        bytes_accessed=2 * depth * vocab_dev + 12 * rows * vocab_dev,
        transcendentals=rows * vocab_dev,
    )


def student_logits(pieces, heads, column, step, chunk):
    rows, (depth, vocab_dev) = column.shape[0], heads[0].shape
    wide = (rows, vocab_dev)
    return pl.pallas_call(
        functools.partial(student_kernel, len(pieces), step, chunk),
        in_specs=[in_place] * (len(pieces) + 2) + [in_vmem],
        out_specs=[in_vmem] * 4,
        out_shape=[
            jax.ShapeDtypeStruct(wide, jnp.float32),
            jax.ShapeDtypeStruct(wide, jnp.float32),
            jax.ShapeDtypeStruct((8, rows), jnp.float32),
            jax.ShapeDtypeStruct((2 * depth, vocab_dev), jnp.bfloat16),
        ],
        scratch_shapes=[
            pltpu.VMEM((rows, 2 * depth), jnp.bfloat16),
            pltpu.VMEM((rows, lanes), jnp.float32),
            pltpu.VMEM((rows, lanes), jnp.float32),
            pltpu.SemaphoreType.DMA((len(pieces) + 2 * len(cuts(vocab_dev, step)),)),
        ],
        compiler_params=pltpu.CompilerParams(vmem_limit_bytes=student_bytes),
        cost_estimate=head_cost(rows, heads[0]),
    )(*pieces, *heads, column)


def teacher_logits(pieces, head, logit_stud, stats_stud, step, chunk):
    wide = logit_stud.shape
    return pl.pallas_call(
        functools.partial(teacher_kernel, len(pieces), step, chunk),
        in_specs=[in_vmem] * (len(pieces) + 3),
        out_specs=[in_vmem] * 2,
        out_shape=[
            jax.ShapeDtypeStruct(wide, jnp.float32),
            jax.ShapeDtypeStruct((8, wide[0]), jnp.float32),
        ],
        scratch_shapes=[pltpu.VMEM((wide[0], lanes), jnp.float32)] * 2,
        compiler_params=pltpu.CompilerParams(vmem_limit_bytes=vmem_bytes),
        cost_estimate=head_cost(wide[0], head),
    )(*pieces, head, logit_stud, stats_stud)


def swapped(values, distance):
    total = values.shape[1]
    lane = lax.broadcasted_iota(jnp.int32, values.shape, 1)
    return jnp.where(
        (lane & distance) != 0, pltpu.roll(values, distance, 1), pltpu.roll(values, total - distance, 1)
    )


def gradient_kernel(bits, step, chunk, place_ref, *refs):
    count = 1 << bits
    tables, refs = refs[:count], refs[count:]
    teach_ref, stud_ref, column_ref, head, loss_ref = refs[:5]
    outs = refs[5 : count + 5]
    entries, upstream, factors = refs[count + 5 :]
    rows = upstream.shape[0]
    blk = rows // count
    me = place_ref[0]
    for mask in range(count):
        values = tables[mask][...]
        for bit in range(bits):
            if mask >> bit & 1:
                values = swapped(values, blk << bit)
        entries[me ^ mask] = values
    every = entries[...]
    top_teach = jnp.max(every[:, 0:1], axis=0)
    top_stud = jnp.max(every[:, 4:5], axis=0)
    weight = jnp.exp(every[:, 0:1] - top_teach)
    total_teach = jnp.sum(weight * every[:, 1:2], axis=0)
    total_stud = jnp.sum(jnp.exp(every[:, 4:5] - top_stud) * every[:, 5:6], axis=0)
    lse_teach = top_teach + jnp.log(total_teach)
    lse_stud = top_stud + jnp.log(total_stud)
    gap = jnp.sum(weight * every[:, 2:3], axis=0) / total_teach
    loss = gap - lse_teach + 2.0 * lse_stud - jnp.sum(every[:, 6:7], axis=0)
    loss = jnp.broadcast_to(loss, loss_ref.shape)
    for bit in range(bits):
        loss = jnp.where(((me >> bit) & 1) == 1, swapped(loss, blk << bit), loss)
    loss_ref[...] = loss
    own = tables[0][...]
    scale_teach = -loss_scale * jnp.exp(own[0:1] - lse_teach)
    scale_stud = 2.0 * loss_scale * jnp.exp(own[4:5] - lse_stud)
    line = lax.broadcasted_iota(jnp.int32, (lanes, rows), 0)
    factors[...] = jnp.where(line == 0, scale_teach, scale_stud).T

    def one(part, carry):
        at = pl.ds(pl.multiple_of(part * chunk, chunk), chunk)
        hit = lax.broadcasted_iota(jnp.int32, (chunk, teach_ref.shape[1]), 1) == column_ref[at, :]
        both = teach_ref[at, :] * factors[at, 0:1] + stud_ref[at, :] * factors[at, 1:2]
        upstream[at, :] = jnp.where(hit, both - loss_scale, both).astype(jnp.bfloat16)
        return carry

    lax.fori_loop(0, rows // chunk, one, 0)

    def two(index, carry):
        at = pl.ds(pl.multiple_of(index * step, step), step)
        product = lax.dot_general(
            upstream[...], head[at, :], (((1,), (1,)), ((), ())), preferred_element_type=jnp.float32
        )
        for piece, out in enumerate(outs):
            out[:, at] = product[piece * blk : (piece + 1) * blk]
        return carry

    lax.fori_loop(0, head.shape[0] // step, two, 0)


def gradient(place, tables, scaled_teach, scaled_stud, column, head, bits, chunk):
    rows, vocab_dev = scaled_teach.shape
    count, width = 1 << bits, head.shape[0]
    step = 512 if width % 512 == 0 else width
    return pl.pallas_call(
        functools.partial(gradient_kernel, bits, step, chunk),
        in_specs=[in_smem] + [in_vmem] * (count + 4),
        out_specs=[in_vmem] * (count + 1),
        out_shape=[jax.ShapeDtypeStruct((8, rows), jnp.float32)]
        + [jax.ShapeDtypeStruct((rows // count, width), jnp.float32)] * count,
        scratch_shapes=[
            pltpu.VMEM((count, 8, rows), jnp.float32),
            pltpu.VMEM((rows, vocab_dev), jnp.bfloat16),
            pltpu.VMEM((rows, lanes), jnp.float32),
        ],
        compiler_params=pltpu.CompilerParams(vmem_limit_bytes=vmem_bytes),
        cost_estimate=head_cost(rows, head),
    )(place, *tables, scaled_teach, scaled_stud, column, head)


def tie(block, *others):
    return lax.optimization_barrier((block, *others))[0]


def make_body(vocab_size):
    bits = vocab_size.bit_length() - 1
    assert vocab_size == 1 << bits

    def swap(block, bit):
        return lax.ppermute(block, "vocab", [(at, at ^ (1 << bit)) for at in range(vocab_size)])

    def lowest(mask):
        return (mask & -mask).bit_length() - 1

    def spread(own, mixed):
        blocks = {0: own}
        masks = range(1, vocab_size)
        if not mixed:
            own_hops = [swap(own, bit) for bit in range(bits - 1)]
            blocks.update({1 << bit: block for bit, block in enumerate(own_hops)})
            masks = [mask for mask in masks if mask not in blocks]
        else:
            masks = sorted(masks, key=lambda mask: mask & 3 == 3 and mask > 3)
        for mask in masks:
            bit = 1 if mixed and mask & 3 == 3 and mask > 3 else lowest(mask)
            block = blocks[mask ^ (1 << bit)]
            if not mixed and mask ^ (1 << bit) == 1 << (bits - 1):
                block = tie(block, *own_hops)
            blocks[mask] = swap(block, bit)
        return [blocks[mask] for mask in range(vocab_size)]

    def reduce_blocks(parts, gates={}):
        terms, line = list(parts), []
        for mask in range(vocab_size - 1, 0, -1):
            bit = lowest(mask)
            block = terms[mask].astype(wire)
            if mask in gates:
                block = tie(block, gates[mask])
            elif bit == 0 and len(line) > 1:
                block = tie(block, line[-2])
            block = swap(block, bit)
            if bit == 0:
                line.append(block)
            terms[mask ^ (1 << bit)] = terms[mask ^ (1 << bit)] + block.astype(jnp.float32)
        return terms[0]

    def body(teacher_rows, owner, counts, proj_weight, student_hidden, head_weight, targets):
        teach_rows = teacher_rows.shape[0]
        slab_rows = targets.shape[0]
        vocab_dev = head_weight.shape[1]
        blk = slab_rows // vocab_size
        chunk = min(slab_rows, 32)
        me = lax.axis_index("vocab")
        core = lax.axis_index("seq")
        place = jnp.stack([me, core]).astype(jnp.int32)

        def in_order(vec):
            grid = vec.reshape((2,) * bits + (blk,))
            for bit in range(bits):
                grid = jnp.where((me >> bit) & 1 == 1, jnp.flip(grid, bits - 1 - bit), grid)
            return grid.reshape(slab_rows)

        def turned(block):
            return jnp.where(core == 1, jnp.roll(block, block.shape[1] // 2, axis=1), block)

        def as_pieces(blocks):
            return blocks if blk % 16 == 0 else [jnp.concatenate(blocks, axis=0)]

        heads = (head_weight, lax.ppermute(head_weight, "seq", [(0, 1), (1, 0)]))

        spot = lax.iota(jnp.int32, slab_rows)
        row_id = ((spot // blk) ^ me) * blk + spot % blk
        alive = lax.iota(jnp.int32, teach_rows) < counts[0]
        member = (owner[None, :] == row_id[:, None]) & alive[None, :]
        parts = project(member.astype(jnp.bfloat16), teacher_rows, proj_weight, vocab_size, 512 if student_hidden.shape[1] % 512 == 0 else student_hidden.shape[1])
        hidden = spread(turned(student_hidden), True)
        gates = dict(zip(range(vocab_size - 1, 0, -2), (hidden[1], hidden[2], hidden[vocab_size // 2])))
        projected_own = tie(reduce_blocks(parts, gates), *hidden[:-1])
        projected = spread(turned(projected_own.astype(jnp.bfloat16)), False)

        column = (in_order(targets) - me * vocab_dev)[:, None]
        logit_stud, scaled_stud, stats_stud, head = student_logits(as_pieces(hidden), heads, column, 256, chunk)
        scaled_teach, stats = teacher_logits(as_pieces(projected), head, logit_stud, stats_stud, 512, chunk)
        tables = [stats]
        for mask in range(1, vocab_size):
            far, near = mask & ~3, mask & 3
            source, hop = (tables[far], near) if near else (stats, far)
            tables.append(lax.ppermute(source, "vocab", [(at, at ^ hop) for at in range(vocab_size)]))
        loss, *terms = gradient(place, tables, scaled_teach, scaled_stud, column, head, bits, chunk)
        return (loss[0], turned(reduce_blocks(terms).astype(jnp.bfloat16)))

    return body


def solution(mesh):
    return jax.shard_map(
        make_body(mesh.shape["vocab"]),
        mesh=mesh,
        in_specs=(
            P(("groups", "seq"), "vocab"),
            P(("groups", "seq")),
            P(("groups", "seq")),
            P("vocab", None),
            P(("groups", "seq", "vocab"), None),
            P("seq", "vocab"),
            P(("groups", "seq")),
        ),
        out_specs=(P(("groups", "seq")), P(("groups", "seq", "vocab"), None)),
        check_vma=False,
    )
```

```python
import functools

import jax
import jax.numpy as jnp
from jax import lax
from jax.experimental import pallas as pl
from jax.experimental.pallas import tpu as pltpu
from jax.sharding import PartitionSpec as P

loss_scale = 64.0
wire = jnp.float16
lanes = 128
vmem_bytes = 12 * 1024 * 1024
project_bytes = 47 * 1024 * 1024

in_vmem = pl.BlockSpec(memory_space=pltpu.VMEM)
in_smem = pl.BlockSpec(memory_space=pltpu.SMEM)
in_place = pl.BlockSpec(memory_space=pl.ANY)


def cuts(total, step):
    return [(start, min(step, total - start)) for start in range(0, total, step)]


def project_kernel(count, step, member_ref, teacher_ref, weight_ref, *rest):
    outs, (teacher, weight, aligned, sems) = rest[:count], rest[count:]
    blk = outs[0].shape[0]
    parts = cuts(weight.shape[1], step)
    first = pltpu.make_async_copy(teacher_ref, teacher, sems.at[len(parts)])
    first.start()
    for index, (start, size) in enumerate(parts):
        at = pl.ds(start, size)
        pltpu.make_async_copy(weight_ref.at[:, at], weight.at[:, at], sems.at[index]).start()
    member = member_ref[...]
    sizes = jnp.sum(member.astype(jnp.float32), axis=1, keepdims=True)
    first.wait()
    summed = jnp.dot(member, teacher[...], preferred_element_type=jnp.float32)
    aligned[...] = (summed / sizes).astype(jnp.bfloat16)

    def one(index, carry):
        at = pl.ds(pl.multiple_of(index * step, step), step)
        pltpu.make_async_copy(weight_ref.at[:, at], weight.at[:, at], sems.at[index]).wait()
        product = jnp.dot(aligned[...], weight[:, at], preferred_element_type=jnp.float32)
        for piece, out in enumerate(outs):
            out[:, at] = product[piece * blk : (piece + 1) * blk]
        return carry

    lax.fori_loop(0, len(parts), one, 0)


def project(member, teacher_rows, proj_weight, count, step):
    slab_rows, (depth, width) = member.shape[0], proj_weight.shape
    blk = slab_rows // count
    return pl.pallas_call(
        functools.partial(project_kernel, count, step),
        in_specs=[in_vmem, in_place, in_place],
        out_specs=[in_vmem] * count,
        out_shape=[jax.ShapeDtypeStruct((blk, width), jnp.float32)] * count,
        scratch_shapes=[
            pltpu.VMEM(teacher_rows.shape, jnp.bfloat16),
            pltpu.VMEM(proj_weight.shape, jnp.bfloat16),
            pltpu.VMEM((slab_rows, depth), jnp.bfloat16),
            pltpu.SemaphoreType.DMA((len(cuts(width, step)) + 1,)),
        ],
        compiler_params=pltpu.CompilerParams(vmem_limit_bytes=project_bytes),
        cost_estimate=pl.CostEstimate(
            flops=2 * slab_rows * depth * (width + teacher_rows.shape[0]),
            bytes_accessed=2 * depth * (width + teacher_rows.shape[0]) + 4 * slab_rows * width,
            transcendentals=0,
        ),
    )(member, teacher_rows, proj_weight)


def multiply(read_rows, heads, logit_ref, highest, step):
    depth, total = heads[0].shape
    highest[...] = jnp.full(highest.shape, -jnp.inf, jnp.float32)

    def one(start, size):
        at = pl.ds(start, size)
        part = jnp.dot(read_rows(0, depth), heads[0][:, at], preferred_element_type=jnp.float32)
        part += jnp.dot(read_rows(depth, 2 * depth), heads[1][:, at], preferred_element_type=jnp.float32)
        logit_ref[:, at] = part
        top = part[:, :lanes]
        for lane in range(lanes, size, lanes):
            top = jnp.maximum(top, part[:, lane : lane + lanes])
        highest[...] = jnp.maximum(highest[...], top)

    def body(index, carry):
        one(pl.multiple_of(index * step, step), step)
        return carry

    full = total // step
    lax.fori_loop(0, full, body, 0)
    if total % step:
        one(full * step, total % step)


def as_columns(first, second, third):
    lane = lax.broadcasted_iota(jnp.int32, (first.shape[0], lanes), 1)
    return jnp.where(lane == 0, first, jnp.where(lane == 1, second, jnp.where(lane == 2, third, 0.0)))


def student_kernel(count, step, chunk, *refs):
    pieces, heads = refs[:count], refs[count : count + 2]
    column_ref, logit_ref, scaled_ref, stats_ref = refs[count + 2 : count + 6]
    held, highest, table, sems = refs[count + 6 :]
    blk = pieces[0].shape[0]
    copies = []
    for i, piece in enumerate(pieces):
        copies.append(pltpu.make_async_copy(piece, held.at[pl.ds(i * blk, blk)], sems.at[i]))
        copies[-1].start()
    for copy in copies:
        copy.wait()
    multiply(lambda start, end: held[:, start:end], heads, logit_ref, highest, step)

    def one(part, carry):
        rows = pl.ds(pl.multiple_of(part * chunk, chunk), chunk)
        logit = logit_ref[rows, :]
        top = jnp.max(highest[rows, :], axis=1, keepdims=True)
        scaled = jnp.exp(logit - top)
        hit = lax.broadcasted_iota(jnp.int32, logit.shape, 1) == column_ref[rows, :]
        picked = jnp.sum(jnp.where(hit, logit, 0.0), axis=1, keepdims=True)
        scaled_ref[rows, :] = scaled
        table[rows, :] = as_columns(top, jnp.sum(scaled, axis=1, keepdims=True), picked)
        return carry

    lax.fori_loop(0, logit_ref.shape[0] // chunk, one, 0)
    stats_ref[...] = table[...].T[0:8]


def teacher_kernel(count, step, chunk, *refs):
    pieces, heads = refs[:count], refs[count : count + 2]
    stud_logit_ref, stud_ref, scaled_ref, stats_ref, highest, table = refs[count + 2 :]

    def read_rows(start, end):
        return jnp.concatenate([ref[:, start:end] for ref in pieces], axis=0)

    multiply(read_rows, heads, scaled_ref, highest, step)

    def one(part, carry):
        rows = pl.ds(pl.multiple_of(part * chunk, chunk), chunk)
        logit = scaled_ref[rows, :]
        top = jnp.max(highest[rows, :], axis=1, keepdims=True)
        scaled = jnp.exp(logit - top)
        gap = jnp.sum(scaled * (logit - stud_logit_ref[rows, :]), axis=1, keepdims=True)
        scaled_ref[rows, :] = scaled
        table[rows, :] = as_columns(top, jnp.sum(scaled, axis=1, keepdims=True), gap)
        return carry

    lax.fori_loop(0, scaled_ref.shape[0] // chunk, one, 0)
    teach = table[...].T[0:8]
    row = lax.broadcasted_iota(jnp.int32, teach.shape, 0)
    stats_ref[...] = jnp.where(row < 4, teach, pltpu.roll(stud_ref[...], 4, 0))


def head_cost(rows, heads):
    depth, vocab_dev = 2 * heads[0].shape[0], heads[0].shape[1]
    return pl.CostEstimate(
        flops=2 * rows * depth * vocab_dev,
        bytes_accessed=2 * depth * vocab_dev + 12 * rows * vocab_dev,
        transcendentals=rows * vocab_dev,
    )


def student_logits(pieces, heads, column, step, chunk):
    rows, (depth, vocab_dev) = column.shape[0], heads[0].shape
    wide = (rows, vocab_dev)
    return pl.pallas_call(
        functools.partial(student_kernel, len(pieces), step, chunk),
        in_specs=[in_place] * len(pieces) + [in_vmem] * 3,
        out_specs=[in_vmem] * 3,
        out_shape=[
            jax.ShapeDtypeStruct(wide, jnp.float32),
            jax.ShapeDtypeStruct(wide, jnp.float32),
            jax.ShapeDtypeStruct((8, rows), jnp.float32),
        ],
        scratch_shapes=[
            pltpu.VMEM((rows, 2 * depth), jnp.bfloat16),
            pltpu.VMEM((rows, lanes), jnp.float32),
            pltpu.VMEM((rows, lanes), jnp.float32),
            pltpu.SemaphoreType.DMA((len(pieces),)),
        ],
        compiler_params=pltpu.CompilerParams(vmem_limit_bytes=vmem_bytes),
        cost_estimate=head_cost(rows, heads),
    )(*pieces, *heads, column)


def teacher_logits(pieces, heads, logit_stud, stats_stud, step, chunk):
    wide = logit_stud.shape
    return pl.pallas_call(
        functools.partial(teacher_kernel, len(pieces), step, chunk),
        in_specs=[in_vmem] * (len(pieces) + 4),
        out_specs=[in_vmem] * 2,
        out_shape=[
            jax.ShapeDtypeStruct(wide, jnp.float32),
            jax.ShapeDtypeStruct((8, wide[0]), jnp.float32),
        ],
        scratch_shapes=[pltpu.VMEM((wide[0], lanes), jnp.float32)] * 2,
        compiler_params=pltpu.CompilerParams(vmem_limit_bytes=vmem_bytes),
        cost_estimate=head_cost(wide[0], heads),
    )(*pieces, *heads, logit_stud, stats_stud)


def swapped(values, distance):
    total = values.shape[1]
    lane = lax.broadcasted_iota(jnp.int32, values.shape, 1)
    return jnp.where(
        (lane & distance) != 0, pltpu.roll(values, distance, 1), pltpu.roll(values, total - distance, 1)
    )


def gradient_kernel(bits, step, chunk, place_ref, *refs):
    count = 1 << bits
    tables, refs = refs[:count], refs[count:]
    teach_ref, stud_ref, column_ref, *heads, loss_ref = refs[:6]
    outs = refs[6 : count + 6]
    entries, upstream, factors = refs[count + 6 :]
    rows = upstream.shape[0]
    blk = rows // count
    me = place_ref[0]
    for mask in range(count):
        values = tables[mask][...]
        for bit in range(bits):
            if mask >> bit & 1:
                values = swapped(values, blk << bit)
        entries[me ^ mask] = values
    every = entries[...]
    top_teach = jnp.max(every[:, 0:1], axis=0)
    top_stud = jnp.max(every[:, 4:5], axis=0)
    weight = jnp.exp(every[:, 0:1] - top_teach)
    total_teach = jnp.sum(weight * every[:, 1:2], axis=0)
    total_stud = jnp.sum(jnp.exp(every[:, 4:5] - top_stud) * every[:, 5:6], axis=0)
    lse_teach = top_teach + jnp.log(total_teach)
    lse_stud = top_stud + jnp.log(total_stud)
    gap = jnp.sum(weight * every[:, 2:3], axis=0) / total_teach
    loss = gap - lse_teach + 2.0 * lse_stud - jnp.sum(every[:, 6:7], axis=0)
    loss = jnp.broadcast_to(loss, loss_ref.shape)
    for bit in range(bits):
        loss = jnp.where(((me >> bit) & 1) == 1, swapped(loss, blk << bit), loss)
    loss_ref[...] = loss
    own = tables[0][...]
    scale_teach = -loss_scale * jnp.exp(own[0:1] - lse_teach)
    scale_stud = 2.0 * loss_scale * jnp.exp(own[4:5] - lse_stud)
    line = lax.broadcasted_iota(jnp.int32, (lanes, rows), 0)
    factors[...] = jnp.where(line == 0, scale_teach, scale_stud).T

    def one(part, carry):
        at = pl.ds(pl.multiple_of(part * chunk, chunk), chunk)
        hit = lax.broadcasted_iota(jnp.int32, (chunk, teach_ref.shape[1]), 1) == column_ref[at, :]
        both = teach_ref[at, :] * factors[at, 0:1] + stud_ref[at, :] * factors[at, 1:2]
        upstream[at, :] = jnp.where(hit, both - loss_scale, both).astype(jnp.bfloat16)
        return carry

    lax.fori_loop(0, rows // chunk, one, 0)

    depth = heads[0].shape[0]
    for half, head in enumerate(heads):

        def two(start, size, half=half, head=head):
            product = lax.dot_general(
                upstream[...],
                head[pl.ds(start, size), :],
                (((1,), (1,)), ((), ())),
                preferred_element_type=jnp.float32,
            )
            at = pl.ds(pl.multiple_of(half * depth + start, lanes), size)
            for piece, out in enumerate(outs):
                out[:, at] = product[piece * blk : (piece + 1) * blk]

        def body(index, carry, two=two):
            two(pl.multiple_of(index * step, step), step)
            return carry

        lax.fori_loop(0, depth // step, body, 0)
        if depth % step:
            two(depth - depth % step, depth % step)


def gradient(place, tables, scaled_teach, scaled_stud, column, heads, bits, chunk):
    rows, vocab_dev = scaled_teach.shape
    count, width = 1 << bits, 2 * heads[0].shape[0]
    step = 512 if width % 256 == 0 else width // 2
    return pl.pallas_call(
        functools.partial(gradient_kernel, bits, step, chunk),
        in_specs=[in_smem] + [in_vmem] * (count + 5),
        out_specs=[in_vmem] * (count + 1),
        out_shape=[jax.ShapeDtypeStruct((8, rows), jnp.float32)]
        + [jax.ShapeDtypeStruct((rows // count, width), jnp.float32)] * count,
        scratch_shapes=[
            pltpu.VMEM((count, 8, rows), jnp.float32),
            pltpu.VMEM((rows, vocab_dev), jnp.bfloat16),
            pltpu.VMEM((rows, lanes), jnp.float32),
        ],
        compiler_params=pltpu.CompilerParams(vmem_limit_bytes=vmem_bytes),
        cost_estimate=head_cost(rows, heads),
    )(place, *tables, scaled_teach, scaled_stud, column, *heads)


def tie(block, *others):
    return lax.optimization_barrier((block, *others))[0]


def make_body(vocab_size):
    bits = vocab_size.bit_length() - 1
    assert vocab_size == 1 << bits

    def swap(block, bit):
        return lax.ppermute(block, "vocab", [(at, at ^ (1 << bit)) for at in range(vocab_size)])

    def lowest(mask):
        return (mask & -mask).bit_length() - 1

    def spread(own, mixed, *between):
        blocks = {0: own}
        masks = range(1, vocab_size)
        if not mixed:
            own_hops = [swap(own, bit) for bit in range(bits - 1)]
            blocks.update({1 << bit: block for bit, block in enumerate(own_hops)})
            masks = [mask for mask in masks if mask not in blocks]
        else:
            masks = sorted(masks, key=lambda mask: mask & 3 == 3 and mask > 3)
        for mask in masks:
            bit = 1 if mixed and mask & 3 == 3 and mask > 3 else lowest(mask)
            block = blocks[mask ^ (1 << bit)]
            if not mixed and mask ^ (1 << bit) == 1 << (bits - 1):
                block = tie(block, *own_hops, *between)
            blocks[mask] = swap(block, bit)
        return [blocks[mask] for mask in range(vocab_size)]

    def reduce_blocks(parts, gates={}):
        terms, line = list(parts), []
        for mask in range(vocab_size - 1, 0, -1):
            bit = lowest(mask)
            block = terms[mask].astype(wire)
            if mask in gates:
                block = tie(block, gates[mask])
            elif bit == 0 and len(line) > 1:
                block = tie(block, line[-2])
            block = swap(block, bit)
            if bit == 0:
                line.append(block)
            terms[mask ^ (1 << bit)] = terms[mask ^ (1 << bit)] + block.astype(jnp.float32)
        return terms[0]

    def body(teacher_rows, owner, counts, proj_weight, student_hidden, head_weight, targets):
        teach_rows = teacher_rows.shape[0]
        slab_rows = targets.shape[0]
        vocab_dev = head_weight.shape[1]
        blk = slab_rows // vocab_size
        chunk = min(slab_rows, 32)
        me = lax.axis_index("vocab")
        core = lax.axis_index("seq")
        place = jnp.stack([me, core]).astype(jnp.int32)

        def in_order(vec):
            grid = vec.reshape((2,) * bits + (blk,))
            for bit in range(bits):
                grid = jnp.where((me >> bit) & 1 == 1, jnp.flip(grid, bits - 1 - bit), grid)
            return grid.reshape(slab_rows)

        def turned(block):
            return jnp.where(core == 1, jnp.roll(block, block.shape[1] // 2, axis=1), block)

        def as_pieces(blocks):
            return blocks if blk % 16 == 0 else [jnp.concatenate(blocks, axis=0)]

        heads = (head_weight, lax.ppermute(head_weight, "seq", [(0, 1), (1, 0)]))

        spot = lax.iota(jnp.int32, slab_rows)
        row_id = ((spot // blk) ^ me) * blk + spot % blk
        alive = lax.iota(jnp.int32, teach_rows) < counts[0]
        member = (owner[None, :] == row_id[:, None]) & alive[None, :]
        parts = project(member.astype(jnp.bfloat16), teacher_rows, proj_weight, vocab_size, 512 if student_hidden.shape[1] % 512 == 0 else student_hidden.shape[1])
        hidden = spread(tie(turned(student_hidden), parts[-1]), True)
        projected_own = tie(reduce_blocks(parts, {3: hidden[1]}), *hidden[:-1])
        column = (in_order(targets) - me * vocab_dev)[:, None]
        logit_stud, scaled_stud, stats_stud = student_logits(as_pieces(hidden), heads, column, 512, chunk)
        projected = spread(turned(projected_own.astype(jnp.bfloat16)), False, stats_stud)
        scaled_teach, stats = teacher_logits(
            as_pieces(projected), heads, logit_stud, stats_stud, 512, chunk
        )
        tables = [stats]
        for mask in range(1, vocab_size):
            far, near = mask & ~3, mask & 3
            source, hop = (tables[far], near) if near else (stats, far)
            tables.append(lax.ppermute(source, "vocab", [(at, at ^ hop) for at in range(vocab_size)]))
        loss, *terms = gradient(place, tables, scaled_teach, scaled_stud, column, heads, bits, chunk)
        return (loss[0], turned(reduce_blocks(terms).astype(jnp.bfloat16)))

    return body


def solution(mesh):
    return jax.shard_map(
        make_body(mesh.shape["vocab"]),
        mesh=mesh,
        in_specs=(
            P(("groups", "seq"), "vocab"),
            P(("groups", "seq")),
            P(("groups", "seq")),
            P("vocab", None),
            P(("groups", "seq", "vocab"), None),
            P("seq", "vocab"),
            P(("groups", "seq")),
        ),
        out_specs=(P(("groups", "seq")), P(("groups", "seq", "vocab"), None)),
        check_vma=False,
    )
```

```python
import functools

import jax
import jax.numpy as jnp
from jax import lax
from jax.experimental import pallas as pl
from jax.experimental.pallas import tpu as pltpu
from jax.sharding import PartitionSpec as P

loss_scale = 64.0
wire = jnp.float16
lanes = 128
vmem_bytes = 12 * 1024 * 1024
logits_bytes = 34 * 1024 * 1024
project_bytes = 50 * 1024 * 1024

in_vmem = pl.BlockSpec(memory_space=pltpu.VMEM)
in_smem = pl.BlockSpec(memory_space=pltpu.SMEM)
in_place = pl.BlockSpec(memory_space=pl.ANY)


def cuts(total, step):
    return [(start, min(step, total - start)) for start in range(0, total, step)]


def project_kernel(count, step, member_ref, teacher_ref, weight_ref, *rest):
    outs, (teacher, weight, aligned, sems) = rest[:count], rest[count:]
    blk = outs[0].shape[0]
    parts = cuts(weight.shape[1], step)
    first = pltpu.make_async_copy(teacher_ref, teacher, sems.at[len(parts)])
    first.start()
    for index, (start, size) in enumerate(parts):
        at = pl.ds(start, size)
        pltpu.make_async_copy(weight_ref.at[:, at], weight.at[:, at], sems.at[index]).start()
    member = member_ref[...]
    sizes = jnp.sum(member.astype(jnp.float32), axis=1, keepdims=True)
    first.wait()
    summed = jnp.dot(member, teacher[...], preferred_element_type=jnp.float32)
    aligned[...] = (summed / sizes).astype(jnp.bfloat16)

    def one(index, carry):
        at = pl.ds(pl.multiple_of(index * step, step), step)
        pltpu.make_async_copy(weight_ref.at[:, at], weight.at[:, at], sems.at[index]).wait()
        product = jnp.dot(aligned[...], weight[:, at], preferred_element_type=jnp.float32)
        for piece, out in enumerate(outs):
            out[:, at] = product[piece * blk : (piece + 1) * blk]
        return carry

    lax.fori_loop(0, len(parts), one, 0)


def project(member, teacher_rows, proj_weight, count, step):
    slab_rows, (depth, width) = member.shape[0], proj_weight.shape
    blk = slab_rows // count
    return pl.pallas_call(
        functools.partial(project_kernel, count, step),
        in_specs=[in_vmem, in_place, in_place],
        out_specs=[in_vmem] * count,
        out_shape=[jax.ShapeDtypeStruct((blk, width), jnp.float32)] * count,
        scratch_shapes=[
            pltpu.VMEM(teacher_rows.shape, jnp.bfloat16),
            pltpu.VMEM(proj_weight.shape, jnp.bfloat16),
            pltpu.VMEM((slab_rows, depth), jnp.bfloat16),
            pltpu.SemaphoreType.DMA((len(cuts(width, step)) + 1,)),
        ],
        compiler_params=pltpu.CompilerParams(vmem_limit_bytes=project_bytes),
        cost_estimate=pl.CostEstimate(
            flops=2 * slab_rows * depth * (width + teacher_rows.shape[0]),
            bytes_accessed=2 * depth * (width + teacher_rows.shape[0]) + 4 * slab_rows * width,
            transcendentals=0,
        ),
    )(member, teacher_rows, proj_weight)


def as_columns(values):
    lane = lax.broadcasted_iota(jnp.int32, (values[0].shape[0], lanes), 1)
    table = jnp.zeros(lane.shape, jnp.float32)
    for at, value in enumerate(values):
        if value is not None:
            table = jnp.where(lane == at, value, table)
    return table


def logits_kernel(count, step, chunk, *refs):
    pieces, heads = refs[:count], refs[count : count + 2]
    column_ref, scaled_ref, stats_ref, head = refs[count + 2 : count + 6]
    held, highest, table, sems = refs[count + 6 :]
    depth, total = heads[0].shape
    blk, slab = pieces[0].shape[0], held.shape[0] // 2
    copies = []
    for i, piece in enumerate(pieces):
        copies.append(pltpu.make_async_copy(piece, held.at[pl.ds(i * blk, blk)], sems.at[i]))
        copies[-1].start()

    def columns(index, half, at):
        source, target = heads[half].at[:, at], head.at[pl.ds(half * depth, depth), at]
        return pltpu.make_async_copy(source, target, sems.at[count + 2 * index + half])

    for index, (start, size) in enumerate(cuts(total, step)):
        for half in range(2):
            columns(index, half, pl.ds(start, size)).start()
    highest[...] = jnp.full(highest.shape, -jnp.inf, jnp.float32)
    for copy in copies:
        copy.wait()

    def one(index, start, size):
        at = pl.ds(start, size)
        for half in range(2):
            columns(index, half, at).wait()
        part = jnp.dot(held[...], head[:, at], preferred_element_type=jnp.float32)
        scaled_ref[:, at] = part
        top = part[:, :lanes]
        for lane in range(lanes, size, lanes):
            top = jnp.maximum(top, part[:, lane : lane + lanes])
        highest[...] = jnp.maximum(highest[...], top)

    def body(index, carry):
        one(index, pl.multiple_of(index * step, step), step)
        return carry

    full = total // step
    lax.fori_loop(0, full, body, 0)
    if total % step:
        one(full, full * step, total % step)

    def two(part, carry):
        start = pl.multiple_of(part * chunk, chunk)
        own, other = pl.ds(start, chunk), pl.ds(slab + start, chunk)
        stud, teach = scaled_ref[own, :], scaled_ref[other, :]
        top_stud = jnp.max(highest[own, :], axis=1, keepdims=True)
        top_teach = jnp.max(highest[other, :], axis=1, keepdims=True)
        hit = lax.broadcasted_iota(jnp.int32, stud.shape, 1) == column_ref[own, :]
        picked = jnp.sum(jnp.where(hit, stud, 0.0), axis=1, keepdims=True)
        scaled_teach = jnp.exp(teach - top_teach)
        gap = jnp.sum(scaled_teach * (teach - stud), axis=1, keepdims=True)
        scaled_stud = jnp.exp(stud - top_stud)
        scaled_ref[own, :] = scaled_stud
        scaled_ref[other, :] = scaled_teach
        sum_teach = jnp.sum(scaled_teach, axis=1, keepdims=True)
        sum_stud = jnp.sum(scaled_stud, axis=1, keepdims=True)
        table[own, :] = as_columns([top_teach, sum_teach, gap, None, top_stud, sum_stud, picked])
        return carry

    lax.fori_loop(0, slab // chunk, two, 0)
    stats_ref[...] = table[...].T[0:8]


def head_cost(rows, head):
    depth, vocab_dev = head.shape
    return pl.CostEstimate(
        flops=2 * rows * depth * vocab_dev,
        bytes_accessed=2 * depth * vocab_dev + 12 * rows * vocab_dev,
        transcendentals=rows * vocab_dev,
    )


def logits(pieces, heads, column, step, chunk):
    slab, (depth, vocab_dev) = column.shape[0], heads[0].shape
    return pl.pallas_call(
        functools.partial(logits_kernel, len(pieces), step, chunk),
        in_specs=[in_place] * (len(pieces) + 2) + [in_vmem],
        out_specs=[in_vmem] * 3,
        out_shape=[
            jax.ShapeDtypeStruct((2 * slab, vocab_dev), jnp.float32),
            jax.ShapeDtypeStruct((8, slab), jnp.float32),
            jax.ShapeDtypeStruct((2 * depth, vocab_dev), jnp.bfloat16),
        ],
        scratch_shapes=[
            pltpu.VMEM((2 * slab, 2 * depth), jnp.bfloat16),
            pltpu.VMEM((2 * slab, lanes), jnp.float32),
            pltpu.VMEM((slab, lanes), jnp.float32),
            pltpu.SemaphoreType.DMA((len(pieces) + 2 * len(cuts(vocab_dev, step)),)),
        ],
        compiler_params=pltpu.CompilerParams(vmem_limit_bytes=logits_bytes),
        cost_estimate=head_cost(4 * slab, heads[0]),
    )(*pieces, *heads, column)


def swapped(values, distance):
    total = values.shape[1]
    lane = lax.broadcasted_iota(jnp.int32, values.shape, 1)
    return jnp.where(
        (lane & distance) != 0, pltpu.roll(values, distance, 1), pltpu.roll(values, total - distance, 1)
    )


def gradient_kernel(bits, step, chunk, place_ref, *refs):
    count = 1 << bits
    tables, refs = refs[:count], refs[count:]
    scaled_ref, column_ref, head, loss_ref = refs[:4]
    outs = refs[4 : count + 4]
    entries, upstream, factors = refs[count + 4 :]
    rows = upstream.shape[0]
    blk = rows // count
    me = place_ref[0]
    for mask in range(count):
        values = tables[mask][...]
        for bit in range(bits):
            if mask >> bit & 1:
                values = swapped(values, blk << bit)
        entries[me ^ mask] = values
    every = entries[...]
    top_teach = jnp.max(every[:, 0:1], axis=0)
    top_stud = jnp.max(every[:, 4:5], axis=0)
    weight = jnp.exp(every[:, 0:1] - top_teach)
    total_teach = jnp.sum(weight * every[:, 1:2], axis=0)
    total_stud = jnp.sum(jnp.exp(every[:, 4:5] - top_stud) * every[:, 5:6], axis=0)
    lse_teach = top_teach + jnp.log(total_teach)
    lse_stud = top_stud + jnp.log(total_stud)
    gap = jnp.sum(weight * every[:, 2:3], axis=0) / total_teach
    loss = gap - lse_teach + 2.0 * lse_stud - jnp.sum(every[:, 6:7], axis=0)
    loss = jnp.broadcast_to(loss, loss_ref.shape)
    for bit in range(bits):
        loss = jnp.where(((me >> bit) & 1) == 1, swapped(loss, blk << bit), loss)
    loss_ref[...] = loss
    own = tables[0][...]
    scale_teach = -loss_scale * jnp.exp(own[0:1] - lse_teach)
    scale_stud = 2.0 * loss_scale * jnp.exp(own[4:5] - lse_stud)
    line = lax.broadcasted_iota(jnp.int32, (lanes, rows), 0)
    factors[...] = jnp.where(line == 0, scale_teach, scale_stud).T

    def one(part, carry):
        start = pl.multiple_of(part * chunk, chunk)
        at, other = pl.ds(start, chunk), pl.ds(rows + start, chunk)
        hit = lax.broadcasted_iota(jnp.int32, (chunk, scaled_ref.shape[1]), 1) == column_ref[at, :]
        both = scaled_ref[other, :] * factors[at, 0:1] + scaled_ref[at, :] * factors[at, 1:2]
        upstream[at, :] = jnp.where(hit, both - loss_scale, both).astype(jnp.bfloat16)
        return carry

    lax.fori_loop(0, rows // chunk, one, 0)

    def two(index, carry):
        at = pl.ds(pl.multiple_of(index * step, step), step)
        product = lax.dot_general(
            upstream[...], head[at, :], (((1,), (1,)), ((), ())), preferred_element_type=jnp.float32
        )
        for piece, out in enumerate(outs):
            out[:, at] = product[piece * blk : (piece + 1) * blk]
        return carry

    lax.fori_loop(0, head.shape[0] // step, two, 0)


def gradient(place, tables, scaled, column, head, bits, chunk):
    rows, vocab_dev = column.shape[0], scaled.shape[1]
    count, width = 1 << bits, head.shape[0]
    step = 512 if width % 512 == 0 else width
    return pl.pallas_call(
        functools.partial(gradient_kernel, bits, step, chunk),
        in_specs=[in_smem] + [in_vmem] * (count + 3),
        out_specs=[in_vmem] * (count + 1),
        out_shape=[jax.ShapeDtypeStruct((8, rows), jnp.float32)]
        + [jax.ShapeDtypeStruct((rows // count, width), jnp.float32)] * count,
        scratch_shapes=[
            pltpu.VMEM((count, 8, rows), jnp.float32),
            pltpu.VMEM((rows, vocab_dev), jnp.bfloat16),
            pltpu.VMEM((rows, lanes), jnp.float32),
        ],
        compiler_params=pltpu.CompilerParams(vmem_limit_bytes=vmem_bytes),
        cost_estimate=head_cost(rows, head),
    )(place, *tables, scaled, column, head)


def tie(block, *others):
    return lax.optimization_barrier((block, *others))[0]


def make_body(vocab_size):
    bits = vocab_size.bit_length() - 1
    assert vocab_size == 1 << bits

    def swap(block, bit):
        return lax.ppermute(block, "vocab", [(at, at ^ (1 << bit)) for at in range(vocab_size)])

    def lowest(mask):
        return (mask & -mask).bit_length() - 1

    def spread(own, line):
        blocks = [own]
        for mask in range(1, vocab_size):
            bit = lowest(mask)
            block = blocks[mask ^ (1 << bit)]
            if bit == 0:
                block = tie(block, line[-3])
            blocks.append(swap(block, bit))
            if bit == 0:
                line.append(blocks[-1])
        return blocks

    def reduce_blocks(parts):
        terms, line = list(parts), []
        for mask in range(vocab_size - 1, 0, -1):
            bit = lowest(mask)
            block = terms[mask].astype(wire)
            if bit == 0 and len(line) > 1:
                block = tie(block, line[-2])
            block = swap(block, bit)
            if bit == 0:
                line.append(block)
            terms[mask ^ (1 << bit)] = terms[mask ^ (1 << bit)] + block.astype(jnp.float32)
        return terms[0], line

    def body(teacher_rows, owner, counts, proj_weight, student_hidden, head_weight, targets):
        teach_rows = teacher_rows.shape[0]
        slab_rows = targets.shape[0]
        vocab_dev = head_weight.shape[1]
        blk = slab_rows // vocab_size
        chunk = min(slab_rows, 32)
        me = lax.axis_index("vocab")
        core = lax.axis_index("seq")
        place = jnp.stack([me, core]).astype(jnp.int32)

        def in_order(vec):
            grid = vec.reshape((2,) * bits + (blk,))
            for bit in range(bits):
                grid = jnp.where((me >> bit) & 1 == 1, jnp.flip(grid, bits - 1 - bit), grid)
            return grid.reshape(slab_rows)

        def turned(block):
            return jnp.where(core == 1, jnp.roll(block, block.shape[1] // 2, axis=1), block)

        def as_pieces(blocks):
            return blocks if blk % 16 == 0 else [jnp.concatenate(blocks, axis=0)]

        heads = (head_weight, lax.ppermute(head_weight, "seq", [(0, 1), (1, 0)]))

        spot = lax.iota(jnp.int32, slab_rows)
        row_id = ((spot // blk) ^ me) * blk + spot % blk
        alive = lax.iota(jnp.int32, teach_rows) < counts[0]
        member = (owner[None, :] == row_id[:, None]) & alive[None, :]
        parts = project(member.astype(jnp.bfloat16), teacher_rows, proj_weight, vocab_size, 512 if student_hidden.shape[1] % 512 == 0 else student_hidden.shape[1])
        projected_own, line = reduce_blocks(parts)
        hidden = spread(tie(turned(student_hidden), parts[-1]), line)
        projected = spread(turned(projected_own.astype(jnp.bfloat16)), line)

        column = (in_order(targets) - me * vocab_dev)[:, None]
        scaled, stats, head = logits(as_pieces(hidden) + as_pieces(projected), heads, column, 512, chunk)
        tables = [stats]
        for mask in range(1, vocab_size):
            far, near = mask & ~3, mask & 3
            source, hop = (tables[far], near) if near else (stats, far)
            tables.append(lax.ppermute(source, "vocab", [(at, at ^ hop) for at in range(vocab_size)]))
        loss, *terms = gradient(place, tables, scaled, column, head, bits, chunk)
        return (loss[0], turned(reduce_blocks(terms)[0].astype(jnp.bfloat16)))

    return body


def solution(mesh):
    return jax.shard_map(
        make_body(mesh.shape["vocab"]),
        mesh=mesh,
        in_specs=(
            P(("groups", "seq"), "vocab"),
            P(("groups", "seq")),
            P(("groups", "seq")),
            P("vocab", None),
            P(("groups", "seq", "vocab"), None),
            P("seq", "vocab"),
            P(("groups", "seq")),
        ),
        out_specs=(P(("groups", "seq")), P(("groups", "seq", "vocab"), None)),
        check_vma=False,
    )
```

```python
import functools

import jax
import jax.numpy as jnp
from jax import lax
from jax.experimental import pallas as pl
from jax.experimental.pallas import tpu as pltpu
from jax.sharding import PartitionSpec as P

loss_scale = 64.0
wire = jnp.float16
lanes = 128
vmem_bytes = 12 * 1024 * 1024
stage_bytes = 8 * 1024 * 1024
project_bytes = 50 * 1024 * 1024

in_vmem = pl.BlockSpec(memory_space=pltpu.VMEM)
in_smem = pl.BlockSpec(memory_space=pltpu.SMEM)
in_place = pl.BlockSpec(memory_space=pl.ANY)


def cuts(total, step):
    return [(start, min(step, total - start)) for start in range(0, total, step)]


def project_kernel(count, step, member_ref, teacher_ref, weight_ref, *rest):
    outs, (teacher, weight, aligned, sems) = rest[:count], rest[count:]
    blk = outs[0].shape[0]
    parts = cuts(weight.shape[1], step)
    first = pltpu.make_async_copy(teacher_ref, teacher, sems.at[len(parts)])
    first.start()
    for index, (start, size) in enumerate(parts):
        at = pl.ds(start, size)
        pltpu.make_async_copy(weight_ref.at[:, at], weight.at[:, at], sems.at[index]).start()
    member = member_ref[...]
    sizes = jnp.sum(member.astype(jnp.float32), axis=1, keepdims=True)
    first.wait()
    summed = jnp.dot(member, teacher[...], preferred_element_type=jnp.float32)
    aligned[...] = (summed / sizes).astype(jnp.bfloat16)

    def one(index, carry):
        at = pl.ds(pl.multiple_of(index * step, step), step)
        pltpu.make_async_copy(weight_ref.at[:, at], weight.at[:, at], sems.at[index]).wait()
        product = jnp.dot(aligned[...], weight[:, at], preferred_element_type=jnp.float32)
        for piece, out in enumerate(outs):
            out[:, at] = product[piece * blk : (piece + 1) * blk]
        return carry

    lax.fori_loop(0, len(parts), one, 0)


def project(member, teacher_rows, proj_weight, count, step):
    slab_rows, (depth, width) = member.shape[0], proj_weight.shape
    blk = slab_rows // count
    return pl.pallas_call(
        functools.partial(project_kernel, count, step),
        in_specs=[in_vmem, in_place, in_place],
        out_specs=[in_vmem] * count,
        out_shape=[jax.ShapeDtypeStruct((blk, width), jnp.float32)] * count,
        scratch_shapes=[
            pltpu.VMEM(teacher_rows.shape, jnp.bfloat16),
            pltpu.VMEM(proj_weight.shape, jnp.bfloat16),
            pltpu.VMEM((slab_rows, depth), jnp.bfloat16),
            pltpu.SemaphoreType.DMA((len(cuts(width, step)) + 1,)),
        ],
        compiler_params=pltpu.CompilerParams(vmem_limit_bytes=project_bytes),
        cost_estimate=pl.CostEstimate(
            flops=2 * slab_rows * depth * (width + teacher_rows.shape[0]),
            bytes_accessed=2 * depth * (width + teacher_rows.shape[0]) + 4 * slab_rows * width,
            transcendentals=0,
        ),
    )(member, teacher_rows, proj_weight)


def multiply(read_rows, head, logit_ref, highest, step):
    total = head.shape[1]
    highest[...] = jnp.full(highest.shape, -jnp.inf, jnp.float32)

    def one(start, size):
        at = pl.ds(start, size)
        part = jnp.dot(read_rows(), head[:, at], preferred_element_type=jnp.float32)
        logit_ref[:, at] = part
        top = part[:, :lanes]
        for lane in range(lanes, size, lanes):
            top = jnp.maximum(top, part[:, lane : lane + lanes])
        highest[...] = jnp.maximum(highest[...], top)

    def body(index, carry):
        one(pl.multiple_of(index * step, step), step)
        return carry

    full = total // step
    lax.fori_loop(0, full, body, 0)
    if total % step:
        one(full * step, total % step)


def stage_kernel(first_ref, second_ref, head, sems):
    depth = first_ref.shape[0]
    copies = []
    for half, source in enumerate((first_ref, second_ref)):
        for start, size in cuts(depth, 256):
            target = head.at[pl.ds(half * depth + start, size)]
            copies.append(
                pltpu.make_async_copy(source.at[pl.ds(start, size)], target, sems.at[len(copies)])
            )
            copies[-1].start()
    for copy in copies:
        copy.wait()


def stage(heads):
    depth, vocab_dev = heads[0].shape
    return pl.pallas_call(
        stage_kernel,
        in_specs=[in_place] * 2,
        out_specs=in_vmem,
        out_shape=jax.ShapeDtypeStruct((2 * depth, vocab_dev), jnp.bfloat16),
        scratch_shapes=[pltpu.SemaphoreType.DMA((2 * len(cuts(depth, 256)),))],
        compiler_params=pltpu.CompilerParams(vmem_limit_bytes=stage_bytes),
        cost_estimate=pl.CostEstimate(flops=0, bytes_accessed=8 * depth * vocab_dev, transcendentals=0),
    )(*heads)


def as_columns(first, second, third):
    lane = lax.broadcasted_iota(jnp.int32, (first.shape[0], lanes), 1)
    return jnp.where(lane == 0, first, jnp.where(lane == 1, second, jnp.where(lane == 2, third, 0.0)))


def student_kernel(count, step, chunk, *refs):
    pieces = refs[:count]
    head, column_ref, logit_ref, scaled_ref, stats_ref, held, highest, table, sems = refs[count:]
    blk = pieces[0].shape[0]
    copies = []
    for i, piece in enumerate(pieces):
        copies.append(pltpu.make_async_copy(piece, held.at[pl.ds(i * blk, blk)], sems.at[i]))
        copies[-1].start()
    for copy in copies:
        copy.wait()
    multiply(lambda: held[...], head, logit_ref, highest, step)

    def one(part, carry):
        rows = pl.ds(pl.multiple_of(part * chunk, chunk), chunk)
        logit = logit_ref[rows, :]
        top = jnp.max(highest[rows, :], axis=1, keepdims=True)
        scaled = jnp.exp(logit - top)
        hit = lax.broadcasted_iota(jnp.int32, logit.shape, 1) == column_ref[rows, :]
        picked = jnp.sum(jnp.where(hit, logit, 0.0), axis=1, keepdims=True)
        scaled_ref[rows, :] = scaled
        table[rows, :] = as_columns(top, jnp.sum(scaled, axis=1, keepdims=True), picked)
        return carry

    lax.fori_loop(0, logit_ref.shape[0] // chunk, one, 0)
    stats_ref[...] = table[...].T[0:8]


def teacher_kernel(count, step, chunk, *refs):
    pieces = refs[:count]
    head, stud_logit_ref, stud_ref, scaled_ref, stats_ref, highest, table = refs[count:]

    def read_rows():
        return jnp.concatenate([ref[...] for ref in pieces], axis=0) if count > 1 else pieces[0][...]

    multiply(read_rows, head, scaled_ref, highest, step)

    def one(part, carry):
        rows = pl.ds(pl.multiple_of(part * chunk, chunk), chunk)
        logit = scaled_ref[rows, :]
        top = jnp.max(highest[rows, :], axis=1, keepdims=True)
        scaled = jnp.exp(logit - top)
        gap = jnp.sum(scaled * (logit - stud_logit_ref[rows, :]), axis=1, keepdims=True)
        scaled_ref[rows, :] = scaled
        table[rows, :] = as_columns(top, jnp.sum(scaled, axis=1, keepdims=True), gap)
        return carry

    lax.fori_loop(0, scaled_ref.shape[0] // chunk, one, 0)
    teach = table[...].T[0:8]
    row = lax.broadcasted_iota(jnp.int32, teach.shape, 0)
    stats_ref[...] = jnp.where(row < 4, teach, pltpu.roll(stud_ref[...], 4, 0))


def head_cost(rows, head):
    depth, vocab_dev = head.shape
    return pl.CostEstimate(
        flops=2 * rows * depth * vocab_dev,
        bytes_accessed=2 * depth * vocab_dev + 12 * rows * vocab_dev,
        transcendentals=rows * vocab_dev,
    )


def student_logits(pieces, head, column, step, chunk):
    rows, vocab_dev = column.shape[0], head.shape[1]
    wide = (rows, vocab_dev)
    return pl.pallas_call(
        functools.partial(student_kernel, len(pieces), step, chunk),
        in_specs=[in_place] * len(pieces) + [in_vmem] * 2,
        out_specs=[in_vmem] * 3,
        out_shape=[
            jax.ShapeDtypeStruct(wide, jnp.float32),
            jax.ShapeDtypeStruct(wide, jnp.float32),
            jax.ShapeDtypeStruct((8, rows), jnp.float32),
        ],
        scratch_shapes=[
            pltpu.VMEM((rows, head.shape[0]), jnp.bfloat16),
            pltpu.VMEM((rows, lanes), jnp.float32),
            pltpu.VMEM((rows, lanes), jnp.float32),
            pltpu.SemaphoreType.DMA((len(pieces),)),
        ],
        compiler_params=pltpu.CompilerParams(vmem_limit_bytes=vmem_bytes),
        cost_estimate=head_cost(rows, head),
    )(*pieces, head, column)


def teacher_logits(pieces, head, logit_stud, stats_stud, step, chunk):
    wide = logit_stud.shape
    return pl.pallas_call(
        functools.partial(teacher_kernel, len(pieces), step, chunk),
        in_specs=[in_vmem] * (len(pieces) + 3),
        out_specs=[in_vmem] * 2,
        out_shape=[
            jax.ShapeDtypeStruct(wide, jnp.float32),
            jax.ShapeDtypeStruct((8, wide[0]), jnp.float32),
        ],
        scratch_shapes=[pltpu.VMEM((wide[0], lanes), jnp.float32)] * 2,
        compiler_params=pltpu.CompilerParams(vmem_limit_bytes=vmem_bytes),
        cost_estimate=head_cost(wide[0], head),
    )(*pieces, head, logit_stud, stats_stud)


def swapped(values, distance):
    total = values.shape[1]
    lane = lax.broadcasted_iota(jnp.int32, values.shape, 1)
    return jnp.where(
        (lane & distance) != 0, pltpu.roll(values, distance, 1), pltpu.roll(values, total - distance, 1)
    )


def gradient_kernel(bits, step, chunk, place_ref, *refs):
    count = 1 << bits
    tables, refs = refs[:count], refs[count:]
    teach_ref, stud_ref, column_ref, head, loss_ref = refs[:5]
    outs = refs[5 : count + 5]
    entries, upstream, factors = refs[count + 5 :]
    rows = upstream.shape[0]
    blk = rows // count
    me = place_ref[0]
    for mask in range(count):
        values = tables[mask][...]
        for bit in range(bits):
            if mask >> bit & 1:
                values = swapped(values, blk << bit)
        entries[me ^ mask] = values
    every = entries[...]
    top_teach = jnp.max(every[:, 0:1], axis=0)
    top_stud = jnp.max(every[:, 4:5], axis=0)
    weight = jnp.exp(every[:, 0:1] - top_teach)
    total_teach = jnp.sum(weight * every[:, 1:2], axis=0)
    total_stud = jnp.sum(jnp.exp(every[:, 4:5] - top_stud) * every[:, 5:6], axis=0)
    lse_teach = top_teach + jnp.log(total_teach)
    lse_stud = top_stud + jnp.log(total_stud)
    gap = jnp.sum(weight * every[:, 2:3], axis=0) / total_teach
    loss = gap - lse_teach + 2.0 * lse_stud - jnp.sum(every[:, 6:7], axis=0)
    loss = jnp.broadcast_to(loss, loss_ref.shape)
    for bit in range(bits):
        loss = jnp.where(((me >> bit) & 1) == 1, swapped(loss, blk << bit), loss)
    loss_ref[...] = loss
    own = tables[0][...]
    scale_teach = -loss_scale * jnp.exp(own[0:1] - lse_teach)
    scale_stud = 2.0 * loss_scale * jnp.exp(own[4:5] - lse_stud)
    line = lax.broadcasted_iota(jnp.int32, (lanes, rows), 0)
    factors[...] = jnp.where(line == 0, scale_teach, scale_stud).T

    def one(part, carry):
        at = pl.ds(pl.multiple_of(part * chunk, chunk), chunk)
        hit = lax.broadcasted_iota(jnp.int32, (chunk, teach_ref.shape[1]), 1) == column_ref[at, :]
        both = teach_ref[at, :] * factors[at, 0:1] + stud_ref[at, :] * factors[at, 1:2]
        upstream[at, :] = jnp.where(hit, both - loss_scale, both).astype(jnp.bfloat16)
        return carry

    lax.fori_loop(0, rows // chunk, one, 0)

    def two(index, carry):
        at = pl.ds(pl.multiple_of(index * step, step), step)
        product = lax.dot_general(
            upstream[...], head[at, :], (((1,), (1,)), ((), ())), preferred_element_type=jnp.float32
        )
        for piece, out in enumerate(outs):
            out[:, at] = product[piece * blk : (piece + 1) * blk]
        return carry

    lax.fori_loop(0, head.shape[0] // step, two, 0)


def gradient(place, tables, scaled_teach, scaled_stud, column, head, bits, chunk):
    rows, vocab_dev = scaled_teach.shape
    count, width = 1 << bits, head.shape[0]
    step = 512 if width % 512 == 0 else width
    return pl.pallas_call(
        functools.partial(gradient_kernel, bits, step, chunk),
        in_specs=[in_smem] + [in_vmem] * (count + 4),
        out_specs=[in_vmem] * (count + 1),
        out_shape=[jax.ShapeDtypeStruct((8, rows), jnp.float32)]
        + [jax.ShapeDtypeStruct((rows // count, width), jnp.float32)] * count,
        scratch_shapes=[
            pltpu.VMEM((count, 8, rows), jnp.float32),
            pltpu.VMEM((rows, vocab_dev), jnp.bfloat16),
            pltpu.VMEM((rows, lanes), jnp.float32),
        ],
        compiler_params=pltpu.CompilerParams(vmem_limit_bytes=vmem_bytes),
        cost_estimate=head_cost(rows, head),
    )(place, *tables, scaled_teach, scaled_stud, column, head)


def tie(block, *others):
    return lax.optimization_barrier((block, *others))[0]


def make_body(vocab_size):
    bits = vocab_size.bit_length() - 1
    assert vocab_size == 1 << bits

    def swap(block, bit):
        return lax.ppermute(block, "vocab", [(at, at ^ (1 << bit)) for at in range(vocab_size)])

    def lowest(mask):
        return (mask & -mask).bit_length() - 1

    def spread(own, line):
        blocks = [own]
        for mask in range(1, vocab_size):
            bit = lowest(mask)
            block = blocks[mask ^ (1 << bit)]
            if bit == 0:
                block = tie(block, line[-3])
            blocks.append(swap(block, bit))
            if bit == 0:
                line.append(blocks[-1])
        return blocks

    def reduce_blocks(parts, beside=None):
        terms, line = list(parts), []
        for mask in range(vocab_size - 1, 0, -1):
            bit = lowest(mask)
            block = terms[mask].astype(wire)
            if bit == 0 and len(line) > 1:
                block = tie(block, line[-2])
                if beside is not None and len(line) == 2:
                    block = tie(block, beside(line[0]))
            block = swap(block, bit)
            if bit == 0:
                line.append(block)
            terms[mask ^ (1 << bit)] = terms[mask ^ (1 << bit)] + block.astype(jnp.float32)
        return terms[0], line

    def body(teacher_rows, owner, counts, proj_weight, student_hidden, head_weight, targets):
        teach_rows = teacher_rows.shape[0]
        slab_rows = targets.shape[0]
        vocab_dev = head_weight.shape[1]
        blk = slab_rows // vocab_size
        chunk = min(slab_rows, 32)
        me = lax.axis_index("vocab")
        core = lax.axis_index("seq")
        place = jnp.stack([me, core]).astype(jnp.int32)

        def in_order(vec):
            grid = vec.reshape((2,) * bits + (blk,))
            for bit in range(bits):
                grid = jnp.where((me >> bit) & 1 == 1, jnp.flip(grid, bits - 1 - bit), grid)
            return grid.reshape(slab_rows)

        def turned(block):
            return jnp.where(core == 1, jnp.roll(block, block.shape[1] // 2, axis=1), block)

        def as_pieces(blocks):
            return blocks if blk % 16 == 0 else [jnp.concatenate(blocks, axis=0)]

        other_half = lax.ppermute(head_weight, "seq", [(0, 1), (1, 0)])

        spot = lax.iota(jnp.int32, slab_rows)
        row_id = ((spot // blk) ^ me) * blk + spot % blk
        alive = lax.iota(jnp.int32, teach_rows) < counts[0]
        member = (owner[None, :] == row_id[:, None]) & alive[None, :]
        parts = project(member.astype(jnp.bfloat16), teacher_rows, proj_weight, vocab_size, 512 if student_hidden.shape[1] % 512 == 0 else student_hidden.shape[1])
        staged = []

        def stage_after(block):
            staged.append(stage((head_weight, tie(other_half, block))))
            return staged[0]

        projected_own, line = reduce_blocks(parts, stage_after)
        head = staged[0]
        hidden = spread(tie(turned(student_hidden), parts[-1]), line)
        projected = spread(turned(projected_own.astype(jnp.bfloat16)), line)

        column = (in_order(targets) - me * vocab_dev)[:, None]
        logit_stud, scaled_stud, stats_stud = student_logits(as_pieces(hidden), head, column, 512, chunk)
        scaled_teach, stats = teacher_logits(as_pieces(projected), head, logit_stud, stats_stud, 512, chunk)
        tables = [stats]
        for mask in range(1, vocab_size):
            far, near = mask & ~3, mask & 3
            source, hop = (tables[far], near) if near else (stats, far)
            tables.append(lax.ppermute(source, "vocab", [(at, at ^ hop) for at in range(vocab_size)]))
        loss, *terms = gradient(place, tables, scaled_teach, scaled_stud, column, head, bits, chunk)
        return (loss[0], turned(reduce_blocks(terms)[0].astype(jnp.bfloat16)))

    return body


def solution(mesh):
    return jax.shard_map(
        make_body(mesh.shape["vocab"]),
        mesh=mesh,
        in_specs=(
            P(("groups", "seq"), "vocab"),
            P(("groups", "seq")),
            P(("groups", "seq")),
            P("vocab", None),
            P(("groups", "seq", "vocab"), None),
            P("seq", "vocab"),
            P(("groups", "seq")),
        ),
        out_specs=(P(("groups", "seq")), P(("groups", "seq", "vocab"), None)),
        check_vma=False,
    )
```

```python
import functools

import jax
import jax.numpy as jnp
from jax import lax
from jax.experimental import pallas as pl
from jax.experimental.pallas import tpu as pltpu
from jax.sharding import PartitionSpec as P

loss_scale = 64.0
wire = jnp.float16
lanes = 128
vmem_bytes = 12 * 1024 * 1024
project_bytes = 50 * 1024 * 1024

in_vmem = pl.BlockSpec(memory_space=pltpu.VMEM)
in_smem = pl.BlockSpec(memory_space=pltpu.SMEM)
in_place = pl.BlockSpec(memory_space=pl.ANY)


def cuts(total, step):
    return [(start, min(step, total - start)) for start in range(0, total, step)]


def project_kernel(count, step, member_ref, teacher_ref, weight_ref, *rest):
    outs, (teacher, weight, aligned, sems) = rest[:count], rest[count:]
    blk = outs[0].shape[0]
    parts = cuts(weight.shape[1], step)
    first = pltpu.make_async_copy(teacher_ref, teacher, sems.at[len(parts)])
    first.start()
    for index, (start, size) in enumerate(parts):
        at = pl.ds(start, size)
        pltpu.make_async_copy(weight_ref.at[:, at], weight.at[:, at], sems.at[index]).start()
    member = member_ref[...]
    sizes = jnp.sum(member.astype(jnp.float32), axis=1, keepdims=True)
    first.wait()
    summed = jnp.dot(member, teacher[...], preferred_element_type=jnp.float32)
    aligned[...] = (summed / sizes).astype(jnp.bfloat16)

    def one(index, carry):
        at = pl.ds(pl.multiple_of(index * step, step), step)
        pltpu.make_async_copy(weight_ref.at[:, at], weight.at[:, at], sems.at[index]).wait()
        product = jnp.dot(aligned[...], weight[:, at], preferred_element_type=jnp.float32)
        for piece, out in enumerate(outs):
            out[:, at] = product[piece * blk : (piece + 1) * blk]
        return carry

    lax.fori_loop(0, len(parts), one, 0)


def project(member, teacher_rows, proj_weight, count, step):
    slab_rows, (depth, width) = member.shape[0], proj_weight.shape
    blk = slab_rows // count
    return pl.pallas_call(
        functools.partial(project_kernel, count, step),
        in_specs=[in_vmem, in_place, in_place],
        out_specs=[in_vmem] * count,
        out_shape=[jax.ShapeDtypeStruct((blk, width), jnp.float32)] * count,
        scratch_shapes=[
            pltpu.VMEM(teacher_rows.shape, jnp.bfloat16),
            pltpu.VMEM(proj_weight.shape, jnp.bfloat16),
            pltpu.VMEM((slab_rows, depth), jnp.bfloat16),
            pltpu.SemaphoreType.DMA((len(cuts(width, step)) + 1,)),
        ],
        compiler_params=pltpu.CompilerParams(vmem_limit_bytes=project_bytes),
        cost_estimate=pl.CostEstimate(
            flops=2 * slab_rows * depth * (width + teacher_rows.shape[0]),
            bytes_accessed=2 * depth * (width + teacher_rows.shape[0]) + 4 * slab_rows * width,
            transcendentals=0,
        ),
    )(member, teacher_rows, proj_weight)


class Fetch:
    def __init__(self, sems):
        self.sems, self.used = sems, 0

    def start(self, source, target):
        copy = pltpu.make_async_copy(source, target, self.sems.at[self.used])
        copy.start()
        self.used += 1
        return copy


def multiply(read_rows, head, logit_ref, highest, step, ready=None):
    total = head.shape[1]
    highest[...] = jnp.full(highest.shape, -jnp.inf, jnp.float32)

    def one(index, start, size):
        at = pl.ds(start, size)
        if ready is not None:
            ready(index, at)
        part = jnp.dot(read_rows(), head[:, at], preferred_element_type=jnp.float32)
        logit_ref[:, at] = part
        top = part[:, :lanes]
        for lane in range(lanes, size, lanes):
            top = jnp.maximum(top, part[:, lane : lane + lanes])
        highest[...] = jnp.maximum(highest[...], top)

    def body(index, carry):
        one(index, pl.multiple_of(index * step, step), step)
        return carry

    full = total // step
    lax.fori_loop(0, full, body, 0)
    if total % step:
        one(full, full * step, total % step)


def as_columns(first, second, third):
    lane = lax.broadcasted_iota(jnp.int32, (first.shape[0], lanes), 1)
    return jnp.where(lane == 0, first, jnp.where(lane == 1, second, jnp.where(lane == 2, third, 0.0)))


def student_kernel(count, step, chunk, *refs):
    pieces, heads = refs[:count], refs[count : count + 2]
    column_ref, logit_ref, scaled_ref, stats_ref, head = refs[count + 2 : count + 7]
    held, highest, table, sems = refs[count + 7 :]
    depth, total = heads[0].shape
    blk = pieces[0].shape[0]
    fetch = Fetch(sems)
    waits = [fetch.start(piece, held.at[pl.ds(i * blk, blk)]) for i, piece in enumerate(pieces)]
    first = fetch.used

    def columns(half, at):
        return heads[half].at[:, at], head.at[pl.ds(half * depth, depth), at]

    for start, size in cuts(total, step):
        for half in range(2):
            fetch.start(*columns(half, pl.ds(start, size)))

    def ready(index, at):
        for half in range(2):
            pltpu.make_async_copy(*columns(half, at), sems.at[first + 2 * index + half]).wait()

    for wait in waits:
        wait.wait()
    multiply(lambda: held[...], head, logit_ref, highest, step, ready)

    def one(part, carry):
        rows = pl.ds(pl.multiple_of(part * chunk, chunk), chunk)
        logit = logit_ref[rows, :]
        top = jnp.max(highest[rows, :], axis=1, keepdims=True)
        scaled = jnp.exp(logit - top)
        hit = lax.broadcasted_iota(jnp.int32, logit.shape, 1) == column_ref[rows, :]
        picked = jnp.sum(jnp.where(hit, logit, 0.0), axis=1, keepdims=True)
        scaled_ref[rows, :] = scaled
        table[rows, :] = as_columns(top, jnp.sum(scaled, axis=1, keepdims=True), picked)
        return carry

    lax.fori_loop(0, logit_ref.shape[0] // chunk, one, 0)
    stats_ref[...] = table[...].T[0:8]


def teacher_kernel(count, step, chunk, *refs):
    pieces = refs[:count]
    head, stud_logit_ref, stud_ref, scaled_ref, stats_ref, highest, table = refs[count:]

    def read_rows():
        return jnp.concatenate([ref[...] for ref in pieces], axis=0) if count > 1 else pieces[0][...]

    multiply(read_rows, head, scaled_ref, highest, step)

    def one(part, carry):
        rows = pl.ds(pl.multiple_of(part * chunk, chunk), chunk)
        logit = scaled_ref[rows, :]
        top = jnp.max(highest[rows, :], axis=1, keepdims=True)
        scaled = jnp.exp(logit - top)
        gap = jnp.sum(scaled * (logit - stud_logit_ref[rows, :]), axis=1, keepdims=True)
        scaled_ref[rows, :] = scaled
        table[rows, :] = as_columns(top, jnp.sum(scaled, axis=1, keepdims=True), gap)
        return carry

    lax.fori_loop(0, scaled_ref.shape[0] // chunk, one, 0)
    teach = table[...].T[0:8]
    row = lax.broadcasted_iota(jnp.int32, teach.shape, 0)
    stats_ref[...] = jnp.where(row < 4, teach, pltpu.roll(stud_ref[...], 4, 0))


def head_cost(rows, head):
    depth, vocab_dev = head.shape
    return pl.CostEstimate(
        flops=2 * rows * depth * vocab_dev,
        bytes_accessed=2 * depth * vocab_dev + 12 * rows * vocab_dev,
        transcendentals=rows * vocab_dev,
    )


def student_logits(pieces, heads, column, step, chunk):
    rows, (depth, vocab_dev) = column.shape[0], heads[0].shape
    wide = (rows, vocab_dev)
    return pl.pallas_call(
        functools.partial(student_kernel, len(pieces), step, chunk),
        in_specs=[in_place] * (len(pieces) + 2) + [in_vmem],
        out_specs=[in_vmem] * 4,
        out_shape=[
            jax.ShapeDtypeStruct(wide, jnp.float32),
            jax.ShapeDtypeStruct(wide, jnp.float32),
            jax.ShapeDtypeStruct((8, rows), jnp.float32),
            jax.ShapeDtypeStruct((2 * depth, vocab_dev), jnp.bfloat16),
        ],
        scratch_shapes=[
            pltpu.VMEM((rows, 2 * depth), jnp.bfloat16),
            pltpu.VMEM((rows, lanes), jnp.float32),
            pltpu.VMEM((rows, lanes), jnp.float32),
            pltpu.SemaphoreType.DMA((len(pieces) + 2 * len(cuts(vocab_dev, step)),)),
        ],
        compiler_params=pltpu.CompilerParams(vmem_limit_bytes=vmem_bytes),
        cost_estimate=head_cost(rows, heads[0]),
    )(*pieces, *heads, column)


def teacher_logits(pieces, head, logit_stud, stats_stud, step, chunk):
    wide = logit_stud.shape
    return pl.pallas_call(
        functools.partial(teacher_kernel, len(pieces), step, chunk),
        in_specs=[in_vmem] * (len(pieces) + 3),
        out_specs=[in_vmem] * 2,
        out_shape=[
            jax.ShapeDtypeStruct(wide, jnp.float32),
            jax.ShapeDtypeStruct((8, wide[0]), jnp.float32),
        ],
        scratch_shapes=[pltpu.VMEM((wide[0], lanes), jnp.float32)] * 2,
        compiler_params=pltpu.CompilerParams(vmem_limit_bytes=vmem_bytes),
        cost_estimate=head_cost(wide[0], head),
    )(*pieces, head, logit_stud, stats_stud)


def swapped(values, distance):
    total = values.shape[1]
    lane = lax.broadcasted_iota(jnp.int32, values.shape, 1)
    return jnp.where(
        (lane & distance) != 0, pltpu.roll(values, distance, 1), pltpu.roll(values, total - distance, 1)
    )


def gradient_kernel(bits, step, chunk, place_ref, *refs):
    count = 1 << bits
    tables, refs = refs[:count], refs[count:]
    teach_ref, stud_ref, column_ref, head, loss_ref = refs[:5]
    outs = refs[5 : count + 5]
    entries, upstream, factors = refs[count + 5 :]
    rows = upstream.shape[0]
    blk = rows // count
    me = place_ref[0]
    for mask in range(count):
        values = tables[mask][...]
        for bit in range(bits):
            if mask >> bit & 1:
                values = swapped(values, blk << bit)
        entries[me ^ mask] = values
    every = entries[...]
    top_teach = jnp.max(every[:, 0:1], axis=0)
    top_stud = jnp.max(every[:, 4:5], axis=0)
    weight = jnp.exp(every[:, 0:1] - top_teach)
    total_teach = jnp.sum(weight * every[:, 1:2], axis=0)
    total_stud = jnp.sum(jnp.exp(every[:, 4:5] - top_stud) * every[:, 5:6], axis=0)
    lse_teach = top_teach + jnp.log(total_teach)
    lse_stud = top_stud + jnp.log(total_stud)
    gap = jnp.sum(weight * every[:, 2:3], axis=0) / total_teach
    loss = gap - lse_teach + 2.0 * lse_stud - jnp.sum(every[:, 6:7], axis=0)
    loss = jnp.broadcast_to(loss, loss_ref.shape)
    for bit in range(bits):
        loss = jnp.where(((me >> bit) & 1) == 1, swapped(loss, blk << bit), loss)
    loss_ref[...] = loss
    own = tables[0][...]
    scale_teach = -loss_scale * jnp.exp(own[0:1] - lse_teach)
    scale_stud = 2.0 * loss_scale * jnp.exp(own[4:5] - lse_stud)
    line = lax.broadcasted_iota(jnp.int32, (lanes, rows), 0)
    factors[...] = jnp.where(line == 0, scale_teach, scale_stud).T

    def one(part, carry):
        at = pl.ds(pl.multiple_of(part * chunk, chunk), chunk)
        hit = lax.broadcasted_iota(jnp.int32, (chunk, teach_ref.shape[1]), 1) == column_ref[at, :]
        both = teach_ref[at, :] * factors[at, 0:1] + stud_ref[at, :] * factors[at, 1:2]
        upstream[at, :] = jnp.where(hit, both - loss_scale, both).astype(jnp.bfloat16)
        return carry

    lax.fori_loop(0, rows // chunk, one, 0)

    def two(index, carry):
        at = pl.ds(pl.multiple_of(index * step, step), step)
        product = lax.dot_general(
            upstream[...], head[at, :], (((1,), (1,)), ((), ())), preferred_element_type=jnp.float32
        )
        for piece, out in enumerate(outs):
            out[:, at] = product[piece * blk : (piece + 1) * blk]
        return carry

    lax.fori_loop(0, head.shape[0] // step, two, 0)


def gradient(place, tables, scaled_teach, scaled_stud, column, head, bits, chunk):
    rows, vocab_dev = scaled_teach.shape
    count, width = 1 << bits, head.shape[0]
    step = 512 if width % 512 == 0 else width
    return pl.pallas_call(
        functools.partial(gradient_kernel, bits, step, chunk),
        in_specs=[in_smem] + [in_vmem] * (count + 4),
        out_specs=[in_vmem] * (count + 1),
        out_shape=[jax.ShapeDtypeStruct((8, rows), jnp.float32)]
        + [jax.ShapeDtypeStruct((rows // count, width), jnp.float32)] * count,
        scratch_shapes=[
            pltpu.VMEM((count, 8, rows), jnp.float32),
            pltpu.VMEM((rows, vocab_dev), jnp.bfloat16),
            pltpu.VMEM((rows, lanes), jnp.float32),
        ],
        compiler_params=pltpu.CompilerParams(vmem_limit_bytes=vmem_bytes),
        cost_estimate=head_cost(rows, head),
    )(place, *tables, scaled_teach, scaled_stud, column, head)


def tie(block, *others):
    return lax.optimization_barrier((block, *others))[0]


def flipped(mask):
    return (mask & ~3) | ((mask & 1) << 1) | ((mask >> 1) & 1)


def make_body(vocab_size, cores):
    bits = vocab_size.bit_length() - 1
    assert vocab_size == 1 << bits

    def trade(block, mask):
        pairs = [
            (core * vocab_size + at, core * vocab_size + (at ^ (flipped(mask) if core % 2 else mask)))
            for core in range(cores)
            for at in range(vocab_size)
        ]
        return lax.ppermute(block, ("seq", "vocab"), pairs)

    def swap(block, bit):
        return trade(block, 1 << bit)

    def lowest(mask):
        return (mask & -mask).bit_length() - 1

    def spread(own, line):
        blocks = [own]
        for mask in range(1, vocab_size):
            bit = lowest(mask)
            block = blocks[mask ^ (1 << bit)]
            if bit == 0:
                block = tie(block, line[-3])
            blocks.append(swap(block, bit))
            if bit == 0:
                line.append(blocks[-1])
        return blocks

    def reduce_blocks(parts):
        terms, line = list(parts), []
        for mask in range(vocab_size - 1, 0, -1):
            bit = lowest(mask)
            block = terms[mask].astype(wire)
            if bit == 0 and len(line) > 1:
                block = tie(block, line[-2])
            block = swap(block, bit)
            if bit == 0:
                line.append(block)
            terms[mask ^ (1 << bit)] = terms[mask ^ (1 << bit)] + block.astype(jnp.float32)
        return terms[0], line

    def body(teacher_rows, owner, counts, proj_weight, student_hidden, head_weight, targets):
        teach_rows = teacher_rows.shape[0]
        slab_rows = targets.shape[0]
        vocab_dev = head_weight.shape[1]
        blk = slab_rows // vocab_size
        chunk = min(slab_rows, 32)
        me = lax.axis_index("vocab")
        core = lax.axis_index("seq")
        odd = core % 2 == 1
        spin = jnp.where(odd, flipped(me), me)
        place = jnp.stack([spin, core]).astype(jnp.int32)

        def by_core(vec):
            grid = vec.reshape(-1, 2, 2, blk)
            return jnp.where(odd, jnp.swapaxes(grid, 1, 2), grid).reshape(slab_rows)

        def in_order(vec):
            grid = by_core(vec).reshape((2,) * bits + (blk,))
            for bit in range(bits):
                grid = jnp.where((spin >> bit) & 1 == 1, jnp.flip(grid, bits - 1 - bit), grid)
            return grid.reshape(slab_rows)

        def turned(block):
            return jnp.where(core == 1, jnp.roll(block, block.shape[1] // 2, axis=1), block)

        def as_pieces(blocks):
            return blocks if blk % 16 == 0 else [jnp.concatenate(blocks, axis=0)]

        heads = (head_weight, lax.ppermute(head_weight, "seq", [(0, 1), (1, 0)]))

        spot = lax.iota(jnp.int32, slab_rows)
        row_id = (jnp.where(odd, flipped(spot // blk), spot // blk) ^ me) * blk + spot % blk
        alive = lax.iota(jnp.int32, teach_rows) < counts[0]
        member = (owner[None, :] == row_id[:, None]) & alive[None, :]
        parts = project(member.astype(jnp.bfloat16), teacher_rows, proj_weight, vocab_size, 512 if student_hidden.shape[1] % 512 == 0 else student_hidden.shape[1])
        projected_own, line = reduce_blocks(parts)
        hidden = spread(tie(turned(student_hidden), parts[-1]), line)
        projected = spread(turned(projected_own.astype(jnp.bfloat16)), line)

        column = (in_order(targets) - me * vocab_dev)[:, None]
        logit_stud, scaled_stud, stats_stud, head = student_logits(as_pieces(hidden), heads, column, 256, chunk)
        scaled_teach, stats = teacher_logits(as_pieces(projected), head, logit_stud, stats_stud, 512, chunk)
        tables = [stats]
        for mask in range(1, vocab_size):
            far, near = mask & ~3, mask & 3
            tables.append(trade(tables[far], near) if near else trade(stats, far))
        loss, *terms = gradient(place, tables, scaled_teach, scaled_stud, column, head, bits, chunk)
        return (by_core(loss[0]), turned(reduce_blocks(terms)[0].astype(jnp.bfloat16)))

    return body


def solution(mesh):
    return jax.shard_map(
        make_body(mesh.shape["vocab"], mesh.shape["seq"]),
        mesh=mesh,
        in_specs=(
            P(("groups", "seq"), "vocab"),
            P(("groups", "seq")),
            P(("groups", "seq")),
            P("vocab", None),
            P(("groups", "seq", "vocab"), None),
            P("seq", "vocab"),
            P(("groups", "seq")),
        ),
        out_specs=(P(("groups", "seq")), P(("groups", "seq", "vocab"), None)),
        check_vma=False,
    )
```

```python
import functools

import jax
import jax.numpy as jnp
from jax import lax
from jax.experimental import pallas as pl
from jax.experimental.pallas import tpu as pltpu
from jax.sharding import PartitionSpec as P

loss_scale = 64.0
wire = jnp.float16
lanes = 128
vmem_bytes = 12 * 1024 * 1024
project_bytes = 50 * 1024 * 1024

in_vmem = pl.BlockSpec(memory_space=pltpu.VMEM)
in_smem = pl.BlockSpec(memory_space=pltpu.SMEM)
in_place = pl.BlockSpec(memory_space=pl.ANY)


def cuts(total, step):
    return [(start, min(step, total - start)) for start in range(0, total, step)]


def project_kernel(count, step, member_ref, teacher_ref, weight_ref, *rest):
    outs, (teacher, weight, aligned, sems) = rest[:count], rest[count:]
    blk = outs[0].shape[0]
    parts = cuts(weight.shape[1], step)
    first = pltpu.make_async_copy(teacher_ref, teacher, sems.at[len(parts)])
    first.start()
    for index, (start, size) in enumerate(parts):
        at = pl.ds(start, size)
        pltpu.make_async_copy(weight_ref.at[:, at], weight.at[:, at], sems.at[index]).start()
    member = member_ref[...]
    sizes = jnp.sum(member.astype(jnp.float32), axis=1, keepdims=True)
    first.wait()
    summed = jnp.dot(member, teacher[...], preferred_element_type=jnp.float32)
    aligned[...] = (summed / sizes).astype(jnp.bfloat16)

    def one(index, carry):
        at = pl.ds(pl.multiple_of(index * step, step), step)
        pltpu.make_async_copy(weight_ref.at[:, at], weight.at[:, at], sems.at[index]).wait()
        product = jnp.dot(aligned[...], weight[:, at], preferred_element_type=jnp.float32)
        for piece, out in enumerate(outs):
            out[:, at] = product[piece * blk : (piece + 1) * blk]
        return carry

    lax.fori_loop(0, len(parts), one, 0)


def project(member, teacher_rows, proj_weight, count, step):
    slab_rows, (depth, width) = member.shape[0], proj_weight.shape
    blk = slab_rows // count
    return pl.pallas_call(
        functools.partial(project_kernel, count, step),
        in_specs=[in_vmem, in_place, in_place],
        out_specs=[in_vmem] * count,
        out_shape=[jax.ShapeDtypeStruct((blk, width), jnp.float32)] * count,
        scratch_shapes=[
            pltpu.VMEM(teacher_rows.shape, jnp.bfloat16),
            pltpu.VMEM(proj_weight.shape, jnp.bfloat16),
            pltpu.VMEM((slab_rows, depth), jnp.bfloat16),
            pltpu.SemaphoreType.DMA((len(cuts(width, step)) + 1,)),
        ],
        compiler_params=pltpu.CompilerParams(vmem_limit_bytes=project_bytes),
        cost_estimate=pl.CostEstimate(
            flops=2 * slab_rows * depth * (width + teacher_rows.shape[0]),
            bytes_accessed=2 * depth * (width + teacher_rows.shape[0]) + 4 * slab_rows * width,
            transcendentals=0,
        ),
    )(member, teacher_rows, proj_weight)


class Fetch:
    def __init__(self, sems):
        self.sems, self.used = sems, 0

    def start(self, source, target):
        copy = pltpu.make_async_copy(source, target, self.sems.at[self.used])
        copy.start()
        self.used += 1
        return copy


def multiply(read_rows, head, logit_ref, highest, step, ready=None):
    total = head.shape[1]
    highest[...] = jnp.full(highest.shape, -jnp.inf, jnp.float32)

    def one(index, start, size):
        at = pl.ds(start, size)
        if ready is not None:
            ready(index, at)
        part = jnp.dot(read_rows(), head[:, at], preferred_element_type=jnp.float32)
        logit_ref[:, at] = part
        top = part[:, :lanes]
        for lane in range(lanes, size, lanes):
            top = jnp.maximum(top, part[:, lane : lane + lanes])
        highest[...] = jnp.maximum(highest[...], top)

    def body(index, carry):
        one(index, pl.multiple_of(index * step, step), step)
        return carry

    full = total // step
    lax.fori_loop(0, full, body, 0)
    if total % step:
        one(full, full * step, total % step)


def as_columns(first, second, third):
    lane = lax.broadcasted_iota(jnp.int32, (first.shape[0], lanes), 1)
    return jnp.where(lane == 0, first, jnp.where(lane == 1, second, jnp.where(lane == 2, third, 0.0)))


def student_kernel(count, step, chunk, *refs):
    pieces, heads = refs[:count], refs[count : count + 2]
    column_ref, logit_ref, scaled_ref, stats_ref, head = refs[count + 2 : count + 7]
    held, highest, table, sems = refs[count + 7 :]
    depth, total = heads[0].shape
    blk = pieces[0].shape[0]
    fetch = Fetch(sems)
    waits = [fetch.start(piece, held.at[pl.ds(i * blk, blk)]) for i, piece in enumerate(pieces)]
    first = fetch.used

    def columns(half, at):
        return heads[half].at[:, at], head.at[pl.ds(half * depth, depth), at]

    for start, size in cuts(total, step):
        for half in range(2):
            fetch.start(*columns(half, pl.ds(start, size)))

    def ready(index, at):
        for half in range(2):
            pltpu.make_async_copy(*columns(half, at), sems.at[first + 2 * index + half]).wait()

    for wait in waits:
        wait.wait()
    multiply(lambda: held[...], head, logit_ref, highest, step, ready)

    def one(part, carry):
        rows = pl.ds(pl.multiple_of(part * chunk, chunk), chunk)
        logit = logit_ref[rows, :]
        top = jnp.max(highest[rows, :], axis=1, keepdims=True)
        scaled = jnp.exp(logit - top)
        hit = lax.broadcasted_iota(jnp.int32, logit.shape, 1) == column_ref[rows, :]
        picked = jnp.sum(jnp.where(hit, logit, 0.0), axis=1, keepdims=True)
        scaled_ref[rows, :] = scaled
        table[rows, :] = as_columns(top, jnp.sum(scaled, axis=1, keepdims=True), picked)
        return carry

    lax.fori_loop(0, logit_ref.shape[0] // chunk, one, 0)
    stats_ref[...] = table[...].T[0:8]


def teacher_kernel(count, step, chunk, *refs):
    pieces = refs[:count]
    head, stud_logit_ref, stud_ref, scaled_ref, stats_ref, highest, table = refs[count:]

    def read_rows():
        return jnp.concatenate([ref[...] for ref in pieces], axis=0) if count > 1 else pieces[0][...]

    multiply(read_rows, head, scaled_ref, highest, step)

    def one(part, carry):
        rows = pl.ds(pl.multiple_of(part * chunk, chunk), chunk)
        logit = scaled_ref[rows, :]
        top = jnp.max(highest[rows, :], axis=1, keepdims=True)
        scaled = jnp.exp(logit - top)
        gap = jnp.sum(scaled * (logit - stud_logit_ref[rows, :]), axis=1, keepdims=True)
        scaled_ref[rows, :] = scaled
        table[rows, :] = as_columns(top, jnp.sum(scaled, axis=1, keepdims=True), gap)
        return carry

    lax.fori_loop(0, scaled_ref.shape[0] // chunk, one, 0)
    teach = table[...].T[0:8]
    row = lax.broadcasted_iota(jnp.int32, teach.shape, 0)
    stats_ref[...] = jnp.where(row < 4, teach, pltpu.roll(stud_ref[...], 4, 0))


def head_cost(rows, head):
    depth, vocab_dev = head.shape
    return pl.CostEstimate(
        flops=2 * rows * depth * vocab_dev,
        bytes_accessed=2 * depth * vocab_dev + 12 * rows * vocab_dev,
        transcendentals=rows * vocab_dev,
    )


def student_logits(pieces, heads, column, step, chunk):
    rows, (depth, vocab_dev) = column.shape[0], heads[0].shape
    wide = (rows, vocab_dev)
    return pl.pallas_call(
        functools.partial(student_kernel, len(pieces), step, chunk),
        in_specs=[in_place] * (len(pieces) + 2) + [in_vmem],
        out_specs=[in_vmem] * 4,
        out_shape=[
            jax.ShapeDtypeStruct(wide, jnp.float32),
            jax.ShapeDtypeStruct(wide, jnp.float32),
            jax.ShapeDtypeStruct((8, rows), jnp.float32),
            jax.ShapeDtypeStruct((2 * depth, vocab_dev), jnp.bfloat16),
        ],
        scratch_shapes=[
            pltpu.VMEM((rows, 2 * depth), jnp.bfloat16),
            pltpu.VMEM((rows, lanes), jnp.float32),
            pltpu.VMEM((rows, lanes), jnp.float32),
            pltpu.SemaphoreType.DMA((len(pieces) + 2 * len(cuts(vocab_dev, step)),)),
        ],
        compiler_params=pltpu.CompilerParams(vmem_limit_bytes=vmem_bytes),
        cost_estimate=head_cost(rows, heads[0]),
    )(*pieces, *heads, column)


def teacher_logits(pieces, head, logit_stud, stats_stud, step, chunk):
    wide = logit_stud.shape
    return pl.pallas_call(
        functools.partial(teacher_kernel, len(pieces), step, chunk),
        in_specs=[in_vmem] * (len(pieces) + 3),
        out_specs=[in_vmem] * 2,
        out_shape=[
            jax.ShapeDtypeStruct(wide, jnp.float32),
            jax.ShapeDtypeStruct((8, wide[0]), jnp.float32),
        ],
        scratch_shapes=[pltpu.VMEM((wide[0], lanes), jnp.float32)] * 2,
        compiler_params=pltpu.CompilerParams(vmem_limit_bytes=vmem_bytes),
        cost_estimate=head_cost(wide[0], head),
    )(*pieces, head, logit_stud, stats_stud)


def swapped(values, distance):
    total = values.shape[1]
    lane = lax.broadcasted_iota(jnp.int32, values.shape, 1)
    return jnp.where(
        (lane & distance) != 0, pltpu.roll(values, distance, 1), pltpu.roll(values, total - distance, 1)
    )


def gradient_kernel(bits, step, chunk, place_ref, *refs):
    count = 1 << bits
    tables, refs = refs[:count], refs[count:]
    teach_ref, stud_ref, column_ref, head, loss_ref = refs[:5]
    outs = refs[5 : count + 5]
    entries, upstream, factors = refs[count + 5 :]
    rows = upstream.shape[0]
    blk = rows // count
    me = place_ref[0]
    for mask in range(count):
        values = tables[mask][...]
        for bit in range(bits):
            if mask >> bit & 1:
                values = swapped(values, blk << bit)
        entries[me ^ mask] = values
    every = entries[...]
    top_teach = jnp.max(every[:, 0:1], axis=0)
    top_stud = jnp.max(every[:, 4:5], axis=0)
    weight = jnp.exp(every[:, 0:1] - top_teach)
    total_teach = jnp.sum(weight * every[:, 1:2], axis=0)
    total_stud = jnp.sum(jnp.exp(every[:, 4:5] - top_stud) * every[:, 5:6], axis=0)
    lse_teach = top_teach + jnp.log(total_teach)
    lse_stud = top_stud + jnp.log(total_stud)
    gap = jnp.sum(weight * every[:, 2:3], axis=0) / total_teach
    loss = gap - lse_teach + 2.0 * lse_stud - jnp.sum(every[:, 6:7], axis=0)
    loss = jnp.broadcast_to(loss, loss_ref.shape)
    for bit in range(bits):
        loss = jnp.where(((me >> bit) & 1) == 1, swapped(loss, blk << bit), loss)
    loss_ref[...] = loss
    own = tables[0][...]
    scale_teach = -loss_scale * jnp.exp(own[0:1] - lse_teach)
    scale_stud = 2.0 * loss_scale * jnp.exp(own[4:5] - lse_stud)
    line = lax.broadcasted_iota(jnp.int32, (lanes, rows), 0)
    factors[...] = jnp.where(line == 0, scale_teach, scale_stud).T

    def one(part, carry):
        at = pl.ds(pl.multiple_of(part * chunk, chunk), chunk)
        hit = lax.broadcasted_iota(jnp.int32, (chunk, teach_ref.shape[1]), 1) == column_ref[at, :]
        both = teach_ref[at, :] * factors[at, 0:1] + stud_ref[at, :] * factors[at, 1:2]
        upstream[at, :] = jnp.where(hit, both - loss_scale, both).astype(jnp.bfloat16)
        return carry

    lax.fori_loop(0, rows // chunk, one, 0)

    def two(index, carry):
        at = pl.ds(pl.multiple_of(index * step, step), step)
        product = lax.dot_general(
            upstream[...], head[at, :], (((1,), (1,)), ((), ())), preferred_element_type=jnp.float32
        )
        for piece, out in enumerate(outs):
            out[:, at] = product[piece * blk : (piece + 1) * blk]
        return carry

    lax.fori_loop(0, head.shape[0] // step, two, 0)


def gradient(place, tables, scaled_teach, scaled_stud, column, head, bits, chunk):
    rows, vocab_dev = scaled_teach.shape
    count, width = 1 << bits, head.shape[0]
    step = 896 if width % 896 == 0 else width
    return pl.pallas_call(
        functools.partial(gradient_kernel, bits, step, chunk),
        in_specs=[in_smem] + [in_vmem] * (count + 4),
        out_specs=[in_vmem] * (count + 1),
        out_shape=[jax.ShapeDtypeStruct((8, rows), jnp.float32)]
        + [jax.ShapeDtypeStruct((rows // count, width), jnp.float32)] * count,
        scratch_shapes=[
            pltpu.VMEM((count, 8, rows), jnp.float32),
            pltpu.VMEM((rows, vocab_dev), jnp.bfloat16),
            pltpu.VMEM((rows, lanes), jnp.float32),
        ],
        compiler_params=pltpu.CompilerParams(vmem_limit_bytes=vmem_bytes),
        cost_estimate=head_cost(rows, head),
    )(place, *tables, scaled_teach, scaled_stud, column, head)


def tie(block, *others):
    return lax.optimization_barrier((block, *others))[0]


def make_body(vocab_size):
    bits = vocab_size.bit_length() - 1
    assert vocab_size == 1 << bits

    def trade(block, mask):
        return lax.ppermute(block, "vocab", [(at, at ^ mask) for at in range(vocab_size)])

    def swap(block, bit):
        return trade(block, 1 << bit)

    def lowest(mask):
        return (mask & -mask).bit_length() - 1

    def spread(own, line, around):
        blocks = [own]
        for mask in range(1, vocab_size):
            bit = 1 if around and mask & 3 == 3 and mask > 3 else lowest(mask)
            block = blocks[mask ^ (1 << bit)]
            if bit == 0:
                block = tie(block, line[-3])
            blocks.append(swap(block, bit))
            if bit == 0:
                line.append(blocks[-1])
        return blocks

    def reduce_blocks(parts):
        terms, line = list(parts), []
        for mask in range(vocab_size - 1, 0, -1):
            bit = lowest(mask)
            block = terms[mask].astype(wire)
            if bit == 0 and len(line) > 1:
                block = tie(block, line[-2])
            block = swap(block, bit)
            if bit == 0:
                line.append(block)
            terms[mask ^ (1 << bit)] = terms[mask ^ (1 << bit)] + block.astype(jnp.float32)
        return terms[0], line

    def body(teacher_rows, owner, counts, proj_weight, student_hidden, head_weight, targets):
        teach_rows = teacher_rows.shape[0]
        slab_rows = targets.shape[0]
        vocab_dev = head_weight.shape[1]
        blk = slab_rows // vocab_size
        chunk = min(slab_rows, 32)
        me = lax.axis_index("vocab")
        core = lax.axis_index("seq")
        place = jnp.stack([me, core]).astype(jnp.int32)

        def in_order(vec):
            grid = vec.reshape((2,) * bits + (blk,))
            for bit in range(bits):
                grid = jnp.where((me >> bit) & 1 == 1, jnp.flip(grid, bits - 1 - bit), grid)
            return grid.reshape(slab_rows)

        def turned(block):
            return jnp.where(core == 1, jnp.roll(block, block.shape[1] // 2, axis=1), block)

        def as_pieces(blocks):
            return blocks if blk % 16 == 0 else [jnp.concatenate(blocks, axis=0)]

        heads = (head_weight, lax.ppermute(head_weight, "seq", [(0, 1), (1, 0)]))

        spot = lax.iota(jnp.int32, slab_rows)
        row_id = ((spot // blk) ^ me) * blk + spot % blk
        alive = lax.iota(jnp.int32, teach_rows) < counts[0]
        member = (owner[None, :] == row_id[:, None]) & alive[None, :]
        parts = project(member.astype(jnp.bfloat16), teacher_rows, proj_weight, vocab_size, 512 if student_hidden.shape[1] % 512 == 0 else student_hidden.shape[1])
        projected_own, line = reduce_blocks(parts)
        hidden = spread(tie(turned(student_hidden), parts[-1]), line, True)
        projected = spread(turned(projected_own.astype(jnp.bfloat16)), line, False)

        column = (in_order(targets) - me * vocab_dev)[:, None]
        logit_stud, scaled_stud, stats_stud, head = student_logits(as_pieces(hidden), heads, column, 256, chunk)
        scaled_teach, stats = teacher_logits(as_pieces(projected), head, logit_stud, stats_stud, 1024, chunk)
        tables = [stats]
        for mask in range(1, vocab_size):
            far, near = mask & ~3, mask & 3
            tables.append(trade(tables[far], near) if near else trade(stats, far))
        loss, *terms = gradient(place, tables, scaled_teach, scaled_stud, column, head, bits, chunk)
        return (loss[0], turned(reduce_blocks(terms)[0].astype(jnp.bfloat16)))

    return body


def solution(mesh):
    return jax.shard_map(
        make_body(mesh.shape["vocab"]),
        mesh=mesh,
        in_specs=(
            P(("groups", "seq"), "vocab"),
            P(("groups", "seq")),
            P(("groups", "seq")),
            P("vocab", None),
            P(("groups", "seq", "vocab"), None),
            P("seq", "vocab"),
            P(("groups", "seq")),
        ),
        out_specs=(P(("groups", "seq")), P(("groups", "seq", "vocab"), None)),
        check_vma=False,
    )
```

```python
import functools

import jax
import jax.numpy as jnp
from jax import lax
from jax.experimental import pallas as pl
from jax.experimental.pallas import tpu as pltpu
from jax.sharding import PartitionSpec as P

loss_scale = 64.0
wire = jnp.float16
lanes = 128
vmem_bytes = 12 * 1024 * 1024
project_bytes = 50 * 1024 * 1024

in_vmem = pl.BlockSpec(memory_space=pltpu.VMEM)
in_smem = pl.BlockSpec(memory_space=pltpu.SMEM)
in_place = pl.BlockSpec(memory_space=pl.ANY)


def cuts(total, step):
    return [(start, min(step, total - start)) for start in range(0, total, step)]


def project_kernel(count, step, member_ref, teacher_ref, weight_ref, *rest):
    outs, (teacher, weight, aligned, sems) = rest[:count], rest[count:]
    blk = outs[0].shape[0]
    parts = cuts(weight.shape[1], step)
    first = pltpu.make_async_copy(teacher_ref, teacher, sems.at[len(parts)])
    first.start()
    for index, (start, size) in enumerate(parts):
        at = pl.ds(start, size)
        pltpu.make_async_copy(weight_ref.at[:, at], weight.at[:, at], sems.at[index]).start()
    member = member_ref[...]
    sizes = jnp.sum(member.astype(jnp.float32), axis=1, keepdims=True)
    first.wait()
    summed = jnp.dot(member, teacher[...], preferred_element_type=jnp.float32)
    aligned[...] = (summed / sizes).astype(jnp.bfloat16)

    def one(index, carry):
        at = pl.ds(pl.multiple_of(index * step, step), step)
        pltpu.make_async_copy(weight_ref.at[:, at], weight.at[:, at], sems.at[index]).wait()
        product = jnp.dot(aligned[...], weight[:, at], preferred_element_type=jnp.float32)
        for piece, out in enumerate(outs):
            out[:, at] = product[piece * blk : (piece + 1) * blk]
        return carry

    lax.fori_loop(0, len(parts), one, 0)


def project(member, teacher_rows, proj_weight, count, step):
    slab_rows, (depth, width) = member.shape[0], proj_weight.shape
    blk = slab_rows // count
    return pl.pallas_call(
        functools.partial(project_kernel, count, step),
        in_specs=[in_vmem, in_place, in_place],
        out_specs=[in_vmem] * count,
        out_shape=[jax.ShapeDtypeStruct((blk, width), jnp.float32)] * count,
        scratch_shapes=[
            pltpu.VMEM(teacher_rows.shape, jnp.bfloat16),
            pltpu.VMEM(proj_weight.shape, jnp.bfloat16),
            pltpu.VMEM((slab_rows, depth), jnp.bfloat16),
            pltpu.SemaphoreType.DMA((len(cuts(width, step)) + 1,)),
        ],
        compiler_params=pltpu.CompilerParams(vmem_limit_bytes=project_bytes),
        cost_estimate=pl.CostEstimate(
            flops=2 * slab_rows * depth * (width + teacher_rows.shape[0]),
            bytes_accessed=2 * depth * (width + teacher_rows.shape[0]) + 4 * slab_rows * width,
            transcendentals=0,
        ),
    )(member, teacher_rows, proj_weight)


class Fetch:
    def __init__(self, sems):
        self.sems, self.used = sems, 0

    def start(self, source, target):
        copy = pltpu.make_async_copy(source, target, self.sems.at[self.used])
        copy.start()
        self.used += 1
        return copy


def multiply(read_rows, head, logit_ref, highest, step, ready=None):
    total = head.shape[1]
    highest[...] = jnp.full(highest.shape, -jnp.inf, jnp.float32)

    def one(index, start, size):
        at = pl.ds(start, size)
        if ready is not None:
            ready(index, at)
        part = jnp.dot(read_rows(), head[:, at], preferred_element_type=jnp.float32)
        logit_ref[:, at] = part
        top = part[:, :lanes]
        for lane in range(lanes, size, lanes):
            top = jnp.maximum(top, part[:, lane : lane + lanes])
        highest[...] = jnp.maximum(highest[...], top)

    def body(index, carry):
        one(index, pl.multiple_of(index * step, step), step)
        return carry

    full = total // step
    lax.fori_loop(0, full, body, 0)
    if total % step:
        one(full, full * step, total % step)


def as_columns(first, second, third):
    lane = lax.broadcasted_iota(jnp.int32, (first.shape[0], lanes), 1)
    return jnp.where(lane == 0, first, jnp.where(lane == 1, second, jnp.where(lane == 2, third, 0.0)))


def student_kernel(count, step, chunk, *refs):
    pieces, heads = refs[:count], refs[count : count + 2]
    column_ref, logit_ref, scaled_ref, stats_ref, head = refs[count + 2 : count + 7]
    held, highest, table, sems = refs[count + 7 :]
    depth, total = heads[0].shape
    blk = pieces[0].shape[0]
    fetch = Fetch(sems)
    waits = [fetch.start(piece, held.at[pl.ds(i * blk, blk)]) for i, piece in enumerate(pieces)]
    first = fetch.used

    def columns(half, at):
        return heads[half].at[:, at], head.at[pl.ds(half * depth, depth), at]

    for start, size in cuts(total, step):
        for half in range(2):
            fetch.start(*columns(half, pl.ds(start, size)))

    def ready(index, at):
        for half in range(2):
            pltpu.make_async_copy(*columns(half, at), sems.at[first + 2 * index + half]).wait()

    for wait in waits:
        wait.wait()
    multiply(lambda: held[...], head, logit_ref, highest, step, ready)

    def one(part, carry):
        rows = pl.ds(pl.multiple_of(part * chunk, chunk), chunk)
        logit = logit_ref[rows, :]
        top = jnp.max(highest[rows, :], axis=1, keepdims=True)
        scaled = jnp.exp(logit - top)
        hit = lax.broadcasted_iota(jnp.int32, logit.shape, 1) == column_ref[rows, :]
        picked = jnp.sum(jnp.where(hit, logit, 0.0), axis=1, keepdims=True)
        scaled_ref[rows, :] = scaled
        table[rows, :] = as_columns(top, jnp.sum(scaled, axis=1, keepdims=True), picked)
        return carry

    lax.fori_loop(0, logit_ref.shape[0] // chunk, one, 0)
    stats_ref[...] = table[...].T[0:8]


def teacher_kernel(count, step, chunk, *refs):
    pieces = refs[:count]
    head, stud_logit_ref, stud_ref, scaled_ref, stats_ref, highest, table = refs[count:]

    def read_rows():
        return jnp.concatenate([ref[...] for ref in pieces], axis=0) if count > 1 else pieces[0][...]

    multiply(read_rows, head, scaled_ref, highest, step)

    def one(part, carry):
        rows = pl.ds(pl.multiple_of(part * chunk, chunk), chunk)
        logit = scaled_ref[rows, :]
        top = jnp.max(highest[rows, :], axis=1, keepdims=True)
        scaled = jnp.exp(logit - top)
        gap = jnp.sum(scaled * (logit - stud_logit_ref[rows, :]), axis=1, keepdims=True)
        scaled_ref[rows, :] = scaled
        table[rows, :] = as_columns(top, jnp.sum(scaled, axis=1, keepdims=True), gap)
        return carry

    lax.fori_loop(0, scaled_ref.shape[0] // chunk, one, 0)
    teach = table[...].T[0:8]
    row = lax.broadcasted_iota(jnp.int32, teach.shape, 0)
    stats_ref[...] = jnp.where(row < 4, teach, pltpu.roll(stud_ref[...], 4, 0))


def head_cost(rows, head):
    depth, vocab_dev = head.shape
    return pl.CostEstimate(
        flops=2 * rows * depth * vocab_dev,
        bytes_accessed=2 * depth * vocab_dev + 12 * rows * vocab_dev,
        transcendentals=rows * vocab_dev,
    )


def student_logits(pieces, heads, column, step, chunk):
    rows, (depth, vocab_dev) = column.shape[0], heads[0].shape
    wide = (rows, vocab_dev)
    return pl.pallas_call(
        functools.partial(student_kernel, len(pieces), step, chunk),
        in_specs=[in_place] * (len(pieces) + 2) + [in_vmem],
        out_specs=[in_vmem] * 4,
        out_shape=[
            jax.ShapeDtypeStruct(wide, jnp.float32),
            jax.ShapeDtypeStruct(wide, jnp.float32),
            jax.ShapeDtypeStruct((8, rows), jnp.float32),
            jax.ShapeDtypeStruct((2 * depth, vocab_dev), jnp.bfloat16),
        ],
        scratch_shapes=[
            pltpu.VMEM((rows, 2 * depth), jnp.bfloat16),
            pltpu.VMEM((rows, lanes), jnp.float32),
            pltpu.VMEM((rows, lanes), jnp.float32),
            pltpu.SemaphoreType.DMA((len(pieces) + 2 * len(cuts(vocab_dev, step)),)),
        ],
        compiler_params=pltpu.CompilerParams(vmem_limit_bytes=vmem_bytes),
        cost_estimate=head_cost(rows, heads[0]),
    )(*pieces, *heads, column)


def teacher_logits(pieces, head, logit_stud, stats_stud, step, chunk):
    wide = logit_stud.shape
    return pl.pallas_call(
        functools.partial(teacher_kernel, len(pieces), step, chunk),
        in_specs=[in_vmem] * (len(pieces) + 3),
        out_specs=[in_vmem] * 2,
        out_shape=[
            jax.ShapeDtypeStruct(wide, jnp.float32),
            jax.ShapeDtypeStruct((8, wide[0]), jnp.float32),
        ],
        scratch_shapes=[pltpu.VMEM((wide[0], lanes), jnp.float32)] * 2,
        compiler_params=pltpu.CompilerParams(vmem_limit_bytes=vmem_bytes),
        cost_estimate=head_cost(wide[0], head),
    )(*pieces, head, logit_stud, stats_stud)


def swapped(values, distance):
    total = values.shape[1]
    lane = lax.broadcasted_iota(jnp.int32, values.shape, 1)
    return jnp.where(
        (lane & distance) != 0, pltpu.roll(values, distance, 1), pltpu.roll(values, total - distance, 1)
    )


def gradient_kernel(bits, step, chunk, place_ref, *refs):
    count = 1 << bits
    tables, refs = refs[:count], refs[count:]
    teach_ref, stud_ref, column_ref, head, loss_ref = refs[:5]
    outs = refs[5 : count + 5]
    entries, upstream, factors = refs[count + 5 :]
    rows = upstream.shape[0]
    blk = rows // count
    me = place_ref[0]
    for mask in range(count):
        values = tables[mask][...]
        for bit in range(bits):
            if mask >> bit & 1:
                values = swapped(values, blk << bit)
        entries[me ^ mask] = values
    every = entries[...]
    top_teach = jnp.max(every[:, 0:1], axis=0)
    top_stud = jnp.max(every[:, 4:5], axis=0)
    weight = jnp.exp(every[:, 0:1] - top_teach)
    total_teach = jnp.sum(weight * every[:, 1:2], axis=0)
    total_stud = jnp.sum(jnp.exp(every[:, 4:5] - top_stud) * every[:, 5:6], axis=0)
    lse_teach = top_teach + jnp.log(total_teach)
    lse_stud = top_stud + jnp.log(total_stud)
    gap = jnp.sum(weight * every[:, 2:3], axis=0) / total_teach
    loss = gap - lse_teach + 2.0 * lse_stud - jnp.sum(every[:, 6:7], axis=0)
    loss = jnp.broadcast_to(loss, loss_ref.shape)
    for bit in range(bits):
        loss = jnp.where(((me >> bit) & 1) == 1, swapped(loss, blk << bit), loss)
    loss_ref[...] = loss
    own = tables[0][...]
    scale_teach = -loss_scale * jnp.exp(own[0:1] - lse_teach)
    scale_stud = 2.0 * loss_scale * jnp.exp(own[4:5] - lse_stud)
    line = lax.broadcasted_iota(jnp.int32, (lanes, rows), 0)
    factors[...] = jnp.where(line == 0, scale_teach, scale_stud).T

    def one(part, carry):
        at = pl.ds(pl.multiple_of(part * chunk, chunk), chunk)
        hit = lax.broadcasted_iota(jnp.int32, (chunk, teach_ref.shape[1]), 1) == column_ref[at, :]
        both = teach_ref[at, :] * factors[at, 0:1] + stud_ref[at, :] * factors[at, 1:2]
        upstream[at, :] = jnp.where(hit, both - loss_scale, both).astype(jnp.bfloat16)
        return carry

    lax.fori_loop(0, rows // chunk, one, 0)

    def two(index, carry):
        at = pl.ds(pl.multiple_of(index * step, step), step)
        product = lax.dot_general(
            upstream[...], head[at, :], (((1,), (1,)), ((), ())), preferred_element_type=jnp.float32
        )
        for piece, out in enumerate(outs):
            out[:, at] = product[piece * blk : (piece + 1) * blk]
        return carry

    lax.fori_loop(0, head.shape[0] // step, two, 0)


def gradient(place, tables, scaled_teach, scaled_stud, column, head, bits, chunk):
    rows, vocab_dev = scaled_teach.shape
    count, width = 1 << bits, head.shape[0]
    step = 512 if width % 512 == 0 else width
    return pl.pallas_call(
        functools.partial(gradient_kernel, bits, step, chunk),
        in_specs=[in_smem] + [in_vmem] * (count + 4),
        out_specs=[in_vmem] * (count + 1),
        out_shape=[jax.ShapeDtypeStruct((8, rows), jnp.float32)]
        + [jax.ShapeDtypeStruct((rows // count, width), jnp.float32)] * count,
        scratch_shapes=[
            pltpu.VMEM((count, 8, rows), jnp.float32),
            pltpu.VMEM((rows, vocab_dev), jnp.bfloat16),
            pltpu.VMEM((rows, lanes), jnp.float32),
        ],
        compiler_params=pltpu.CompilerParams(vmem_limit_bytes=vmem_bytes),
        cost_estimate=head_cost(rows, head),
    )(place, *tables, scaled_teach, scaled_stud, column, head)


def tie(block, *others):
    return lax.optimization_barrier((block, *others))[0]


def make_body(vocab_size):
    bits = vocab_size.bit_length() - 1
    assert vocab_size == 1 << bits

    def trade(block, mask):
        return lax.ppermute(block, "vocab", [(at, at ^ mask) for at in range(vocab_size)])

    def swap(block, bit):
        return trade(block, 1 << bit)

    def lowest(mask):
        return (mask & -mask).bit_length() - 1

    def spread(own, line):
        blocks = [own]
        for mask in range(1, vocab_size):
            bit = lowest(mask)
            block = blocks[mask ^ (1 << bit)]
            if bit == 0:
                block = tie(block, line[-3])
            blocks.append(swap(block, bit))
            if bit == 0:
                line.append(blocks[-1])
        return blocks

    def reduce_blocks(parts):
        terms, line = list(parts), []
        for mask in range(vocab_size - 1, 0, -1):
            bit = lowest(mask)
            block = terms[mask].astype(wire)
            if bit == 0 and len(line) > 1:
                block = tie(block, line[-2])
            block = swap(block, bit)
            if bit == 0:
                line.append(block)
            terms[mask ^ (1 << bit)] = terms[mask ^ (1 << bit)] + block.astype(jnp.float32)
        return terms[0], line

    def body(teacher_rows, owner, counts, proj_weight, student_hidden, head_weight, targets):
        teach_rows = teacher_rows.shape[0]
        slab_rows = targets.shape[0]
        vocab_dev = head_weight.shape[1]
        blk = slab_rows // vocab_size
        chunk = min(slab_rows, 32)
        me = lax.axis_index("vocab")
        core = lax.axis_index("seq")
        place = jnp.stack([me, core]).astype(jnp.int32)

        def in_order(vec):
            grid = vec.reshape((2,) * bits + (blk,))
            for bit in range(bits):
                grid = jnp.where((me >> bit) & 1 == 1, jnp.flip(grid, bits - 1 - bit), grid)
            return grid.reshape(slab_rows)

        def turned(block):
            return jnp.where(core == 1, jnp.roll(block, block.shape[1] // 2, axis=1), block)

        def as_pieces(blocks):
            return blocks if blk % 16 == 0 else [jnp.concatenate(blocks, axis=0)]

        heads = (head_weight, lax.ppermute(head_weight, "seq", [(0, 1), (1, 0)]))

        spot = lax.iota(jnp.int32, slab_rows)
        row_id = ((spot // blk) ^ me) * blk + spot % blk
        alive = lax.iota(jnp.int32, teach_rows) < counts[0]
        member = (owner[None, :] == row_id[:, None]) & alive[None, :]
        parts = project(member.astype(jnp.bfloat16), teacher_rows, proj_weight, vocab_size, 512 if student_hidden.shape[1] % 512 == 0 else student_hidden.shape[1])
        projected_own, line = reduce_blocks(parts)
        hidden = spread(tie(turned(student_hidden), parts[-1]), line)
        projected = spread(turned(projected_own.astype(jnp.bfloat16)), line)

        column = (in_order(targets) - me * vocab_dev)[:, None]
        logit_stud, scaled_stud, stats_stud, head = student_logits(as_pieces(hidden), heads, column, 512, chunk)
        scaled_teach, stats = teacher_logits(as_pieces(projected), head, logit_stud, stats_stud, 1024, chunk)
        tables = [stats]
        for mask in range(1, vocab_size):
            far, near = mask & ~3, mask & 3
            tables.append(trade(tables[far], near) if near else trade(stats, far))
        loss, *terms = gradient(place, tables, scaled_teach, scaled_stud, column, head, bits, chunk)
        return (loss[0], turned(reduce_blocks(terms)[0].astype(jnp.bfloat16)))

    return body


def solution(mesh):
    return jax.shard_map(
        make_body(mesh.shape["vocab"]),
        mesh=mesh,
        in_specs=(
            P(("groups", "seq"), "vocab"),
            P(("groups", "seq")),
            P(("groups", "seq")),
            P("vocab", None),
            P(("groups", "seq", "vocab"), None),
            P("seq", "vocab"),
            P(("groups", "seq")),
        ),
        out_specs=(P(("groups", "seq")), P(("groups", "seq", "vocab"), None)),
        check_vma=False,
    )
```

```python
import functools

import jax
import jax.numpy as jnp
from jax import lax
from jax.experimental import pallas as pl
from jax.experimental.pallas import tpu as pltpu
from jax.sharding import PartitionSpec as P

loss_scale = 64.0
wire = jnp.float16
lanes = 128
vmem_bytes = 12 * 1024 * 1024
project_bytes = 50 * 1024 * 1024

in_vmem = pl.BlockSpec(memory_space=pltpu.VMEM)
in_smem = pl.BlockSpec(memory_space=pltpu.SMEM)
in_place = pl.BlockSpec(memory_space=pl.ANY)


def cuts(total, step):
    return [(start, min(step, total - start)) for start in range(0, total, step)]


def project_kernel(count, step, member_ref, teacher_ref, weight_ref, *rest):
    outs, (teacher, weight, aligned, sems) = rest[:count], rest[count:]
    blk = outs[0].shape[0]
    parts = cuts(weight.shape[1], step)
    first = pltpu.make_async_copy(teacher_ref, teacher, sems.at[len(parts)])
    first.start()
    for index, (start, size) in enumerate(parts):
        at = pl.ds(start, size)
        pltpu.make_async_copy(weight_ref.at[:, at], weight.at[:, at], sems.at[index]).start()
    member = member_ref[...]
    sizes = jnp.sum(member.astype(jnp.float32), axis=1, keepdims=True)
    first.wait()
    summed = jnp.dot(member, teacher[...], preferred_element_type=jnp.float32)
    aligned[...] = (summed / sizes).astype(jnp.bfloat16)

    def one(index, carry):
        at = pl.ds(pl.multiple_of(index * step, step), step)
        pltpu.make_async_copy(weight_ref.at[:, at], weight.at[:, at], sems.at[index]).wait()
        product = jnp.dot(aligned[...], weight[:, at], preferred_element_type=jnp.float32)
        for piece, out in enumerate(outs):
            out[:, at] = product[piece * blk : (piece + 1) * blk]
        return carry

    lax.fori_loop(0, len(parts), one, 0)


def project(member, teacher_rows, proj_weight, count, step):
    slab_rows, (depth, width) = member.shape[0], proj_weight.shape
    blk = slab_rows // count
    return pl.pallas_call(
        functools.partial(project_kernel, count, step),
        in_specs=[in_vmem, in_place, in_place],
        out_specs=[in_vmem] * count,
        out_shape=[jax.ShapeDtypeStruct((blk, width), jnp.float32)] * count,
        scratch_shapes=[
            pltpu.VMEM(teacher_rows.shape, jnp.bfloat16),
            pltpu.VMEM(proj_weight.shape, jnp.bfloat16),
            pltpu.VMEM((slab_rows, depth), jnp.bfloat16),
            pltpu.SemaphoreType.DMA((len(cuts(width, step)) + 1,)),
        ],
        compiler_params=pltpu.CompilerParams(vmem_limit_bytes=project_bytes),
        cost_estimate=pl.CostEstimate(
            flops=2 * slab_rows * depth * (width + teacher_rows.shape[0]),
            bytes_accessed=2 * depth * (width + teacher_rows.shape[0]) + 4 * slab_rows * width,
            transcendentals=0,
        ),
    )(member, teacher_rows, proj_weight)


class Fetch:
    def __init__(self, sems):
        self.sems, self.used = sems, 0

    def start(self, source, target):
        copy = pltpu.make_async_copy(source, target, self.sems.at[self.used])
        copy.start()
        self.used += 1
        return copy


def multiply(read_rows, head, logit_ref, highest, step, ready=None):
    total = head.shape[1]
    highest[...] = jnp.full(highest.shape, -jnp.inf, jnp.float32)

    def one(index, start, size):
        at = pl.ds(start, size)
        if ready is not None:
            ready(index, at)
        part = jnp.dot(read_rows(), head[:, at], preferred_element_type=jnp.float32)
        logit_ref[:, at] = part
        top = part[:, :lanes]
        for lane in range(lanes, size, lanes):
            top = jnp.maximum(top, part[:, lane : lane + lanes])
        highest[...] = jnp.maximum(highest[...], top)

    def body(index, carry):
        one(index, pl.multiple_of(index * step, step), step)
        return carry

    full = total // step
    lax.fori_loop(0, full, body, 0)
    if total % step:
        one(full, full * step, total % step)


def as_columns(first, second, third):
    lane = lax.broadcasted_iota(jnp.int32, (first.shape[0], lanes), 1)
    return jnp.where(lane == 0, first, jnp.where(lane == 1, second, jnp.where(lane == 2, third, 0.0)))


def student_kernel(count, step, chunk, *refs):
    pieces, heads = refs[:count], refs[count : count + 2]
    column_ref, logit_ref, scaled_ref, stats_ref, head = refs[count + 2 : count + 7]
    held, highest, table, sems = refs[count + 7 :]
    depth, total = heads[0].shape
    blk = pieces[0].shape[0]
    fetch = Fetch(sems)
    waits = [fetch.start(piece, held.at[pl.ds(i * blk, blk)]) for i, piece in enumerate(pieces)]
    first = fetch.used

    def columns(half, at):
        return heads[half].at[:, at], head.at[pl.ds(half * depth, depth), at]

    for start, size in cuts(total, step):
        for half in range(2):
            fetch.start(*columns(half, pl.ds(start, size)))

    def ready(index, at):
        for half in range(2):
            pltpu.make_async_copy(*columns(half, at), sems.at[first + 2 * index + half]).wait()

    for wait in waits:
        wait.wait()
    multiply(lambda: held[...], head, logit_ref, highest, step, ready)

    def one(part, carry):
        rows = pl.ds(pl.multiple_of(part * chunk, chunk), chunk)
        logit = logit_ref[rows, :]
        top = jnp.max(highest[rows, :], axis=1, keepdims=True)
        scaled = jnp.exp(logit - top)
        hit = lax.broadcasted_iota(jnp.int32, logit.shape, 1) == column_ref[rows, :]
        picked = jnp.sum(jnp.where(hit, logit, 0.0), axis=1, keepdims=True)
        scaled_ref[rows, :] = scaled
        table[rows, :] = as_columns(top, jnp.sum(scaled, axis=1, keepdims=True), picked)
        return carry

    lax.fori_loop(0, logit_ref.shape[0] // chunk, one, 0)
    stats_ref[...] = table[...].T[0:8]


def teacher_kernel(count, step, chunk, *refs):
    pieces = refs[:count]
    head, stud_logit_ref, stud_ref, scaled_ref, stats_ref, highest, table = refs[count:]

    def read_rows():
        return jnp.concatenate([ref[...] for ref in pieces], axis=0) if count > 1 else pieces[0][...]

    multiply(read_rows, head, scaled_ref, highest, step)

    def one(part, carry):
        rows = pl.ds(pl.multiple_of(part * chunk, chunk), chunk)
        logit = scaled_ref[rows, :]
        top = jnp.max(highest[rows, :], axis=1, keepdims=True)
        scaled = jnp.exp(logit - top)
        gap = jnp.sum(scaled * (logit - stud_logit_ref[rows, :]), axis=1, keepdims=True)
        scaled_ref[rows, :] = scaled
        table[rows, :] = as_columns(top, jnp.sum(scaled, axis=1, keepdims=True), gap)
        return carry

    lax.fori_loop(0, scaled_ref.shape[0] // chunk, one, 0)
    teach = table[...].T[0:8]
    row = lax.broadcasted_iota(jnp.int32, teach.shape, 0)
    stats_ref[...] = jnp.where(row < 4, teach, pltpu.roll(stud_ref[...], 4, 0))


def head_cost(rows, head):
    depth, vocab_dev = head.shape
    return pl.CostEstimate(
        flops=2 * rows * depth * vocab_dev,
        bytes_accessed=2 * depth * vocab_dev + 12 * rows * vocab_dev,
        transcendentals=rows * vocab_dev,
    )


def student_logits(pieces, heads, column, step, chunk):
    rows, (depth, vocab_dev) = column.shape[0], heads[0].shape
    wide = (rows, vocab_dev)
    return pl.pallas_call(
        functools.partial(student_kernel, len(pieces), step, chunk),
        in_specs=[in_place] * (len(pieces) + 2) + [in_vmem],
        out_specs=[in_vmem] * 4,
        out_shape=[
            jax.ShapeDtypeStruct(wide, jnp.float32),
            jax.ShapeDtypeStruct(wide, jnp.float32),
            jax.ShapeDtypeStruct((8, rows), jnp.float32),
            jax.ShapeDtypeStruct((2 * depth, vocab_dev), jnp.bfloat16),
        ],
        scratch_shapes=[
            pltpu.VMEM((rows, 2 * depth), jnp.bfloat16),
            pltpu.VMEM((rows, lanes), jnp.float32),
            pltpu.VMEM((rows, lanes), jnp.float32),
            pltpu.SemaphoreType.DMA((len(pieces) + 2 * len(cuts(vocab_dev, step)),)),
        ],
        compiler_params=pltpu.CompilerParams(vmem_limit_bytes=vmem_bytes),
        cost_estimate=head_cost(rows, heads[0]),
    )(*pieces, *heads, column)


def teacher_logits(pieces, head, logit_stud, stats_stud, step, chunk):
    wide = logit_stud.shape
    return pl.pallas_call(
        functools.partial(teacher_kernel, len(pieces), step, chunk),
        in_specs=[in_vmem] * (len(pieces) + 3),
        out_specs=[in_vmem] * 2,
        out_shape=[
            jax.ShapeDtypeStruct(wide, jnp.float32),
            jax.ShapeDtypeStruct((8, wide[0]), jnp.float32),
        ],
        scratch_shapes=[pltpu.VMEM((wide[0], lanes), jnp.float32)] * 2,
        compiler_params=pltpu.CompilerParams(vmem_limit_bytes=vmem_bytes),
        cost_estimate=head_cost(wide[0], head),
    )(*pieces, head, logit_stud, stats_stud)


def swapped(values, distance):
    total = values.shape[1]
    lane = lax.broadcasted_iota(jnp.int32, values.shape, 1)
    return jnp.where(
        (lane & distance) != 0, pltpu.roll(values, distance, 1), pltpu.roll(values, total - distance, 1)
    )


def gradient_kernel(bits, step, chunk, place_ref, *refs):
    count = 1 << bits
    tables, refs = refs[:count], refs[count:]
    teach_ref, stud_ref, column_ref, head, loss_ref = refs[:5]
    outs = refs[5 : count + 5]
    entries, upstream, factors = refs[count + 5 :]
    rows = upstream.shape[0]
    blk = rows // count
    me = place_ref[0]
    for mask in range(count):
        values = tables[mask][...]
        for bit in range(bits):
            if mask >> bit & 1:
                values = swapped(values, blk << bit)
        entries[me ^ mask] = values
    every = entries[...]
    top_teach = jnp.max(every[:, 0:1], axis=0)
    top_stud = jnp.max(every[:, 4:5], axis=0)
    weight = jnp.exp(every[:, 0:1] - top_teach)
    total_teach = jnp.sum(weight * every[:, 1:2], axis=0)
    total_stud = jnp.sum(jnp.exp(every[:, 4:5] - top_stud) * every[:, 5:6], axis=0)
    lse_teach = top_teach + jnp.log(total_teach)
    lse_stud = top_stud + jnp.log(total_stud)
    gap = jnp.sum(weight * every[:, 2:3], axis=0) / total_teach
    loss = gap - lse_teach + 2.0 * lse_stud - jnp.sum(every[:, 6:7], axis=0)
    loss = jnp.broadcast_to(loss, loss_ref.shape)
    for bit in range(bits):
        loss = jnp.where(((me >> bit) & 1) == 1, swapped(loss, blk << bit), loss)
    loss_ref[...] = loss
    own = tables[0][...]
    scale_teach = -loss_scale * jnp.exp(own[0:1] - lse_teach)
    scale_stud = 2.0 * loss_scale * jnp.exp(own[4:5] - lse_stud)
    line = lax.broadcasted_iota(jnp.int32, (lanes, rows), 0)
    factors[...] = jnp.where(line == 0, scale_teach, scale_stud).T

    def one(part, carry):
        at = pl.ds(pl.multiple_of(part * chunk, chunk), chunk)
        hit = lax.broadcasted_iota(jnp.int32, (chunk, teach_ref.shape[1]), 1) == column_ref[at, :]
        both = teach_ref[at, :] * factors[at, 0:1] + stud_ref[at, :] * factors[at, 1:2]
        upstream[at, :] = jnp.where(hit, both - loss_scale, both).astype(jnp.bfloat16)
        return carry

    lax.fori_loop(0, rows // chunk, one, 0)

    def two(index, carry):
        at = pl.ds(pl.multiple_of(index * step, step), step)
        product = lax.dot_general(
            upstream[...], head[at, :], (((1,), (1,)), ((), ())), preferred_element_type=jnp.float32
        )
        for piece, out in enumerate(outs):
            out[:, at] = product[piece * blk : (piece + 1) * blk]
        return carry

    lax.fori_loop(0, head.shape[0] // step, two, 0)


def gradient(place, tables, scaled_teach, scaled_stud, column, head, bits, chunk):
    rows, vocab_dev = scaled_teach.shape
    count, width = 1 << bits, head.shape[0]
    step = 512 if width % 512 == 0 else width
    return pl.pallas_call(
        functools.partial(gradient_kernel, bits, step, chunk),
        in_specs=[in_smem] + [in_vmem] * (count + 4),
        out_specs=[in_vmem] * (count + 1),
        out_shape=[jax.ShapeDtypeStruct((8, rows), jnp.float32)]
        + [jax.ShapeDtypeStruct((rows // count, width), jnp.float32)] * count,
        scratch_shapes=[
            pltpu.VMEM((count, 8, rows), jnp.float32),
            pltpu.VMEM((rows, vocab_dev), jnp.bfloat16),
            pltpu.VMEM((rows, lanes), jnp.float32),
        ],
        compiler_params=pltpu.CompilerParams(vmem_limit_bytes=vmem_bytes),
        cost_estimate=head_cost(rows, head),
    )(place, *tables, scaled_teach, scaled_stud, column, head)


def tie(block, *others):
    return lax.optimization_barrier((block, *others))[0]


def make_body(vocab_size):
    bits = vocab_size.bit_length() - 1
    assert vocab_size == 1 << bits

    def trade(block, mask):
        return lax.ppermute(block, "vocab", [(at, at ^ mask) for at in range(vocab_size)])

    def swap(block, bit):
        return trade(block, 1 << bit)

    def lowest(mask):
        return (mask & -mask).bit_length() - 1

    def spread(own, line):
        blocks = [own]
        for mask in range(1, vocab_size):
            bit = lowest(mask)
            block = blocks[mask ^ (1 << bit)]
            if bit == 0:
                block = tie(block, line[-3])
            blocks.append(swap(block, bit))
            if bit == 0:
                line.append(blocks[-1])
        return blocks

    def reduce_blocks(parts):
        terms, line = list(parts), []
        for mask in range(vocab_size - 1, 0, -1):
            bit = lowest(mask)
            block = terms[mask].astype(wire)
            if bit == 0 and len(line) > 1:
                block = tie(block, line[-2])
            block = swap(block, bit)
            if bit == 0:
                line.append(block)
            terms[mask ^ (1 << bit)] = terms[mask ^ (1 << bit)] + block.astype(jnp.float32)
        return terms[0], line

    def body(teacher_rows, owner, counts, proj_weight, student_hidden, head_weight, targets):
        teach_rows = teacher_rows.shape[0]
        slab_rows = targets.shape[0]
        vocab_dev = head_weight.shape[1]
        blk = slab_rows // vocab_size
        chunk = min(slab_rows, 32)
        me = lax.axis_index("vocab")
        core = lax.axis_index("seq")
        place = jnp.stack([me, core]).astype(jnp.int32)

        def in_order(vec):
            grid = vec.reshape((2,) * bits + (blk,))
            for bit in range(bits):
                grid = jnp.where((me >> bit) & 1 == 1, jnp.flip(grid, bits - 1 - bit), grid)
            return grid.reshape(slab_rows)

        def turned(block):
            return jnp.where(core == 1, jnp.roll(block, block.shape[1] // 2, axis=1), block)

        def as_pieces(blocks):
            return blocks if blk % 16 == 0 else [jnp.concatenate(blocks, axis=0)]

        heads = (
            lax.ppermute(head_weight, "seq", [(0, 0), (1, 1)]),
            lax.ppermute(head_weight, "seq", [(0, 1), (1, 0)]),
        )

        spot = lax.iota(jnp.int32, slab_rows)
        row_id = ((spot // blk) ^ me) * blk + spot % blk
        alive = lax.iota(jnp.int32, teach_rows) < counts[0]
        member = (owner[None, :] == row_id[:, None]) & alive[None, :]
        parts = project(member.astype(jnp.bfloat16), teacher_rows, proj_weight, vocab_size, 512 if student_hidden.shape[1] % 512 == 0 else student_hidden.shape[1])
        projected_own, line = reduce_blocks(parts)
        hidden = spread(tie(turned(student_hidden), parts[-1]), line)
        projected = spread(turned(projected_own.astype(jnp.bfloat16)), line)

        column = (in_order(targets) - me * vocab_dev)[:, None]
        logit_stud, scaled_stud, stats_stud, head = student_logits(as_pieces(hidden), heads, column, 512, chunk)
        scaled_teach, stats = teacher_logits(as_pieces(projected), head, logit_stud, stats_stud, 1024, chunk)
        tables = [stats]
        for mask in range(1, vocab_size):
            far, near = mask & ~3, mask & 3
            tables.append(trade(tables[far], near) if near else trade(stats, far))
        loss, *terms = gradient(place, tables, scaled_teach, scaled_stud, column, head, bits, chunk)
        return (loss[0], turned(reduce_blocks(terms)[0].astype(jnp.bfloat16)))

    return body


def solution(mesh):
    return jax.shard_map(
        make_body(mesh.shape["vocab"]),
        mesh=mesh,
        in_specs=(
            P(("groups", "seq"), "vocab"),
            P(("groups", "seq")),
            P(("groups", "seq")),
            P("vocab", None),
            P(("groups", "seq", "vocab"), None),
            P("seq", "vocab"),
            P(("groups", "seq")),
        ),
        out_specs=(P(("groups", "seq")), P(("groups", "seq", "vocab"), None)),
        check_vma=False,
    )
```

```python
import functools

import jax
import jax.numpy as jnp
from jax import lax
from jax.experimental import pallas as pl
from jax.experimental.pallas import tpu as pltpu
from jax.sharding import PartitionSpec as P

loss_scale = 64.0
wire = jnp.float16
lanes = 128
vmem_bytes = 12 * 1024 * 1024
project_bytes = 49 * 1024 * 1024

in_vmem = pl.BlockSpec(memory_space=pltpu.VMEM)
in_smem = pl.BlockSpec(memory_space=pltpu.SMEM)
in_place = pl.BlockSpec(memory_space=pl.ANY)


def cuts(total, step):
    return [(start, min(step, total - start)) for start in range(0, total, step)]


def project_kernel(count, step, place_ref, member_ref, student_ref, teacher_ref, weight_ref, turned_ref, *rest):
    outs, (teacher, weight, aligned, sems) = rest[:count], rest[count:]
    blk = outs[0].shape[0]
    parts = cuts(weight.shape[1], step)
    first = pltpu.make_async_copy(teacher_ref, teacher, sems.at[len(parts)])
    first.start()
    for index, (start, size) in enumerate(parts):
        at = pl.ds(start, size)
        pltpu.make_async_copy(weight_ref.at[:, at], weight.at[:, at], sems.at[index]).start()
    half = student_ref.shape[1] // 2
    odd = place_ref[1] == 1
    low, high = student_ref[:, :half], student_ref[:, half:]
    turned_ref[:, :half] = jnp.where(odd, high, low)
    turned_ref[:, half:] = jnp.where(odd, low, high)
    member = member_ref[...]
    sizes = jnp.sum(member.astype(jnp.float32), axis=1, keepdims=True)
    first.wait()
    summed = jnp.dot(member, teacher[...], preferred_element_type=jnp.float32)
    aligned[...] = (summed / sizes).astype(jnp.bfloat16)

    def one(index, carry):
        at = pl.ds(pl.multiple_of(index * step, step), step)
        pltpu.make_async_copy(weight_ref.at[:, at], weight.at[:, at], sems.at[index]).wait()
        product = jnp.dot(aligned[...], weight[:, at], preferred_element_type=jnp.float32)
        for piece, out in enumerate(outs):
            out[:, at] = product[piece * blk : (piece + 1) * blk]
        return carry

    lax.fori_loop(0, len(parts), one, 0)


def project(place, member, student, teacher_rows, proj_weight, count, step):
    slab_rows, (depth, width) = member.shape[0], proj_weight.shape
    blk = slab_rows // count
    return pl.pallas_call(
        functools.partial(project_kernel, count, step),
        in_specs=[in_smem, in_vmem, in_vmem, in_place, in_place],
        out_specs=[in_vmem] * (count + 1),
        out_shape=[jax.ShapeDtypeStruct(student.shape, jnp.bfloat16)]
        + [jax.ShapeDtypeStruct((blk, width), jnp.float32)] * count,
        scratch_shapes=[
            pltpu.VMEM(teacher_rows.shape, jnp.bfloat16),
            pltpu.VMEM(proj_weight.shape, jnp.bfloat16),
            pltpu.VMEM((slab_rows, depth), jnp.bfloat16),
            pltpu.SemaphoreType.DMA((len(cuts(width, step)) + 1,)),
        ],
        compiler_params=pltpu.CompilerParams(vmem_limit_bytes=project_bytes),
        cost_estimate=pl.CostEstimate(
            flops=2 * slab_rows * depth * (width + teacher_rows.shape[0]),
            bytes_accessed=2 * depth * (width + teacher_rows.shape[0]) + 4 * slab_rows * width,
            transcendentals=0,
        ),
    )(place, member, student, teacher_rows, proj_weight)


class Fetch:
    def __init__(self, sems):
        self.sems, self.used = sems, 0

    def start(self, source, target):
        copy = pltpu.make_async_copy(source, target, self.sems.at[self.used])
        copy.start()
        self.used += 1
        return copy


def multiply(read_rows, head, logit_ref, highest, step, ready=None):
    total = head.shape[1]
    highest[...] = jnp.full(highest.shape, -jnp.inf, jnp.float32)

    def one(index, start, size):
        at = pl.ds(start, size)
        if ready is not None:
            ready(index, at)
        part = jnp.dot(read_rows(), head[:, at], preferred_element_type=jnp.float32)
        logit_ref[:, at] = part
        top = part[:, :lanes]
        for lane in range(lanes, size, lanes):
            top = jnp.maximum(top, part[:, lane : lane + lanes])
        highest[...] = jnp.maximum(highest[...], top)

    def body(index, carry):
        one(index, pl.multiple_of(index * step, step), step)
        return carry

    full = total // step
    lax.fori_loop(0, full, body, 0)
    if total % step:
        one(full, full * step, total % step)


def as_columns(first, second, third):
    lane = lax.broadcasted_iota(jnp.int32, (first.shape[0], lanes), 1)
    return jnp.where(lane == 0, first, jnp.where(lane == 1, second, jnp.where(lane == 2, third, 0.0)))


def student_kernel(count, step, chunk, *refs):
    pieces, heads = refs[:count], refs[count : count + 2]
    column_ref, logit_ref, scaled_ref, stats_ref, head = refs[count + 2 : count + 7]
    held, highest, table, sems = refs[count + 7 :]
    depth, total = heads[0].shape
    blk = pieces[0].shape[0]
    fetch = Fetch(sems)
    waits = [fetch.start(piece, held.at[pl.ds(i * blk, blk)]) for i, piece in enumerate(pieces)]
    first = fetch.used

    def columns(half, at):
        return heads[half].at[:, at], head.at[pl.ds(half * depth, depth), at]

    for start, size in cuts(total, step):
        for half in range(2):
            fetch.start(*columns(half, pl.ds(start, size)))

    def ready(index, at):
        for half in range(2):
            pltpu.make_async_copy(*columns(half, at), sems.at[first + 2 * index + half]).wait()

    for wait in waits:
        wait.wait()
    multiply(lambda: held[...], head, logit_ref, highest, step, ready)

    def one(part, carry):
        rows = pl.ds(pl.multiple_of(part * chunk, chunk), chunk)
        logit = logit_ref[rows, :]
        top = jnp.max(highest[rows, :], axis=1, keepdims=True)
        scaled = jnp.exp(logit - top)
        hit = lax.broadcasted_iota(jnp.int32, logit.shape, 1) == column_ref[rows, :]
        picked = jnp.sum(jnp.where(hit, logit, 0.0), axis=1, keepdims=True)
        scaled_ref[rows, :] = scaled
        table[rows, :] = as_columns(top, jnp.sum(scaled, axis=1, keepdims=True), picked)
        return carry

    lax.fori_loop(0, logit_ref.shape[0] // chunk, one, 0)
    stats_ref[...] = table[...].T[0:8]


def teacher_kernel(count, step, chunk, *refs):
    pieces = refs[:count]
    head, stud_logit_ref, stud_ref, scaled_ref, stats_ref, highest, table = refs[count:]

    def read_rows():
        return jnp.concatenate([ref[...] for ref in pieces], axis=0) if count > 1 else pieces[0][...]

    multiply(read_rows, head, scaled_ref, highest, step)

    def one(part, carry):
        rows = pl.ds(pl.multiple_of(part * chunk, chunk), chunk)
        logit = scaled_ref[rows, :]
        top = jnp.max(highest[rows, :], axis=1, keepdims=True)
        scaled = jnp.exp(logit - top)
        gap = jnp.sum(scaled * (logit - stud_logit_ref[rows, :]), axis=1, keepdims=True)
        scaled_ref[rows, :] = scaled
        table[rows, :] = as_columns(top, jnp.sum(scaled, axis=1, keepdims=True), gap)
        return carry

    lax.fori_loop(0, scaled_ref.shape[0] // chunk, one, 0)
    teach = table[...].T[0:8]
    row = lax.broadcasted_iota(jnp.int32, teach.shape, 0)
    stats_ref[...] = jnp.where(row < 4, teach, pltpu.roll(stud_ref[...], 4, 0))


def head_cost(rows, head):
    depth, vocab_dev = head.shape
    return pl.CostEstimate(
        flops=2 * rows * depth * vocab_dev,
        bytes_accessed=2 * depth * vocab_dev + 12 * rows * vocab_dev,
        transcendentals=rows * vocab_dev,
    )


def student_logits(pieces, heads, column, step, chunk):
    rows, (depth, vocab_dev) = column.shape[0], heads[0].shape
    wide = (rows, vocab_dev)
    return pl.pallas_call(
        functools.partial(student_kernel, len(pieces), step, chunk),
        in_specs=[in_place] * (len(pieces) + 2) + [in_vmem],
        out_specs=[in_vmem] * 4,
        out_shape=[
            jax.ShapeDtypeStruct(wide, jnp.float32),
            jax.ShapeDtypeStruct(wide, jnp.float32),
            jax.ShapeDtypeStruct((8, rows), jnp.float32),
            jax.ShapeDtypeStruct((2 * depth, vocab_dev), jnp.bfloat16),
        ],
        scratch_shapes=[
            pltpu.VMEM((rows, 2 * depth), jnp.bfloat16),
            pltpu.VMEM((rows, lanes), jnp.float32),
            pltpu.VMEM((rows, lanes), jnp.float32),
            pltpu.SemaphoreType.DMA((len(pieces) + 2 * len(cuts(vocab_dev, step)),)),
        ],
        compiler_params=pltpu.CompilerParams(vmem_limit_bytes=vmem_bytes),
        cost_estimate=head_cost(rows, heads[0]),
    )(*pieces, *heads, column)


def teacher_logits(pieces, head, logit_stud, stats_stud, step, chunk):
    wide = logit_stud.shape
    return pl.pallas_call(
        functools.partial(teacher_kernel, len(pieces), step, chunk),
        in_specs=[in_vmem] * (len(pieces) + 3),
        out_specs=[in_vmem] * 2,
        out_shape=[
            jax.ShapeDtypeStruct(wide, jnp.float32),
            jax.ShapeDtypeStruct((8, wide[0]), jnp.float32),
        ],
        scratch_shapes=[pltpu.VMEM((wide[0], lanes), jnp.float32)] * 2,
        compiler_params=pltpu.CompilerParams(vmem_limit_bytes=vmem_bytes),
        cost_estimate=head_cost(wide[0], head),
    )(*pieces, head, logit_stud, stats_stud)


def swapped(values, distance):
    total = values.shape[1]
    lane = lax.broadcasted_iota(jnp.int32, values.shape, 1)
    return jnp.where(
        (lane & distance) != 0, pltpu.roll(values, distance, 1), pltpu.roll(values, total - distance, 1)
    )


def gradient_kernel(bits, step, chunk, place_ref, *refs):
    count = 1 << bits
    tables, refs = refs[:count], refs[count:]
    teach_ref, stud_ref, column_ref, head, loss_ref = refs[:5]
    outs = refs[5 : count + 5]
    entries, upstream, factors = refs[count + 5 :]
    rows = upstream.shape[0]
    blk = rows // count
    me = place_ref[0]
    for mask in range(count):
        values = tables[mask][...]
        for bit in range(bits):
            if mask >> bit & 1:
                values = swapped(values, blk << bit)
        entries[me ^ mask] = values
    every = entries[...]
    top_teach = jnp.max(every[:, 0:1], axis=0)
    top_stud = jnp.max(every[:, 4:5], axis=0)
    weight = jnp.exp(every[:, 0:1] - top_teach)
    total_teach = jnp.sum(weight * every[:, 1:2], axis=0)
    total_stud = jnp.sum(jnp.exp(every[:, 4:5] - top_stud) * every[:, 5:6], axis=0)
    lse_teach = top_teach + jnp.log(total_teach)
    lse_stud = top_stud + jnp.log(total_stud)
    gap = jnp.sum(weight * every[:, 2:3], axis=0) / total_teach
    loss = gap - lse_teach + 2.0 * lse_stud - jnp.sum(every[:, 6:7], axis=0)
    loss = jnp.broadcast_to(loss, loss_ref.shape)
    for bit in range(bits):
        loss = jnp.where(((me >> bit) & 1) == 1, swapped(loss, blk << bit), loss)
    loss_ref[...] = loss
    own = tables[0][...]
    scale_teach = -loss_scale * jnp.exp(own[0:1] - lse_teach)
    scale_stud = 2.0 * loss_scale * jnp.exp(own[4:5] - lse_stud)
    line = lax.broadcasted_iota(jnp.int32, (lanes, rows), 0)
    factors[...] = jnp.where(line == 0, scale_teach, scale_stud).T

    def one(part, carry):
        at = pl.ds(pl.multiple_of(part * chunk, chunk), chunk)
        hit = lax.broadcasted_iota(jnp.int32, (chunk, teach_ref.shape[1]), 1) == column_ref[at, :]
        both = teach_ref[at, :] * factors[at, 0:1] + stud_ref[at, :] * factors[at, 1:2]
        upstream[at, :] = jnp.where(hit, both - loss_scale, both).astype(jnp.bfloat16)
        return carry

    lax.fori_loop(0, rows // chunk, one, 0)

    def two(index, carry):
        at = pl.ds(pl.multiple_of(index * step, step), step)
        product = lax.dot_general(
            upstream[...], head[at, :], (((1,), (1,)), ((), ())), preferred_element_type=jnp.float32
        )
        for piece, out in enumerate(outs):
            out[:, at] = product[piece * blk : (piece + 1) * blk]
        return carry

    lax.fori_loop(0, head.shape[0] // step, two, 0)


def gradient(place, tables, scaled_teach, scaled_stud, column, head, bits, chunk):
    rows, vocab_dev = scaled_teach.shape
    count, width = 1 << bits, head.shape[0]
    step = 512 if width % 512 == 0 else width
    return pl.pallas_call(
        functools.partial(gradient_kernel, bits, step, chunk),
        in_specs=[in_smem] + [in_vmem] * (count + 4),
        out_specs=[in_vmem] * (count + 1),
        out_shape=[jax.ShapeDtypeStruct((8, rows), jnp.float32)]
        + [jax.ShapeDtypeStruct((rows // count, width), jnp.float32)] * count,
        scratch_shapes=[
            pltpu.VMEM((count, 8, rows), jnp.float32),
            pltpu.VMEM((rows, vocab_dev), jnp.bfloat16),
            pltpu.VMEM((rows, lanes), jnp.float32),
        ],
        compiler_params=pltpu.CompilerParams(vmem_limit_bytes=vmem_bytes),
        cost_estimate=head_cost(rows, head),
    )(place, *tables, scaled_teach, scaled_stud, column, head)


def tie(block, *others):
    return lax.optimization_barrier((block, *others))[0]


def make_body(vocab_size):
    bits = vocab_size.bit_length() - 1
    assert vocab_size == 1 << bits

    def trade(block, mask):
        return lax.ppermute(block, "vocab", [(at, at ^ mask) for at in range(vocab_size)])

    def swap(block, bit):
        return trade(block, 1 << bit)

    def lowest(mask):
        return (mask & -mask).bit_length() - 1

    def spread(own, line):
        blocks = [own]
        for mask in range(1, vocab_size):
            bit = lowest(mask)
            block = blocks[mask ^ (1 << bit)]
            if bit == 0:
                block = tie(block, line[-3])
            blocks.append(swap(block, bit))
            if bit == 0:
                line.append(blocks[-1])
        return blocks

    def reduce_blocks(parts):
        terms, line = list(parts), []
        for mask in range(vocab_size - 1, 0, -1):
            bit = lowest(mask)
            block = terms[mask].astype(wire)
            if bit == 0 and len(line) > 1:
                block = tie(block, line[-2])
            block = swap(block, bit)
            if bit == 0:
                line.append(block)
            terms[mask ^ (1 << bit)] = terms[mask ^ (1 << bit)] + block.astype(jnp.float32)
        return terms[0], line

    def body(teacher_rows, owner, counts, proj_weight, student_hidden, head_weight, targets):
        teach_rows = teacher_rows.shape[0]
        slab_rows = targets.shape[0]
        vocab_dev = head_weight.shape[1]
        blk = slab_rows // vocab_size
        chunk = min(slab_rows, 32)
        me = lax.axis_index("vocab")
        core = lax.axis_index("seq")
        place = jnp.stack([me, core]).astype(jnp.int32)

        def in_order(vec):
            grid = vec.reshape((2,) * bits + (blk,))
            for bit in range(bits):
                grid = jnp.where((me >> bit) & 1 == 1, jnp.flip(grid, bits - 1 - bit), grid)
            return grid.reshape(slab_rows)

        def turned(block):
            return jnp.where(core == 1, jnp.roll(block, block.shape[1] // 2, axis=1), block)

        def as_pieces(blocks):
            return blocks if blk % 16 == 0 else [jnp.concatenate(blocks, axis=0)]

        heads = (head_weight, lax.ppermute(head_weight, "seq", [(0, 1), (1, 0)]))

        spot = lax.iota(jnp.int32, slab_rows)
        row_id = ((spot // blk) ^ me) * blk + spot % blk
        alive = lax.iota(jnp.int32, teach_rows) < counts[0]
        member = (owner[None, :] == row_id[:, None]) & alive[None, :]
        own_rows, *parts = project(
            place, member.astype(jnp.bfloat16), student_hidden, teacher_rows, proj_weight, vocab_size,
            512 if student_hidden.shape[1] % 512 == 0 else student_hidden.shape[1],
        )
        projected_own, line = reduce_blocks(parts)
        hidden = spread(own_rows, line)
        projected = spread(turned(projected_own.astype(jnp.bfloat16)), line)

        column = (in_order(targets) - me * vocab_dev)[:, None]
        logit_stud, scaled_stud, stats_stud, head = student_logits(as_pieces(hidden), heads, column, 512, chunk)
        scaled_teach, stats = teacher_logits(as_pieces(projected), head, logit_stud, stats_stud, 1024, chunk)
        tables = [stats]
        for mask in range(1, vocab_size):
            far, near = mask & ~3, mask & 3
            tables.append(trade(tables[far], near) if near else trade(stats, far))
        loss, *terms = gradient(place, tables, scaled_teach, scaled_stud, column, head, bits, chunk)
        return (loss[0], turned(reduce_blocks(terms)[0].astype(jnp.bfloat16)))

    return body


def solution(mesh):
    return jax.shard_map(
        make_body(mesh.shape["vocab"]),
        mesh=mesh,
        in_specs=(
            P(("groups", "seq"), "vocab"),
            P(("groups", "seq")),
            P(("groups", "seq")),
            P("vocab", None),
            P(("groups", "seq", "vocab"), None),
            P("seq", "vocab"),
            P(("groups", "seq")),
        ),
        out_specs=(P(("groups", "seq")), P(("groups", "seq", "vocab"), None)),
        check_vma=False,
    )
```

```python
import functools

import jax
import jax.numpy as jnp
from jax import lax
from jax.experimental import pallas as pl
from jax.experimental.pallas import tpu as pltpu
from jax.sharding import PartitionSpec as P

loss_scale = 64.0
wire = jnp.float16
lanes = 128
vmem_bytes = 12 * 1024 * 1024
project_bytes = 49 * 1024 * 1024

in_vmem = pl.BlockSpec(memory_space=pltpu.VMEM)
in_smem = pl.BlockSpec(memory_space=pltpu.SMEM)
in_place = pl.BlockSpec(memory_space=pl.ANY)


def cuts(total, step):
    return [(start, min(step, total - start)) for start in range(0, total, step)]


def project_kernel(count, step, member_ref, teacher_ref, weight_ref, *rest):
    outs, (teacher, weight, aligned, sems) = rest[:count], rest[count:]
    blk = outs[0].shape[0]
    parts = cuts(weight.shape[1], step)
    first = pltpu.make_async_copy(teacher_ref, teacher, sems.at[len(parts)])
    first.start()
    for index, (start, size) in enumerate(parts):
        at = pl.ds(start, size)
        pltpu.make_async_copy(weight_ref.at[:, at], weight.at[:, at], sems.at[index]).start()
    member = member_ref[...]
    sizes = jnp.sum(member.astype(jnp.float32), axis=1, keepdims=True)
    first.wait()
    summed = jnp.dot(member, teacher[...], preferred_element_type=jnp.float32)
    aligned[...] = (summed / sizes).astype(jnp.bfloat16)

    def one(index, carry):
        at = pl.ds(pl.multiple_of(index * step, step), step)
        pltpu.make_async_copy(weight_ref.at[:, at], weight.at[:, at], sems.at[index]).wait()
        product = jnp.dot(aligned[...], weight[:, at], preferred_element_type=jnp.float32)
        for piece, out in enumerate(outs):
            out[:, at] = product[piece * blk : (piece + 1) * blk]
        return carry

    lax.fori_loop(0, len(parts), one, 0)


def project(member, teacher_rows, proj_weight, count, step):
    slab_rows, (depth, width) = member.shape[0], proj_weight.shape
    blk = slab_rows // count
    return pl.pallas_call(
        functools.partial(project_kernel, count, step),
        in_specs=[in_vmem, in_place, in_place],
        out_specs=[in_vmem] * count,
        out_shape=[jax.ShapeDtypeStruct((blk, width), jnp.float32)] * count,
        scratch_shapes=[
            pltpu.VMEM(teacher_rows.shape, jnp.bfloat16),
            pltpu.VMEM(proj_weight.shape, jnp.bfloat16),
            pltpu.VMEM((slab_rows, depth), jnp.bfloat16),
            pltpu.SemaphoreType.DMA((len(cuts(width, step)) + 1,)),
        ],
        compiler_params=pltpu.CompilerParams(vmem_limit_bytes=project_bytes),
        cost_estimate=pl.CostEstimate(
            flops=2 * slab_rows * depth * (width + teacher_rows.shape[0]),
            bytes_accessed=2 * depth * (width + teacher_rows.shape[0]) + 4 * slab_rows * width,
            transcendentals=0,
        ),
    )(member, teacher_rows, proj_weight)


class Fetch:
    def __init__(self, sems):
        self.sems, self.used = sems, 0

    def start(self, source, target):
        copy = pltpu.make_async_copy(source, target, self.sems.at[self.used])
        copy.start()
        self.used += 1
        return copy


def multiply(read_rows, head, logit_ref, highest, step, ready=None):
    total = head.shape[1]
    highest[...] = jnp.full(highest.shape, -jnp.inf, jnp.float32)

    def one(index, start, size):
        at = pl.ds(start, size)
        if ready is not None:
            ready(index, at)
        part = jnp.dot(read_rows(), head[:, at], preferred_element_type=jnp.float32)
        logit_ref[:, at] = part
        top = part[:, :lanes]
        for lane in range(lanes, size, lanes):
            top = jnp.maximum(top, part[:, lane : lane + lanes])
        highest[...] = jnp.maximum(highest[...], top)

    def body(index, carry):
        one(index, pl.multiple_of(index * step, step), step)
        return carry

    full = total // step
    lax.fori_loop(0, full, body, 0)
    if total % step:
        one(full, full * step, total % step)


def as_columns(first, second, third):
    lane = lax.broadcasted_iota(jnp.int32, (first.shape[0], lanes), 1)
    return jnp.where(lane == 0, first, jnp.where(lane == 1, second, jnp.where(lane == 2, third, 0.0)))


def student_kernel(count, step, chunk, *refs):
    pieces, heads = refs[:count], refs[count : count + 2]
    column_ref, logit_ref, scaled_ref, stats_ref, head = refs[count + 2 : count + 7]
    held, highest, table, sems = refs[count + 7 :]
    depth, total = heads[0].shape
    blk = pieces[0].shape[0]
    fetch = Fetch(sems)
    waits = [fetch.start(piece, held.at[pl.ds(i * blk, blk)]) for i, piece in enumerate(pieces)]
    first = fetch.used

    def columns(half, at):
        return heads[half].at[:, at], head.at[pl.ds(half * depth, depth), at]

    for start, size in cuts(total, step):
        for half in range(2):
            fetch.start(*columns(half, pl.ds(start, size)))

    def ready(index, at):
        for half in range(2):
            pltpu.make_async_copy(*columns(half, at), sems.at[first + 2 * index + half]).wait()

    for wait in waits:
        wait.wait()
    multiply(lambda: held[...], head, logit_ref, highest, step, ready)

    def one(part, carry):
        rows = pl.ds(pl.multiple_of(part * chunk, chunk), chunk)
        logit = logit_ref[rows, :]
        top = jnp.max(highest[rows, :], axis=1, keepdims=True)
        scaled = jnp.exp(logit - top)
        hit = lax.broadcasted_iota(jnp.int32, logit.shape, 1) == column_ref[rows, :]
        picked = jnp.sum(jnp.where(hit, logit, 0.0), axis=1, keepdims=True)
        scaled_ref[rows, :] = scaled
        table[rows, :] = as_columns(top, jnp.sum(scaled, axis=1, keepdims=True), picked)
        return carry

    lax.fori_loop(0, logit_ref.shape[0] // chunk, one, 0)
    stats_ref[...] = table[...].T[0:8]


def teacher_kernel(count, step, chunk, *refs):
    pieces = refs[:count]
    head, stud_logit_ref, stud_ref, scaled_ref, stats_ref, highest, table = refs[count:]

    def read_rows():
        return jnp.concatenate([ref[...] for ref in pieces], axis=0) if count > 1 else pieces[0][...]

    multiply(read_rows, head, scaled_ref, highest, step)

    def one(part, carry):
        rows = pl.ds(pl.multiple_of(part * chunk, chunk), chunk)
        logit = scaled_ref[rows, :]
        top = jnp.max(highest[rows, :], axis=1, keepdims=True)
        scaled = jnp.exp(logit - top)
        gap = jnp.sum(scaled * (logit - stud_logit_ref[rows, :]), axis=1, keepdims=True)
        scaled_ref[rows, :] = scaled
        table[rows, :] = as_columns(top, jnp.sum(scaled, axis=1, keepdims=True), gap)
        return carry

    lax.fori_loop(0, scaled_ref.shape[0] // chunk, one, 0)
    teach = table[...].T[0:8]
    row = lax.broadcasted_iota(jnp.int32, teach.shape, 0)
    stats_ref[...] = jnp.where(row < 4, teach, pltpu.roll(stud_ref[...], 4, 0))


def head_cost(rows, head):
    depth, vocab_dev = head.shape
    return pl.CostEstimate(
        flops=2 * rows * depth * vocab_dev,
        bytes_accessed=2 * depth * vocab_dev + 12 * rows * vocab_dev,
        transcendentals=rows * vocab_dev,
    )


def student_logits(pieces, heads, column, step, chunk):
    rows, (depth, vocab_dev) = column.shape[0], heads[0].shape
    wide = (rows, vocab_dev)
    return pl.pallas_call(
        functools.partial(student_kernel, len(pieces), step, chunk),
        in_specs=[in_place] * (len(pieces) + 2) + [in_vmem],
        out_specs=[in_vmem] * 4,
        out_shape=[
            jax.ShapeDtypeStruct(wide, jnp.float32),
            jax.ShapeDtypeStruct(wide, jnp.float32),
            jax.ShapeDtypeStruct((8, rows), jnp.float32),
            jax.ShapeDtypeStruct((2 * depth, vocab_dev), jnp.bfloat16),
        ],
        scratch_shapes=[
            pltpu.VMEM((rows, 2 * depth), jnp.bfloat16),
            pltpu.VMEM((rows, lanes), jnp.float32),
            pltpu.VMEM((rows, lanes), jnp.float32),
            pltpu.SemaphoreType.DMA((len(pieces) + 2 * len(cuts(vocab_dev, step)),)),
        ],
        compiler_params=pltpu.CompilerParams(vmem_limit_bytes=vmem_bytes),
        cost_estimate=head_cost(rows, heads[0]),
    )(*pieces, *heads, column)


def teacher_logits(pieces, head, logit_stud, stats_stud, step, chunk):
    wide = logit_stud.shape
    return pl.pallas_call(
        functools.partial(teacher_kernel, len(pieces), step, chunk),
        in_specs=[in_vmem] * (len(pieces) + 3),
        out_specs=[in_vmem] * 2,
        out_shape=[
            jax.ShapeDtypeStruct(wide, jnp.float32),
            jax.ShapeDtypeStruct((8, wide[0]), jnp.float32),
        ],
        scratch_shapes=[pltpu.VMEM((wide[0], lanes), jnp.float32)] * 2,
        compiler_params=pltpu.CompilerParams(vmem_limit_bytes=vmem_bytes),
        cost_estimate=head_cost(wide[0], head),
    )(*pieces, head, logit_stud, stats_stud)


def swapped(values, distance):
    total = values.shape[1]
    lane = lax.broadcasted_iota(jnp.int32, values.shape, 1)
    return jnp.where(
        (lane & distance) != 0, pltpu.roll(values, distance, 1), pltpu.roll(values, total - distance, 1)
    )


def gradient_kernel(bits, step, chunk, place_ref, *refs):
    count = 1 << bits
    tables, refs = refs[:count], refs[count:]
    teach_ref, stud_ref, column_ref, head, loss_ref = refs[:5]
    outs = refs[5 : count + 5]
    entries, upstream, factors = refs[count + 5 :]
    rows = upstream.shape[0]
    blk = rows // count
    me = place_ref[0]
    for mask in range(count):
        values = tables[mask][...]
        for bit in range(bits):
            if mask >> bit & 1:
                values = swapped(values, blk << bit)
        entries[me ^ mask] = values
    every = entries[...]
    top_teach = jnp.max(every[:, 0:1], axis=0)
    top_stud = jnp.max(every[:, 4:5], axis=0)
    weight = jnp.exp(every[:, 0:1] - top_teach)
    total_teach = jnp.sum(weight * every[:, 1:2], axis=0)
    total_stud = jnp.sum(jnp.exp(every[:, 4:5] - top_stud) * every[:, 5:6], axis=0)
    lse_teach = top_teach + jnp.log(total_teach)
    lse_stud = top_stud + jnp.log(total_stud)
    gap = jnp.sum(weight * every[:, 2:3], axis=0) / total_teach
    loss = gap - lse_teach + 2.0 * lse_stud - jnp.sum(every[:, 6:7], axis=0)
    loss = jnp.broadcast_to(loss, loss_ref.shape)
    for bit in range(bits):
        loss = jnp.where(((me >> bit) & 1) == 1, swapped(loss, blk << bit), loss)
    loss_ref[...] = loss
    own = tables[0][...]
    scale_teach = -loss_scale * jnp.exp(own[0:1] - lse_teach)
    scale_stud = 2.0 * loss_scale * jnp.exp(own[4:5] - lse_stud)
    line = lax.broadcasted_iota(jnp.int32, (lanes, rows), 0)
    factors[...] = jnp.where(line == 0, scale_teach, scale_stud).T

    def one(part, carry):
        at = pl.ds(pl.multiple_of(part * chunk, chunk), chunk)
        hit = lax.broadcasted_iota(jnp.int32, (chunk, teach_ref.shape[1]), 1) == column_ref[at, :]
        both = teach_ref[at, :] * factors[at, 0:1] + stud_ref[at, :] * factors[at, 1:2]
        upstream[at, :] = jnp.where(hit, both - loss_scale, both).astype(jnp.bfloat16)
        return carry

    lax.fori_loop(0, rows // chunk, one, 0)

    def two(index, carry):
        at = pl.ds(pl.multiple_of(index * step, step), step)
        product = lax.dot_general(
            upstream[...], head[at, :], (((1,), (1,)), ((), ())), preferred_element_type=jnp.float32
        )
        for piece, out in enumerate(outs):
            out[:, at] = product[piece * blk : (piece + 1) * blk]
        return carry

    lax.fori_loop(0, head.shape[0] // step, two, 0)


def gradient(place, tables, scaled_teach, scaled_stud, column, head, bits, chunk):
    rows, vocab_dev = scaled_teach.shape
    count, width = 1 << bits, head.shape[0]
    step = 512 if width % 512 == 0 else width
    return pl.pallas_call(
        functools.partial(gradient_kernel, bits, step, chunk),
        in_specs=[in_smem] + [in_vmem] * (count + 4),
        out_specs=[in_vmem] * (count + 1),
        out_shape=[jax.ShapeDtypeStruct((8, rows), jnp.float32)]
        + [jax.ShapeDtypeStruct((rows // count, width), jnp.float32)] * count,
        scratch_shapes=[
            pltpu.VMEM((count, 8, rows), jnp.float32),
            pltpu.VMEM((rows, vocab_dev), jnp.bfloat16),
            pltpu.VMEM((rows, lanes), jnp.float32),
        ],
        compiler_params=pltpu.CompilerParams(vmem_limit_bytes=vmem_bytes),
        cost_estimate=head_cost(rows, head),
    )(place, *tables, scaled_teach, scaled_stud, column, head)


def tie(block, *others):
    return lax.optimization_barrier((block, *others))[0]


def make_body(vocab_size):
    bits = vocab_size.bit_length() - 1
    assert vocab_size == 1 << bits

    def trade(block, mask):
        return lax.ppermute(block, "vocab", [(at, at ^ mask) for at in range(vocab_size)])

    def swap(block, bit):
        return trade(block, 1 << bit)

    def lowest(mask):
        return (mask & -mask).bit_length() - 1

    def spread(own, line):
        blocks = [own]
        for mask in range(1, vocab_size):
            bit = lowest(mask)
            block = blocks[mask ^ (1 << bit)]
            if bit == 0:
                block = tie(block, line[-3])
            blocks.append(swap(block, bit))
            if bit == 0:
                line.append(blocks[-1])
        return blocks

    def reduce_blocks(parts):
        terms, line = list(parts), []
        for mask in range(vocab_size - 1, 0, -1):
            bit = lowest(mask)
            block = terms[mask].astype(wire)
            if bit == 0 and len(line) > 1:
                block = tie(block, line[-2])
            block = swap(block, bit)
            if bit == 0:
                line.append(block)
            terms[mask ^ (1 << bit)] = terms[mask ^ (1 << bit)] + block.astype(jnp.float32)
        return terms[0], line

    def body(teacher_rows, owner, counts, proj_weight, student_hidden, head_weight, targets):
        teach_rows = teacher_rows.shape[0]
        slab_rows = targets.shape[0]
        vocab_dev = head_weight.shape[1]
        blk = slab_rows // vocab_size
        chunk = min(slab_rows, 32)
        me = lax.axis_index("vocab")
        core = lax.axis_index("seq")
        place = jnp.stack([me, core]).astype(jnp.int32)

        def in_order(vec):
            grid = vec.reshape((2,) * bits + (blk,))
            for bit in range(bits):
                grid = jnp.where((me >> bit) & 1 == 1, jnp.flip(grid, bits - 1 - bit), grid)
            return grid.reshape(slab_rows)

        def turned(block):
            return jnp.where(core == 1, jnp.roll(block, block.shape[1] // 2, axis=1), block)

        def as_pieces(blocks):
            return blocks if blk % 16 == 0 else [jnp.concatenate(blocks, axis=0)]

        heads = (head_weight, lax.ppermute(head_weight, "seq", [(0, 1), (1, 0)]))

        spot = lax.iota(jnp.int32, slab_rows)
        row_id = ((spot // blk) ^ me) * blk + spot % blk
        alive = lax.iota(jnp.int32, teach_rows) < counts[0]
        member = (owner[None, :] == row_id[:, None]) & alive[None, :]
        parts = project(member.astype(jnp.bfloat16), teacher_rows, proj_weight, vocab_size, 512 if student_hidden.shape[1] % 512 == 0 else student_hidden.shape[1])
        projected_own, line = reduce_blocks(parts)
        hidden = spread(tie(turned(student_hidden), parts[-1]), line)
        projected = spread(turned(projected_own.astype(jnp.bfloat16)), line)

        column = (in_order(targets) - me * vocab_dev)[:, None]
        logit_stud, scaled_stud, stats_stud, head = student_logits(as_pieces(hidden), heads, column, 512, chunk)
        scaled_teach, stats = teacher_logits(as_pieces(projected), head, logit_stud, stats_stud, 1024, chunk)
        tables = [stats]
        for mask in range(1, vocab_size):
            far, near = mask & ~3, mask & 3
            tables.append(trade(tables[far], near) if near else trade(stats, far))
        loss, *terms = gradient(place, tables, scaled_teach, scaled_stud, column, head, bits, chunk)
        return (loss[0], turned(reduce_blocks(terms)[0].astype(jnp.bfloat16)))

    return body


def solution(mesh):
    return jax.shard_map(
        make_body(mesh.shape["vocab"]),
        mesh=mesh,
        in_specs=(
            P(("groups", "seq"), "vocab"),
            P(("groups", "seq")),
            P(("groups", "seq")),
            P("vocab", None),
            P(("groups", "seq", "vocab"), None),
            P("seq", "vocab"),
            P(("groups", "seq")),
        ),
        out_specs=(P(("groups", "seq")), P(("groups", "seq", "vocab"), None)),
        check_vma=False,
    )
```

```python
import functools

import jax
import jax.numpy as jnp
from jax import lax
from jax.experimental import pallas as pl
from jax.experimental.pallas import tpu as pltpu
from jax.sharding import PartitionSpec as P

loss_scale = 64.0
wire = jnp.float16
lanes = 128
vmem_bytes = 12 * 1024 * 1024
project_bytes = 50 * 1024 * 1024

in_vmem = pl.BlockSpec(memory_space=pltpu.VMEM)
in_smem = pl.BlockSpec(memory_space=pltpu.SMEM)
in_place = pl.BlockSpec(memory_space=pl.ANY)


def cuts(total, step):
    return [(start, min(step, total - start)) for start in range(0, total, step)]


def project_kernel(count, step, member_ref, teacher_ref, weight_ref, *rest):
    outs, (teacher, weight, aligned, sems) = rest[:count], rest[count:]
    blk = outs[0].shape[0]
    parts = cuts(weight.shape[1], step)
    first = pltpu.make_async_copy(teacher_ref, teacher, sems.at[len(parts)])
    first.start()
    for index, (start, size) in enumerate(parts):
        at = pl.ds(start, size)
        pltpu.make_async_copy(weight_ref.at[:, at], weight.at[:, at], sems.at[index]).start()
    member = member_ref[...]
    sizes = jnp.sum(member.astype(jnp.float32), axis=1, keepdims=True)
    first.wait()
    summed = jnp.dot(member, teacher[...], preferred_element_type=jnp.float32)
    aligned[...] = (summed / sizes).astype(jnp.bfloat16)

    def one(index, carry):
        at = pl.ds(pl.multiple_of(index * step, step), step)
        pltpu.make_async_copy(weight_ref.at[:, at], weight.at[:, at], sems.at[index]).wait()
        product = jnp.dot(aligned[...], weight[:, at], preferred_element_type=jnp.float32)
        for piece, out in enumerate(outs):
            out[:, at] = product[piece * blk : (piece + 1) * blk]
        return carry

    lax.fori_loop(0, len(parts), one, 0)


def project(member, teacher_rows, proj_weight, count, step):
    slab_rows, (depth, width) = member.shape[0], proj_weight.shape
    blk = slab_rows // count
    return pl.pallas_call(
        functools.partial(project_kernel, count, step),
        in_specs=[in_vmem, in_place, in_place],
        out_specs=[in_vmem] * count,
        out_shape=[jax.ShapeDtypeStruct((blk, width), jnp.float32)] * count,
        scratch_shapes=[
            pltpu.VMEM(teacher_rows.shape, jnp.bfloat16),
            pltpu.VMEM(proj_weight.shape, jnp.bfloat16),
            pltpu.VMEM((slab_rows, depth), jnp.bfloat16),
            pltpu.SemaphoreType.DMA((len(cuts(width, step)) + 1,)),
        ],
        compiler_params=pltpu.CompilerParams(vmem_limit_bytes=project_bytes),
        cost_estimate=pl.CostEstimate(
            flops=2 * slab_rows * depth * (width + teacher_rows.shape[0]),
            bytes_accessed=2 * depth * (width + teacher_rows.shape[0]) + 4 * slab_rows * width,
            transcendentals=0,
        ),
    )(member, teacher_rows, proj_weight)


class Fetch:
    def __init__(self, sems):
        self.sems, self.used = sems, 0

    def start(self, source, target):
        copy = pltpu.make_async_copy(source, target, self.sems.at[self.used])
        copy.start()
        self.used += 1
        return copy


def multiply(read_rows, head, logit_ref, highest, step, ready=None):
    total = head.shape[1]
    highest[...] = jnp.full(highest.shape, -jnp.inf, jnp.float32)

    def one(index, start, size):
        at = pl.ds(start, size)
        if ready is not None:
            ready(index, at)
        part = jnp.dot(read_rows(), head[:, at], preferred_element_type=jnp.float32)
        logit_ref[:, at] = part
        top = part[:, :lanes]
        for lane in range(lanes, size, lanes):
            top = jnp.maximum(top, part[:, lane : lane + lanes])
        highest[...] = jnp.maximum(highest[...], top)

    def body(index, carry):
        one(index, pl.multiple_of(index * step, step), step)
        return carry

    full = total // step
    lax.fori_loop(0, full, body, 0)
    if total % step:
        one(full, full * step, total % step)


def as_columns(first, second, third):
    lane = lax.broadcasted_iota(jnp.int32, (first.shape[0], lanes), 1)
    return jnp.where(lane == 0, first, jnp.where(lane == 1, second, jnp.where(lane == 2, third, 0.0)))


def student_kernel(count, step, chunk, *refs):
    pieces, heads = refs[:count], refs[count : count + 2]
    column_ref, logit_ref, scaled_ref, stats_ref, head = refs[count + 2 : count + 7]
    held, highest, table, sems = refs[count + 7 :]
    depth, total = heads[0].shape
    blk = pieces[0].shape[0]
    fetch = Fetch(sems)
    waits = [fetch.start(piece, held.at[pl.ds(i * blk, blk)]) for i, piece in enumerate(pieces)]
    first = fetch.used

    def columns(half, at):
        return heads[half].at[:, at], head.at[pl.ds(half * depth, depth), at]

    for start, size in cuts(total, step):
        for half in range(2):
            fetch.start(*columns(half, pl.ds(start, size)))

    def ready(index, at):
        for half in range(2):
            pltpu.make_async_copy(*columns(half, at), sems.at[first + 2 * index + half]).wait()

    for wait in waits:
        wait.wait()
    multiply(lambda: held[...], head, logit_ref, highest, step, ready)

    def one(part, carry):
        rows = pl.ds(pl.multiple_of(part * chunk, chunk), chunk)
        logit = logit_ref[rows, :]
        top = jnp.max(highest[rows, :], axis=1, keepdims=True)
        scaled = jnp.exp(logit - top)
        hit = lax.broadcasted_iota(jnp.int32, logit.shape, 1) == column_ref[rows, :]
        picked = jnp.sum(jnp.where(hit, logit, 0.0), axis=1, keepdims=True)
        scaled_ref[rows, :] = scaled
        table[rows, :] = as_columns(top, jnp.sum(scaled, axis=1, keepdims=True), picked)
        return carry

    lax.fori_loop(0, logit_ref.shape[0] // chunk, one, 0)
    stats_ref[...] = table[...].T[0:8]


def teacher_kernel(count, step, chunk, *refs):
    pieces = refs[:count]
    head, stud_logit_ref, stud_ref, scaled_ref, stats_ref, highest, table = refs[count:]

    def read_rows():
        return jnp.concatenate([ref[...] for ref in pieces], axis=0) if count > 1 else pieces[0][...]

    multiply(read_rows, head, scaled_ref, highest, step)

    def one(part, carry):
        rows = pl.ds(pl.multiple_of(part * chunk, chunk), chunk)
        logit = scaled_ref[rows, :]
        top = jnp.max(highest[rows, :], axis=1, keepdims=True)
        scaled = jnp.exp(logit - top)
        gap = jnp.sum(scaled * (logit - stud_logit_ref[rows, :]), axis=1, keepdims=True)
        scaled_ref[rows, :] = scaled
        table[rows, :] = as_columns(top, jnp.sum(scaled, axis=1, keepdims=True), gap)
        return carry

    lax.fori_loop(0, scaled_ref.shape[0] // chunk, one, 0)
    teach = table[...].T[0:8]
    row = lax.broadcasted_iota(jnp.int32, teach.shape, 0)
    stats_ref[...] = jnp.where(row < 4, teach, pltpu.roll(stud_ref[...], 4, 0))


def head_cost(rows, head):
    depth, vocab_dev = head.shape
    return pl.CostEstimate(
        flops=2 * rows * depth * vocab_dev,
        bytes_accessed=2 * depth * vocab_dev + 12 * rows * vocab_dev,
        transcendentals=rows * vocab_dev,
    )


def student_logits(pieces, heads, column, step, chunk):
    rows, (depth, vocab_dev) = column.shape[0], heads[0].shape
    wide = (rows, vocab_dev)
    return pl.pallas_call(
        functools.partial(student_kernel, len(pieces), step, chunk),
        in_specs=[in_place] * (len(pieces) + 2) + [in_vmem],
        out_specs=[in_vmem] * 4,
        out_shape=[
            jax.ShapeDtypeStruct(wide, jnp.float32),
            jax.ShapeDtypeStruct(wide, jnp.float32),
            jax.ShapeDtypeStruct((8, rows), jnp.float32),
            jax.ShapeDtypeStruct((2 * depth, vocab_dev), jnp.bfloat16),
        ],
        scratch_shapes=[
            pltpu.VMEM((rows, 2 * depth), jnp.bfloat16),
            pltpu.VMEM((rows, lanes), jnp.float32),
            pltpu.VMEM((rows, lanes), jnp.float32),
            pltpu.SemaphoreType.DMA((len(pieces) + 2 * len(cuts(vocab_dev, step)),)),
        ],
        compiler_params=pltpu.CompilerParams(vmem_limit_bytes=vmem_bytes),
        cost_estimate=head_cost(rows, heads[0]),
    )(*pieces, *heads, column)


def teacher_logits(pieces, head, logit_stud, stats_stud, step, chunk):
    wide = logit_stud.shape
    return pl.pallas_call(
        functools.partial(teacher_kernel, len(pieces), step, chunk),
        in_specs=[in_vmem] * (len(pieces) + 3),
        out_specs=[in_vmem] * 2,
        out_shape=[
            jax.ShapeDtypeStruct(wide, jnp.float32),
            jax.ShapeDtypeStruct((8, wide[0]), jnp.float32),
        ],
        scratch_shapes=[pltpu.VMEM((wide[0], lanes), jnp.float32)] * 2,
        compiler_params=pltpu.CompilerParams(vmem_limit_bytes=vmem_bytes),
        cost_estimate=head_cost(wide[0], head),
    )(*pieces, head, logit_stud, stats_stud)


def swapped(values, distance):
    total = values.shape[1]
    lane = lax.broadcasted_iota(jnp.int32, values.shape, 1)
    return jnp.where(
        (lane & distance) != 0, pltpu.roll(values, distance, 1), pltpu.roll(values, total - distance, 1)
    )


def gradient_kernel(bits, step, chunk, place_ref, *refs):
    count = 1 << bits
    tables, refs = refs[:count], refs[count:]
    teach_ref, stud_ref, column_ref, head, loss_ref = refs[:5]
    outs = refs[5 : count + 5]
    entries, upstream, factors = refs[count + 5 :]
    rows = upstream.shape[0]
    blk = rows // count
    me = place_ref[0]
    for mask in range(count):
        values = tables[mask][...]
        for bit in range(bits):
            if mask >> bit & 1:
                values = swapped(values, blk << bit)
        entries[me ^ mask] = values
    every = entries[...]
    top_teach = jnp.max(every[:, 0:1], axis=0)
    top_stud = jnp.max(every[:, 4:5], axis=0)
    weight = jnp.exp(every[:, 0:1] - top_teach)
    total_teach = jnp.sum(weight * every[:, 1:2], axis=0)
    total_stud = jnp.sum(jnp.exp(every[:, 4:5] - top_stud) * every[:, 5:6], axis=0)
    lse_teach = top_teach + jnp.log(total_teach)
    lse_stud = top_stud + jnp.log(total_stud)
    gap = jnp.sum(weight * every[:, 2:3], axis=0) / total_teach
    loss = gap - lse_teach + 2.0 * lse_stud - jnp.sum(every[:, 6:7], axis=0)
    loss = jnp.broadcast_to(loss, loss_ref.shape)
    for bit in range(bits):
        loss = jnp.where(((me >> bit) & 1) == 1, swapped(loss, blk << bit), loss)
    loss_ref[...] = loss
    own = tables[0][...]
    scale_teach = -loss_scale * jnp.exp(own[0:1] - lse_teach)
    scale_stud = 2.0 * loss_scale * jnp.exp(own[4:5] - lse_stud)
    line = lax.broadcasted_iota(jnp.int32, (lanes, rows), 0)
    factors[...] = jnp.where(line == 0, scale_teach, scale_stud).T

    def one(part, carry):
        at = pl.ds(pl.multiple_of(part * chunk, chunk), chunk)
        hit = lax.broadcasted_iota(jnp.int32, (chunk, teach_ref.shape[1]), 1) == column_ref[at, :]
        both = teach_ref[at, :] * factors[at, 0:1] + stud_ref[at, :] * factors[at, 1:2]
        upstream[at, :] = jnp.where(hit, both - loss_scale, both).astype(jnp.bfloat16)
        return carry

    lax.fori_loop(0, rows // chunk, one, 0)

    def two(index, carry):
        at = pl.ds(pl.multiple_of(index * step, step), step)
        product = lax.dot_general(
            upstream[...], head[at, :], (((1,), (1,)), ((), ())), preferred_element_type=jnp.float32
        )
        for piece, out in enumerate(outs):
            out[:, at] = product[piece * blk : (piece + 1) * blk]
        return carry

    lax.fori_loop(0, head.shape[0] // step, two, 0)


def gradient(place, tables, scaled_teach, scaled_stud, column, head, bits, chunk):
    rows, vocab_dev = scaled_teach.shape
    count, width = 1 << bits, head.shape[0]
    step = 512 if width % 512 == 0 else width
    return pl.pallas_call(
        functools.partial(gradient_kernel, bits, step, chunk),
        in_specs=[in_smem] + [in_vmem] * (count + 4),
        out_specs=[in_vmem] * (count + 1),
        out_shape=[jax.ShapeDtypeStruct((8, rows), jnp.float32)]
        + [jax.ShapeDtypeStruct((rows // count, width), jnp.float32)] * count,
        scratch_shapes=[
            pltpu.VMEM((count, 8, rows), jnp.float32),
            pltpu.VMEM((rows, vocab_dev), jnp.bfloat16),
            pltpu.VMEM((rows, lanes), jnp.float32),
        ],
        compiler_params=pltpu.CompilerParams(vmem_limit_bytes=vmem_bytes),
        cost_estimate=head_cost(rows, head),
    )(place, *tables, scaled_teach, scaled_stud, column, head)


def tie(block, *others):
    return lax.optimization_barrier((block, *others))[0]


def make_body(vocab_size):
    bits = vocab_size.bit_length() - 1
    assert vocab_size == 1 << bits

    def trade(block, mask):
        return lax.ppermute(block, "vocab", [(at, at ^ mask) for at in range(vocab_size)])

    def swap(block, bit):
        return trade(block, 1 << bit)

    def lowest(mask):
        return (mask & -mask).bit_length() - 1

    def spread(own, line):
        blocks = [own]
        for mask in range(1, vocab_size):
            bit = lowest(mask)
            block = blocks[mask ^ (1 << bit)]
            if bit == 0:
                block = tie(block, line[-3])
            blocks.append(swap(block, bit))
            if bit == 0:
                line.append(blocks[-1])
        return blocks

    def reduce_blocks(parts, single=False):
        terms, line = list(parts), []
        for mask in range(vocab_size - 1, 0, -1):
            bit = lowest(mask)
            block = terms[mask].astype(wire)
            if bit == 0 and len(line) > 1:
                block = tie(block, line[-1] if single and len(line) > 2 else line[-2])
            block = swap(block, bit)
            if bit == 0:
                line.append(block)
            terms[mask ^ (1 << bit)] = terms[mask ^ (1 << bit)] + block.astype(jnp.float32)
        return terms[0], line

    def body(teacher_rows, owner, counts, proj_weight, student_hidden, head_weight, targets):
        teach_rows = teacher_rows.shape[0]
        slab_rows = targets.shape[0]
        vocab_dev = head_weight.shape[1]
        blk = slab_rows // vocab_size
        chunk = min(slab_rows, 32)
        me = lax.axis_index("vocab")
        core = lax.axis_index("seq")
        place = jnp.stack([me, core]).astype(jnp.int32)

        def in_order(vec):
            grid = vec.reshape((2,) * bits + (blk,))
            for bit in range(bits):
                grid = jnp.where((me >> bit) & 1 == 1, jnp.flip(grid, bits - 1 - bit), grid)
            return grid.reshape(slab_rows)

        def turned(block):
            return jnp.where(core == 1, jnp.roll(block, block.shape[1] // 2, axis=1), block)

        def as_pieces(blocks):
            return blocks if blk % 16 == 0 else [jnp.concatenate(blocks, axis=0)]

        heads = (head_weight, lax.ppermute(head_weight, "seq", [(0, 1), (1, 0)]))

        spot = lax.iota(jnp.int32, slab_rows)
        row_id = ((spot // blk) ^ me) * blk + spot % blk
        alive = lax.iota(jnp.int32, teach_rows) < counts[0]
        member = (owner[None, :] == row_id[:, None]) & alive[None, :]
        parts = project(member.astype(jnp.bfloat16), teacher_rows, proj_weight, vocab_size, 512 if student_hidden.shape[1] % 512 == 0 else student_hidden.shape[1])
        projected_own, line = reduce_blocks(parts)
        hidden = spread(tie(turned(student_hidden), parts[-1]), line)
        projected = spread(turned(projected_own.astype(jnp.bfloat16)), line)

        column = (in_order(targets) - me * vocab_dev)[:, None]
        logit_stud, scaled_stud, stats_stud, head = student_logits(as_pieces(hidden), heads, column, 512, chunk)
        scaled_teach, stats = teacher_logits(as_pieces(projected), head, logit_stud, stats_stud, 1024, chunk)
        tables = [stats]
        for mask in range(1, vocab_size):
            far, near = mask & ~3, mask & 3
            tables.append(trade(tables[far], near) if near else trade(stats, far))
        loss, *terms = gradient(place, tables, scaled_teach, scaled_stud, column, head, bits, chunk)
        return (loss[0], turned(reduce_blocks(terms, True)[0].astype(jnp.bfloat16)))

    return body


def solution(mesh):
    return jax.shard_map(
        make_body(mesh.shape["vocab"]),
        mesh=mesh,
        in_specs=(
            P(("groups", "seq"), "vocab"),
            P(("groups", "seq")),
            P(("groups", "seq")),
            P("vocab", None),
            P(("groups", "seq", "vocab"), None),
            P("seq", "vocab"),
            P(("groups", "seq")),
        ),
        out_specs=(P(("groups", "seq")), P(("groups", "seq", "vocab"), None)),
        check_vma=False,
    )
```
